32 devices in a mesh: section: 2 (over y), dp: 16 (over z, x, core).
Axes of the slice: x: 2, y: 2, z: 4, core: 2. Of those that a mesh axis runs over, the one named last changes fastest.
Arguments:
- base: bfloat16 [6144, 8192], P('dp'), may hold values from -6 to 6
- cotangent: bfloat16 [6144, 8192], P('dp'), may hold values from -6 to 6
- gain: float32 [2, 8192], P('section'), may hold values from 0.1 to 1.9
- weight_in: bfloat16 [2, 8192, 128], P('section', 'dp'), may hold values from -0.0625 to 0.0625
- weight_out: bfloat16 [2, 8192, 128], P('section', 'dp'), may hold values from -0.5 to 0.5
- subspace: bfloat16 [8192, 256], P('dp'), may hold values from -0.0625 to 0.0625
Outputs:
- codes: bfloat16 [2, 6144, 256], P('section', 'dp')
- grad_in: float32 [2, 8192, 128], P('section', 'dp')
- grad_out: float32 [2, 8192, 128], P('section', 'dp')
The draws below stay inside these ranges and needn't reach their ends.
All inputs are finite; a program needn't handle non-finite values.
Results may differ from the reference program's by a relative error of at most 0.0076.
Values may be sent and summed in bfloat16 or wider, within the bound.
No kernel may reach another device: no remote copies, remote signals or barrier semaphores. Data moves between devices by JAX's collectives and lax.ppermute only.
A program may use at most 128 MiB of HBM per device.

```python
import jax
import jax.numpy as jnp
from jax import lax

D = 8192
K = 256
R = 128
SECTIONS = 2
TOKENS = 6144
N_SECTION = 2


def raised(entries, key, source, target, parts, factor):
    def block_of(axis_at):
        return (jnp.arange(entries.shape[axis_at]) // (entries.shape[axis_at] // parts)).reshape((-1,) + (1,) * (entries.ndim - 1 - axis_at))

    first = jax.random.permutation(key, parts)[block_of(target)]
    second = (block_of(target) + parts // 2) % parts
    return jnp.where((block_of(source) == first) | (block_of(source) == second), factor * entries, entries)


def block_levels(key, shape, shards, smallest, top_value):
    def one(position, blocks):
        steps = jax.random.uniform(jax.random.fold_in(jax.random.fold_in(key, 6), position), (blocks,), jnp.float32, smallest / len(shards), top_value / len(shards))
        return jnp.repeat(jnp.exp(steps), shape[position] // blocks).reshape((-1,) + (1,) * (len(shape) - position - 1))

    loudness = one(*shards[0])
    for cut in shards[1:]:
        loudness = loudness * one(*cut)
    return loudness


def gaussian(rng, shape, deviation, most, pieces=(), kind=jnp.bfloat16):
    factor_of = block_levels(rng, shape, pieces, -0.22, 0.18) if pieces else 1.0
    entries = jax.random.normal(rng, shape, jnp.float32) * deviation * factor_of
    return jnp.minimum(jnp.maximum(entries, -most), most).astype(kind)


def gaussian_with(stream_key, shape, width, bound, cuts, heavy, dtype=jnp.bfloat16):
    array = width * jax.random.normal(stream_key, shape, jnp.float32)
    if cuts:
        array = array * block_levels(stream_key, shape, cuts, -0.22, 0.18)
    return jnp.clip(raised(array, jax.random.fold_in(stream_key, 3), *heavy), -bound, bound).astype(dtype)


def setup_inputs(seed: int = 0) -> dict:
    splits = jax.random.split(jax.random.key(seed), 7)
    return {
        "base": gaussian(splits[0], (TOKENS, D), 1.0, 6.0, ((0, 16),)),
        "cotangent": gaussian_with(splits[1], (TOKENS, D), 1.0, 6.0, ((0, 16),), (0, 1, 16, 2.0)),
        "gain": jnp.clip(1.0 + 0.18 * jax.random.normal(splits[2], (SECTIONS, D), jnp.float32), 0.1, 1.9),
        "weight_in": gaussian(splits[3], (SECTIONS, D, R), D ** -0.5, 0.0625, ((0, 2), (1, 16))),
        "weight_out": gaussian(splits[4], (SECTIONS, D, R), R ** -0.5, 0.5, ((0, 2), (1, 16))),
        "subspace": gaussian(splits[5], (D, K), D ** -0.5, 0.0625, ((0, 16),)),
    }


def rebuild(base_rows, coded, subspace):
    return (base_rows.astype(jnp.float32) + jnp.dot(coded, subspace.T, preferred_element_type=jnp.float32)).astype(jnp.bfloat16)

def branch_parts(residual, gain_row, weight_in):
    residual_f = residual.astype(jnp.float32)
    inverse = lax.rsqrt(lax.optimization_barrier(jnp.mean(residual_f * residual_f, axis=-1, keepdims=True)) + 1e-05)
    normed = (residual_f * inverse * gain_row).astype(jnp.bfloat16)
    inner_act = jnp.dot(normed, weight_in, preferred_element_type=jnp.float32)
    active = jax.nn.silu(inner_act).astype(jnp.bfloat16)
    return (residual_f, inverse, normed, inner_act, active)

def layer_forward(residual, base_rows, gain_row, weight_in, weight_out, subspace):
    residual_f, inverse, normed, inner_act, active = branch_parts(residual, gain_row, weight_in)
    output = residual_f + jnp.dot(active, weight_out.T, preferred_element_type=jnp.float32)
    offset = (output - base_rows.astype(jnp.float32)).astype(jnp.bfloat16)
    return jnp.dot(offset, subspace, preferred_element_type=jnp.float32).astype(jnp.bfloat16)

def layer_backward(residual, grad_y, gain_row, weight_in, weight_out, subspace):
    residual_f, inverse, normed, inner_act, active = branch_parts(residual, gain_row, weight_in)
    grad_half = grad_y.astype(jnp.bfloat16)
    grad_wout = jnp.dot(grad_half.T, active, preferred_element_type=jnp.float32)
    grad_active = jnp.dot(grad_half, weight_out, preferred_element_type=jnp.float32)
    logistic = jax.nn.sigmoid(inner_act)
    grad_inner = (grad_active * logistic * (1.0 + inner_act * (1.0 - logistic))).astype(jnp.bfloat16)
    grad_win = jnp.dot(normed.T, grad_inner, preferred_element_type=jnp.float32)
    grad_normed = jnp.dot(grad_inner, weight_in.T, preferred_element_type=jnp.float32) * gain_row
    grad_resid = grad_y + inverse * grad_normed - residual_f * inverse ** 3 * lax.optimization_barrier(jnp.mean(residual_f * grad_normed, axis=-1, keepdims=True))
    sent_back = jnp.dot(grad_resid.astype(jnp.bfloat16), subspace, preferred_element_type=jnp.float32).astype(jnp.bfloat16)
    return (sent_back, grad_win, grad_wout)

def reference(base, cotangent, gain, weight_in, weight_out, subspace):
    saved = []
    code_list = []
    residual = base
    coded = None
    for section_id in range(N_SECTION):
        if section_id > 0:
            residual = rebuild(base, coded, subspace)
        coded = layer_forward(residual, base, gain[section_id], weight_in[section_id], weight_out[section_id], subspace)
        saved.append(residual)
        code_list.append(coded)
    grad_y = cotangent.astype(jnp.float32)
    list_in = [None] * N_SECTION
    list_out = [None] * N_SECTION
    for section_id in range(N_SECTION - 1, -1, -1):
        sent_back, grad_win, grad_wout = layer_backward(saved[section_id], grad_y, gain[section_id], weight_in[section_id], weight_out[section_id], subspace)
        list_in[section_id] = grad_win
        list_out[section_id] = grad_wout
        grad_y = jnp.dot(sent_back, subspace.T, preferred_element_type=jnp.float32)
    return (jnp.stack(code_list), jnp.stack(list_in), jnp.stack(list_out))
```

```python
import jax
import jax.numpy as jnp
from jax import lax
from jax.sharding import PartitionSpec as P

F32 = jnp.float32
BF16 = jnp.bfloat16


def mm(a, b, dims=((1,), (0,))):
    return lax.dot_general(a, b, (dims, ((), ())), preferred_element_type=F32)


def exact(a, b, dims=((1,), (0,))):
    return lax.dot_general(
        a.astype(F32),
        b.astype(F32),
        (dims, ((), ())),
        precision=lax.Precision.HIGHEST,
        preferred_element_type=F32,
    )


def swap(value, axis, bit):
    peers = lax.axis_size(axis)
    return lax.ppermute(value, axis, [(i, i ^ bit) for i in range(peers)])


def sum_over(value, axis):
    peers = lax.axis_size(axis)
    bit = 1
    while bit < peers:
        value = value + swap(value, axis, bit)
        bit *= 2
    return value


def share_sections(value):
    sections = lax.axis_size("section")
    here = lax.axis_index("section")
    around = [(i, (i + 1) % sections) for i in range(sections)]
    held = [value]
    for _ in range(sections - 1):
        held.append(lax.ppermute(held[-1], "section", around))
    stacked = jnp.stack(held)
    order = (here - jnp.arange(sections)) % sections
    return [lax.dynamic_index_in_dim(stacked, order[s], 0, keepdims=False) for s in range(sections)]


def pick(values, index):
    return lax.dynamic_index_in_dim(jnp.stack(values), index, 0, keepdims=False)


def chain(squares, based, coted, aux, gram, width, last_rank):
    base_p, base_s = based
    cot_w, cot_s = coted
    sections = len(base_p)
    acts, codes, inners, inverses, resid_s = [], [], [], [], []
    code = None
    for s in range(sections):
        m_s, q_t = aux[s]
        if s == 0:
            total, moved, inner = squares, None, base_p[s]
            resid_s.append(base_s)
        else:
            code_f = code.astype(F32)
            moved = exact(code, gram)
            total = squares + jnp.sum((2.0 * base_s + moved) * code_f, axis=-1, keepdims=True)
            inner = base_p[s] + exact(code, q_t, ((1,), (1,)))
            resid_s.append(base_s + moved)
        inverse = lax.rsqrt(jnp.maximum(total, 0.0) / width + 1e-05)
        inner = inner * inverse
        active = inner * jax.nn.sigmoid(inner)
        grown = exact(active, m_s)
        code = (grown if s == 0 else moved + grown).astype(BF16)
        acts.append(active.astype(BF16))
        codes.append(code)
        inners.append(inner)
        inverses.append(inverse)
    scaled, t_in, t_out = [None] * sections, [None] * sections, [None] * sections
    back = None
    for s in range(sections - 1, -1, -1):
        m_s, q_t = aux[s]
        if s == sections - 1:
            grad_active, grad_y = cot_w, cot_s
            t_out[s] = jnp.zeros((gram.shape[0], acts[s].shape[1]), F32)
        else:
            grad_active, grad_y = exact(back, m_s, ((1,), (1,))), exact(back, gram)
            t_out[s] = mm(back, acts[s], ((0,), (0,)))
        inner, inverse = inners[s], inverses[s]
        logistic = jax.nn.sigmoid(inner)
        grad_inner = grad_active * logistic * (1.0 + inner * (1.0 - logistic))
        scaled[s] = (inverse * grad_inner).astype(BF16)
        if s > 0:
            t_in[s] = mm(codes[s - 1], scaled[s], ((0,), (0,)))
            along = jnp.sum(inner * grad_inner, axis=-1, keepdims=True) * (inverse * inverse / width)
            back = (grad_y + exact(scaled[s], q_t) - resid_s[s] * along).astype(BF16)
        else:
            t_in[s] = jnp.zeros((gram.shape[0], acts[s].shape[1]), F32)
    return codes, acts, scaled, t_in, t_out


def on_device(base, cotangent, gain, weight_in, weight_out, subspace):
    sections = lax.axis_size("section")
    here = lax.axis_index("section")
    spot = lax.axis_index("dp")
    rows, width = base.shape
    part, size = subspace.shape
    rank = weight_in.shape[2]
    last = sections - 1
    own_gain = lax.dynamic_slice_in_dim(gain[0], spot * part, part, 0)[:, None]
    scaled_in = (own_gain * weight_in[0].astype(F32)).astype(BF16)
    out_rows = weight_out[0]
    cut = size - rank // 2
    first_part = jnp.concatenate([scaled_in, subspace[:, :cut]], axis=1)
    last_part = jnp.concatenate([scaled_in, out_rows, subspace[:, cut:]], axis=1)
    mine = jnp.where(here == last, last_part, first_part)
    wide = lax.all_gather(mine, "dp", axis=0, tiled=True)

    small = mm(jnp.concatenate([out_rows, scaled_in, subspace], axis=1), subspace, ((0,), (0,)))
    small = sum_over(small, "dp")
    aux = [(a[:rank], a[rank:]) for a in share_sections(small[: 2 * rank].astype(BF16))]
    gram = small[2 * rank :]

    base_f = base.astype(F32)
    squares = jnp.sum(base_f * base_f, axis=-1, keepdims=True)
    from_base = mm(base, wide)
    from_cot = mm(cotangent, wide[:, rank:])
    projected = share_sections(jnp.concatenate([from_base, from_cot], axis=1).astype(BF16))
    projected = [p.astype(F32) for p in projected]
    base_p = [p[:, :rank] for p in projected]
    ends = rank + cut
    base_s = jnp.concatenate([projected[0][:, rank:ends], projected[last][:, 2 * rank : ends]], axis=1)
    cot_w = projected[last][:, ends : ends + rank]
    cot_s = jnp.concatenate([projected[0][:, ends:], projected[last][:, ends + rank :]], axis=1)
    codes, acts, scaled, t_in, t_out = chain(
        squares, (base_p, base_s), (cot_w, cot_s), aux, gram, width, rank
    )
    my_scaled = pick(scaled, here)
    grad_in = mm(base, my_scaled, ((0,), (0,))).astype(BF16)
    grad_out = mm(cotangent, acts[last], ((0,), (0,))).astype(BF16)
    both = lax.psum_scatter(
        jnp.concatenate([grad_in, grad_out], axis=1), "dp", scatter_dimension=0, tiled=True
    ).astype(F32)
    thin = jnp.concatenate([pick(t_in, here), pick(t_out, here)], axis=1)
    thin = sum_over(thin, "dp")
    lifted = mm(subspace, thin.astype(BF16))
    total_in = own_gain * (both[:, :rank] + lifted[:, :rank])
    total_out = jnp.where(here == last, both[:, rank:], lifted[:, rank:])
    return pick(codes, here)[None], total_in[None], total_out[None]


def solution(mesh):
    placed = (
        P("dp", None),
        P("dp", None),
        P("section", None),
        P("section", "dp", None),
        P("section", "dp", None),
        P("dp", None),
    )
    return jax.shard_map(
        on_device,
        mesh=mesh,
        in_specs=placed,
        out_specs=(P("section", "dp", None), P("section", "dp", None), P("section", "dp", None)),
        check_vma=False,
    )
```

```python
import functools

import jax
import jax.numpy as jnp
from jax import lax
from jax.experimental import pallas as pl
from jax.experimental.pallas import tpu as pltpu
from jax.sharding import PartitionSpec as P

F32 = jnp.float32
BF16 = jnp.bfloat16
VMEM_BYTES = 48 * 1024 * 1024


def mm(a, b, dims=((1,), (0,))):
    return lax.dot_general(a, b, (dims, ((), ())), preferred_element_type=F32)


def exact(a, b, dims=((1,), (0,))):
    return lax.dot_general(
        a.astype(F32),
        b.astype(F32),
        (dims, ((), ())),
        precision=lax.Precision.HIGHEST,
        preferred_element_type=F32,
    )


def swap(value, bits, axis="dp"):
    peers = lax.axis_size(axis)
    return lax.ppermute(value, axis, [(i, i ^ bits) for i in range(peers)])


def share_sections(value):
    sections = lax.axis_size("section")
    here = lax.axis_index("section")
    if sections == 2:
        other = swap(value, 1, "section")
        return [jnp.where(here == 0, value, other), jnp.where(here == 0, other, value)]
    around = [(i, (i + 1) % sections) for i in range(sections)]
    held = [value]
    for _ in range(sections - 1):
        held.append(lax.ppermute(held[-1], "section", around))
    stacked = jnp.stack(held)
    order = (here - jnp.arange(sections)) % sections
    return [lax.dynamic_index_in_dim(stacked, order[s], 0, keepdims=False) for s in range(sections)]


def pick(values, index):
    if len(values) == 2:
        return jnp.where(index == 0, values[0], values[1])
    return lax.dynamic_index_in_dim(jnp.stack(values), index, 0, keepdims=False)


def add_first(ids, base_ref, piece_ref, acc_ref, square_ref, out_ref, squares_ref):
    @pl.when(pl.program_id(0) == 0)
    def _():
        out_ref[...] = acc_ref[...]
        squares_ref[...] = square_ref[...]

    out_ref[...] += mm(base_ref[...], piece_ref[0])
    block = base_ref[...].astype(F32)
    block = block * block
    lanes = squares_ref.shape[1]
    total = squares_ref[...]
    for at in range(0, block.shape[1], lanes):
        total = total + block[:, at : at + lanes]
    squares_ref[...] = total


def project_first(ids, base, pieces, acc, squares):
    rows = base.shape[0]
    count, part, rank = pieces.shape
    whole = lambda a: pl.BlockSpec(a.shape, lambda j, ids: (0, 0))
    return pl.pallas_call(
        add_first,
        grid_spec=pltpu.PrefetchScalarGridSpec(
            num_scalar_prefetch=1,
            grid=(count,),
            in_specs=[
                pl.BlockSpec((rows, part), lambda j, ids: (0, ids[j])),
                pl.BlockSpec((1, part, rank), lambda j, ids: (j, 0, 0)),
                whole(acc),
                whole(squares),
            ],
            out_specs=[whole(acc), whole(squares)],
        ),
        out_shape=[jax.ShapeDtypeStruct(acc.shape, F32), jax.ShapeDtypeStruct(squares.shape, F32)],
        compiler_params=pltpu.CompilerParams(vmem_limit_bytes=VMEM_BYTES),
        cost_estimate=pl.CostEstimate(
            flops=2 * rows * count * part * rank,
            bytes_accessed=2 * count * part * (rows + rank),
            transcendentals=0,
        ),
    )(ids, base, pieces, acc, squares)


def add_second(ids, base_ref, cot_ref, piece_ref, acc_b, acc_c, out_b, out_c):
    @pl.when(pl.program_id(0) == 0)
    def _():
        out_b[...] = acc_b[...]
        out_c[...] = acc_c[...]

    part = base_ref.shape[1]
    rank = piece_ref.shape[2]
    half = part // 2
    at = pl.multiple_of(ids[pl.num_programs(0)] * half, half)
    for tokens, out in ((base_ref, out_b), (cot_ref, out_c)):
        out[:, :rank] += mm(tokens[...], piece_ref[0, :part])
        out[:, rank:] += mm(tokens[:, pl.ds(at, half)], piece_ref[0, part:])


def project_second(ids, base, cotangent, pieces, acc_b, acc_c):
    rows = base.shape[0]
    count, tall, rank = pieces.shape
    part = tall * 2 // 3
    whole = lambda a: pl.BlockSpec(a.shape, lambda j, ids: (0, 0))
    block = pl.BlockSpec((rows, part), lambda j, ids: (0, ids[j]))
    return pl.pallas_call(
        add_second,
        grid_spec=pltpu.PrefetchScalarGridSpec(
            num_scalar_prefetch=1,
            grid=(count,),
            in_specs=[
                block,
                block,
                pl.BlockSpec((1, tall, rank), lambda j, ids: (j, 0, 0)),
                whole(acc_b),
                whole(acc_c),
            ],
            out_specs=[whole(acc_b), whole(acc_c)],
        ),
        out_shape=[jax.ShapeDtypeStruct(acc_b.shape, F32)] * 2,
        compiler_params=pltpu.CompilerParams(vmem_limit_bytes=VMEM_BYTES),
        cost_estimate=pl.CostEstimate(
            flops=4 * rows * count * tall * rank,
            bytes_accessed=2 * count * (2 * part * rows + tall * rank),
            transcendentals=0,
        ),
    )(ids, base, cotangent, pieces, acc_b, acc_c)


def outer_block(ids, small_ref, tokens_ref, out_ref):
    out_ref[0] = mm(small_ref[...], tokens_ref[...]).astype(BF16)


def outer_blocks(ids, small_t, tokens, columns):
    rank, rows = small_t.shape
    count = ids.shape[0]
    return pl.pallas_call(
        outer_block,
        grid_spec=pltpu.PrefetchScalarGridSpec(
            num_scalar_prefetch=1,
            grid=(count,),
            in_specs=[
                pl.BlockSpec((rank, rows), lambda j, ids: (0, 0)),
                pl.BlockSpec((rows, columns), lambda j, ids: (0, ids[j])),
            ],
            out_specs=pl.BlockSpec((1, rank, columns), lambda j, ids: (j, 0, 0)),
        ),
        out_shape=jax.ShapeDtypeStruct((count, rank, columns), BF16),
        compiler_params=pltpu.CompilerParams(vmem_limit_bytes=VMEM_BYTES),
        cost_estimate=pl.CostEstimate(
            flops=2 * rows * count * columns * rank,
            bytes_accessed=2 * count * columns * (rows + rank),
            transcendentals=0,
        ),
    )(ids, small_t, tokens)


def gather_chunk(own, spot):
    peers = lax.axis_size("dp")
    across = swap(own, 2)
    held, marks = own[None], [0]
    bit = peers // 2
    while bit > 2:
        held = jnp.concatenate([held, swap(held, bit)])
        marks = marks + [m ^ bit for m in marks]
        bit //= 2
    beside = jnp.concatenate([across[None], swap(held[1:], 2)])
    other = [swap(held, 1), swap(beside, 1)]
    flips = [0, 2, 1, 3]
    return [
        (jnp.stack([spot ^ (m ^ f) for m in marks]).astype(jnp.int32), shards)
        for f, shards in zip(flips, [held, beside, *other])
    ]


def sum_small(local):
    peers = lax.axis_size("dp")
    core = lax.axis_index("dp") % 2
    half = local.shape[0] // 2
    keep = lax.dynamic_slice_in_dim(local, core * half, half, 0)
    give = lax.dynamic_slice_in_dim(local, (1 - core) * half, half, 0)
    keep = keep + swap(give, 1)
    bit = 2
    while bit < peers:
        keep = keep + swap(keep, bit)
        bit *= 2
    other = swap(keep, 1)
    return jnp.where(
        core == 0, jnp.concatenate([keep, other]), jnp.concatenate([other, keep])
    )


def scatter_sum(spot, small_t, tokens, at, columns, per_part):
    peers = lax.axis_size("dp")
    near = [4 * k for k in range(peers // 4)]
    marks = near + [m ^ 2 for m in near]
    to_ids = lambda who: jnp.stack([(who ^ m) * per_part + at for m in marks]).astype(jnp.int32)
    give = outer_blocks(to_ids(spot ^ 1), small_t, tokens, columns)
    got = swap(give, 1)
    keep = outer_blocks(to_ids(spot), small_t, tokens, columns)
    half = len(near)
    summed = (keep[half:].astype(F32) + got[half:].astype(F32)).astype(BF16)
    got_x = swap(summed, 2)
    total = keep[:half].astype(F32) + got[:half].astype(F32) + got_x.astype(F32)
    sent = total[1:].astype(BF16)
    result = total[0]
    for k, m in enumerate(near[1:]):
        result = result + swap(sent[k], m).astype(F32)
    return result


def on_device(base, cotangent, gain, weight_in, weight_out, subspace):
    sections = lax.axis_size("section")
    here = lax.axis_index("section")
    spot = lax.axis_index("dp")
    rows, width = base.shape
    part, size = subspace.shape
    rank = weight_in.shape[2]
    last = sections - 1
    is_last = here == last
    row_gain = lax.dynamic_slice_in_dim(gain, spot * part, part, 1)
    own_in = (row_gain.reshape(part, 1) * weight_in[0].astype(F32)).astype(BF16)
    own_out = weight_out[0]
    own_rest = jnp.where(
        is_last,
        jnp.concatenate([own_out, subspace[part // 2 :, rank:]]),
        jnp.concatenate([subspace[:, :rank], subspace[: part // 2, rank:]]),
    )
    gram_cols = jnp.where(is_last, subspace[:, rank:], subspace[:, :rank])
    local = jnp.concatenate([mm(a, subspace, ((0,), (0,))) for a in (own_out, own_in, gram_cols)])

    first = gather_chunk(own_in, spot)
    second = gather_chunk(own_rest, spot)
    small = sum_small(local)
    smalls = share_sections(small)

    acc = jnp.zeros((rows, rank), F32)
    squares = jnp.zeros((rows, 128), F32)
    for ids, shards in first:
        acc, squares = project_first(ids, base, shards, acc, squares)
    base_p = share_sections(acc.astype(BF16))
    acc_b = jnp.zeros((rows, 2 * rank), F32)
    acc_c = jnp.zeros((rows, 2 * rank), F32)
    flag = is_last.astype(jnp.int32)[None]
    for ids, shards in second:
        acc_b, acc_c = project_second(
            jnp.concatenate([ids, flag]), base, cotangent, shards, acc_b, acc_c
        )
    from_b = share_sections(acc_b.astype(BF16))
    from_c = share_sections(acc_c.astype(BF16))
    base_p = [p.astype(F32) for p in base_p]
    from_b = [p.astype(F32) for p in from_b]
    from_c = [p.astype(F32) for p in from_c]
    spread = lambda parts: jnp.concatenate(
        [parts[0][:, :rank], parts[0][:, rank:] + parts[last][:, rank:]], axis=1
    )
    base_s, cot_s = spread(from_b), spread(from_c)
    cot_w = from_c[last][:, :rank]
    gram = jnp.concatenate([smalls[0][2 * rank :], smalls[last][2 * rank :]])
    square = jnp.sum(squares, axis=1, keepdims=True)

    acts, codes, inners, inverses, resid_s = [], [], [], [], []
    for s in range(sections):
        m_s, q_t = smalls[s][:rank], smalls[s][rank : 2 * rank]
        if s == 0:
            total, moved, inner = square, None, base_p[s]
            resid_s.append(base_s)
        else:
            moved = exact(codes[-1], gram)
            total = square + jnp.sum(
                (2.0 * base_s + moved) * codes[-1].astype(F32), axis=-1, keepdims=True
            )
            inner = base_p[s] + exact(codes[-1], q_t, ((1,), (1,)))
            resid_s.append(base_s + moved)
        inverse = lax.rsqrt(jnp.maximum(total, 0.0) / width + 1e-05)
        inner = inner * inverse
        active = inner * jax.nn.sigmoid(inner)
        grown = exact(active, m_s)
        codes.append((grown if s == 0 else moved + grown).astype(BF16))
        acts.append(active.astype(BF16))
        inners.append(inner)
        inverses.append(inverse)

    if sections == 2:
        half_out = scatter_sum(spot, acts[last].T, cotangent, flag[0], part // 2, 2)
        whole_out = swap(half_out, 1, "section")
        sum_out = jnp.concatenate([whole_out, half_out], axis=1)
    else:
        sum_out = scatter_sum(spot, acts[last].T, cotangent, 0, part, 1)

    scaled, t_in, t_out = [None] * sections, [None] * sections, [None] * sections
    back = None
    for s in range(last, -1, -1):
        m_s, q_t = smalls[s][:rank], smalls[s][rank : 2 * rank]
        if s == last:
            grad_active, grad_y = cot_w, cot_s
            t_out[s] = jnp.zeros((rank, size), F32)
        else:
            grad_active = exact(back, m_s, ((1,), (1,)))
            grad_y = exact(back, gram) if s > 0 else None
            t_out[s] = mm(acts[s], back, ((0,), (0,)))
        inner, inverse = inners[s], inverses[s]
        logistic = jax.nn.sigmoid(inner)
        grad_inner = grad_active * logistic * (1.0 + inner * (1.0 - logistic))
        scaled[s] = (inverse * grad_inner).astype(BF16)
        if s > 0:
            t_in[s] = mm(scaled[s], codes[s - 1], ((0,), (0,)))
            along = jnp.sum(inner * grad_inner, axis=-1, keepdims=True) * (inverse * inverse / width)
            back = (grad_y + exact(scaled[s], q_t) - resid_s[s] * along).astype(BF16)
        else:
            t_in[s] = jnp.zeros((rank, size), F32)
    scaled_t = pick(scaled, here).T
    halves = [
        scatter_sum(spot, scaled_t, base, k, part // 2, 2) for k in range(2)
    ]
    sum_in = jnp.concatenate(halves, axis=1)
    lift = lambda thin: exact(thin, subspace, ((1,), (1,)))
    if sections == 2:
        lifted = lift(sum_small(jnp.where(is_last, t_in[1], t_out[0])))
        lift_in = jnp.where(is_last, lifted, 0.0)
        lift_out = lifted
    else:
        lift_in = lift(sum_small(pick(t_in, here)))
        lift_out = lift(sum_small(pick(t_out, here)))
    grad_in = (row_gain * (sum_in + lift_in)).T
    grad_out = jnp.where(is_last, sum_out, lift_out).T
    return pick(codes, here)[None], grad_in[None], grad_out[None]


def solution(mesh):
    placed = (
        P("dp", None),
        P("dp", None),
        P("section", None),
        P("section", "dp", None),
        P("section", "dp", None),
        P("dp", None),
    )
    return jax.shard_map(
        on_device,
        mesh=mesh,
        in_specs=placed,
        out_specs=(P("section", "dp", None), P("section", "dp", None), P("section", "dp", None)),
        check_vma=False,
    )
```

```python
import functools

import functools

import jax
import jax.numpy as jnp
from jax import lax
from jax.experimental import pallas as pl
from jax.experimental.pallas import tpu as pltpu
from jax.sharding import PartitionSpec as P

F32 = jnp.float32
BF16 = jnp.bfloat16
VMEM_BYTES = 20 * 1024 * 1024


def mm(a, b, dims=((1,), (0,))):
    return lax.dot_general(a, b, (dims, ((), ())), preferred_element_type=F32)


def exact(a, b, dims=((1,), (0,))):
    return lax.dot_general(
        a.astype(F32),
        b.astype(F32),
        (dims, ((), ())),
        precision=lax.Precision.HIGH,
        preferred_element_type=F32,
    )


def swap(value, bits, axis="dp"):
    peers = lax.axis_size(axis)
    return lax.ppermute(value, axis, [(i, i ^ bits) for i in range(peers)])


def share_sections(value):
    sections = lax.axis_size("section")
    here = lax.axis_index("section")
    if sections == 2:
        other = swap(value, 1, "section")
        return [jnp.where(here == 0, value, other), jnp.where(here == 0, other, value)]
    around = [(i, (i + 1) % sections) for i in range(sections)]
    held = [value]
    for _ in range(sections - 1):
        held.append(lax.ppermute(held[-1], "section", around))
    stacked = jnp.stack(held)
    order = (here - jnp.arange(sections)) % sections
    return [lax.dynamic_index_in_dim(stacked, order[s], 0, keepdims=False) for s in range(sections)]


def share_sections_of(own, sent):
    here = lax.axis_index("section")
    all_sent = share_sections(sent)
    return [jnp.where(here == s, own, v.astype(F32)) for s, v in enumerate(all_sent)]


def pick(values, index):
    if len(values) == 2:
        return jnp.where(index == 0, values[0], values[1])
    return lax.dynamic_index_in_dim(jnp.stack(values), index, 0, keepdims=False)


def after(value, *others):
    return lax.optimization_barrier((value, *others))[0]


def project_kernel(count, ids, base_ref, cot_ref, gain_ref, *refs):
    pieces, acc_ref, out_ref = refs[:count], refs[count], refs[count + 1]
    tall, rank = pieces[0].shape
    part = tall * 2 // 5
    half = part // 2
    out_ref[...] = acc_ref[...]
    skip = ids[count] * half
    for t, piece in enumerate(pieces):
        start = pl.multiple_of(ids[t] * part, part)
        half_start = pl.multiple_of(start + skip, half)
        block = base_ref[:, pl.ds(start, part)]
        block_f = block.astype(F32)
        normed = (block_f * gain_ref[:, pl.ds(start, part)]).astype(BF16)
        square = block_f * block_f
        lanes = out_ref.shape[1] - 5 * rank
        total = square[:, :lanes]
        for at in range(lanes, part, lanes):
            total = total + square[:, at : at + lanes]
        out_ref[:, :rank] += mm(normed, piece[:part])
        out_ref[:, rank : 2 * rank] += mm(block, piece[part : 2 * part])
        out_ref[:, 2 * rank : 3 * rank] += mm(
            base_ref[:, pl.ds(half_start, half)], piece[2 * part :]
        )
        out_ref[:, 3 * rank : 4 * rank] += mm(
            cot_ref[:, pl.ds(start, part)], piece[part : 2 * part]
        )
        out_ref[:, 4 * rank : 5 * rank] += mm(
            cot_ref[:, pl.ds(half_start, half)], piece[2 * part :]
        )
        out_ref[:, 5 * rank :] += total
    if len(refs) > count + 2:
        refs[count + 2][...] = out_ref[:, : 3 * rank].astype(BF16)
        refs[count + 3][...] = out_ref[:, 3 * rank : 5 * rank].astype(BF16)


def project(ids, base, cotangent, gain, pieces, acc, rounded=False):
    rows = base.shape[0]
    count = len(pieces)
    tall, rank = pieces[0].shape
    in_vmem = pl.BlockSpec(memory_space=pltpu.VMEM)
    shapes = [jax.ShapeDtypeStruct(acc.shape, F32)]
    if rounded:
        shapes += [
            jax.ShapeDtypeStruct((rows, 3 * rank), BF16),
            jax.ShapeDtypeStruct((rows, 2 * rank), BF16),
        ]
    return pl.pallas_call(
        functools.partial(project_kernel, count),
        in_specs=[pl.BlockSpec(memory_space=pltpu.SMEM)] + [in_vmem] * (count + 4),
        out_specs=[in_vmem] * len(shapes),
        out_shape=shapes,
        compiler_params=pltpu.CompilerParams(vmem_limit_bytes=VMEM_BYTES),
        cost_estimate=pl.CostEstimate(
            flops=4 * rows * count * tall * rank,
            bytes_accessed=2 * count * tall * (rows + rank),
            transcendentals=0,
        ),
    )(ids, base, cotangent, gain, *pieces, acc)


def outer_kernel(ids, small_ref, tokens_ref, *outs):
    small = small_ref[...]
    at = 0
    for out in outs:
        count, _, columns = out.shape
        for j in range(count):
            start = pl.multiple_of(ids[at] * columns, columns)
            out[j] = mm(small, tokens_ref[:, pl.ds(start, columns)]).astype(BF16)
            at += 1


def outer_blocks(id_lists, small_t, tokens, columns):
    rank, rows = small_t.shape
    counts = [len(ids) for ids in id_lists]
    in_vmem = pl.BlockSpec(memory_space=pltpu.VMEM)
    return pl.pallas_call(
        outer_kernel,
        in_specs=[pl.BlockSpec(memory_space=pltpu.SMEM), in_vmem, in_vmem],
        out_specs=[in_vmem] * len(counts),
        out_shape=[jax.ShapeDtypeStruct((n, rank, columns), BF16) for n in counts],
        compiler_params=pltpu.CompilerParams(vmem_limit_bytes=VMEM_BYTES),
        cost_estimate=pl.CostEstimate(
            flops=2 * rows * sum(counts) * columns * rank,
            bytes_accessed=2 * sum(counts) * columns * (rows + rank),
            transcendentals=0,
        ),
    )(jnp.stack(sum(id_lists, [])).astype(jnp.int32), small_t, tokens)


def gather_shards(own):
    peers = lax.axis_size("dp")
    held = {0: own}
    bit = peers // 2
    while bit > 2:
        for m in list(held):
            held[m ^ bit] = swap(held[m], bit)
        bit //= 2
    near = sorted(held)
    sent = []
    for m in near:
        value = held[m]
        if len(sent) > 1:
            value = after(value, sent[-2])
        held[m ^ 2] = swap(value, 2)
        sent.append(held[m ^ 2])
    for m in list(held):
        held[m ^ 1] = swap(held[m], 1)
    return near, held


def sum_small(local, wait_for):
    peers = lax.axis_size("dp")
    core = lax.axis_index("dp") % 2
    half = local.shape[0] // 2
    keep = lax.dynamic_slice_in_dim(local, core * half, half, 0)
    give = lax.dynamic_slice_in_dim(local, (1 - core) * half, half, 0)
    keep = after(keep + swap(give, 1), wait_for)
    bit = peers // 2
    while bit > 2:
        keep = keep + swap(keep, bit)
        bit //= 2
    return keep + swap(keep.astype(BF16), 2).astype(F32)


def sum_thin(value):
    peers = lax.axis_size("dp")
    bit = 1
    while bit < peers:
        value = value + swap(value, bit)
        bit *= 2
    return value


def block_marks():
    near = [4 * k for k in range(lax.axis_size("dp") // 4)]
    return near, near + [m ^ 2 for m in near]


def scatter_sum(give, keep):
    near, _ = block_marks()
    half = len(near)
    got = swap(give, 1)
    summed = (keep[half:].astype(F32) + got[half:].astype(F32)).astype(BF16)
    got_x = swap(summed, 2)
    total = keep[:half].astype(F32) + got[:half].astype(F32) + got_x.astype(F32)
    sent = total[1:].astype(BF16)
    result = total[0]
    for k, m in enumerate(near[1:]):
        result = result + swap(sent[k], m).astype(F32)
    return result


def on_device(base, cotangent, gain, weight_in, weight_out, subspace):
    sections = lax.axis_size("section")
    here = lax.axis_index("section")
    spot = lax.axis_index("dp")
    rows, width = base.shape
    part, size = subspace.shape
    rank = weight_in.shape[2]
    last = sections - 1
    is_last = here == last
    flag = is_last.astype(jnp.int32)
    own_in, own_out = weight_in[0], weight_out[0]
    own = jnp.where(
        is_last,
        jnp.concatenate([own_in, own_out, subspace[part // 2 :, rank:]]),
        jnp.concatenate([own_in, subspace[:, :rank], subspace[: part // 2, rank:]]),
    )
    near, shards = gather_shards(own)

    row_gain = lax.dynamic_slice_in_dim(gain, spot * part, part, 1)
    scaled_in = (row_gain.reshape(part, 1) * own_in.astype(F32)).astype(BF16)
    gram_cols = jnp.where(is_last, subspace[:, rank:], subspace[:, :rank])
    local = jnp.concatenate([mm(a, subspace, ((0,), (0,))) for a in (own_out, scaled_in, gram_cols)])
    small = sum_small(local, shards[4])
    halves = share_sections(small)
    core = spot % 2
    mine = jnp.stack(halves)
    other = swap(mine, 1)
    smalls = jnp.where(
        core == 0,
        jnp.concatenate([mine, other], axis=1),
        jnp.concatenate([other, mine], axis=1),
    )

    acc = jnp.zeros((rows, 6 * rank), F32)
    marks = [
        near,
        [m ^ 1 for m in near],
        [m ^ 2 for m in near[:-1]] + [m ^ 3 for m in near[:-1]],
        [near[-1] ^ 2, near[-1] ^ 3],
    ]
    for k, some in enumerate(marks):
        ids = jnp.stack([spot ^ m for m in some] + [flag]).astype(jnp.int32)
        acc, *rounded = project(
            ids, base, cotangent, gain, [shards[m] for m in some], acc, k == len(marks) - 1
        )
    from_b = [p.astype(F32) for p in share_sections_of(acc[:, : 3 * rank], rounded[0])]
    from_c = [p.astype(F32) for p in share_sections_of(acc[:, 3 * rank : 5 * rank], rounded[1])]
    base_p = [p[:, :rank] for p in from_b]
    base_s = jnp.concatenate(
        [from_b[0][:, rank : 2 * rank], from_b[0][:, 2 * rank :] + from_b[last][:, 2 * rank :]], axis=1
    )
    cot_s = jnp.concatenate(
        [from_c[0][:, :rank], from_c[0][:, rank:] + from_c[last][:, rank:]], axis=1
    )
    cot_w = from_c[last][:, :rank]
    gram = jnp.concatenate([smalls[0, 2 * rank :], smalls[last, 2 * rank :]])
    square = jnp.sum(acc[:, 5 * rank :], axis=1, keepdims=True)

    acts, codes, inners, inverses, resid_s = [], [], [], [], []
    for s in range(sections):
        m_s, q_t = smalls[s, :rank], smalls[s, rank : 2 * rank]
        if s == 0:
            total, moved, inner = square, None, base_p[s]
            resid_s.append(base_s)
        else:
            moved = exact(codes[-1], gram)
            total = square + jnp.sum(
                (2.0 * base_s + moved) * codes[-1].astype(F32), axis=-1, keepdims=True
            )
            inner = base_p[s] + exact(codes[-1], q_t, ((1,), (1,)))
            resid_s.append(base_s + moved)
        inverse = lax.rsqrt(jnp.maximum(total, 0.0) / width + 1e-05)
        inner = inner * inverse
        active = inner * jax.nn.sigmoid(inner)
        grown = exact(active, m_s)
        codes.append((grown if s == 0 else moved + grown).astype(BF16))
        acts.append(active.astype(BF16))
        inners.append(inner)
        inverses.append(inverse)

    _, every = block_marks()
    if sections == 2:
        ids = [[(who ^ m) * 2 + flag for m in every] for who in (spot ^ 1, spot)]
        half_out = scatter_sum(*outer_blocks(ids, acts[last].T, cotangent, part // 2))
        whole_out = swap(half_out, 1, "section")
        sum_out = jnp.concatenate([whole_out, half_out], axis=1)
    else:
        ids = [[who ^ m for m in every] for who in (spot ^ 1, spot)]
        sum_out = scatter_sum(*outer_blocks(ids, acts[last].T, cotangent, part))

    scaled, t_in, t_out = [None] * sections, [None] * sections, [None] * sections
    back = None
    for s in range(last, -1, -1):
        m_s, q_t = smalls[s, :rank], smalls[s, rank : 2 * rank]
        if s == last:
            grad_active, grad_y = cot_w, cot_s
            t_out[s] = jnp.zeros((rank, size), F32)
        else:
            grad_active = exact(back, m_s, ((1,), (1,)))
            grad_y = exact(back, gram) if s > 0 else None
            t_out[s] = mm(acts[s], back, ((0,), (0,)))
        inner, inverse = inners[s], inverses[s]
        logistic = jax.nn.sigmoid(inner)
        grad_inner = grad_active * logistic * (1.0 + inner * (1.0 - logistic))
        scaled[s] = (inverse * grad_inner).astype(BF16)
        if s > 0:
            t_in[s] = mm(scaled[s], codes[s - 1], ((0,), (0,)))
            along = jnp.sum(inner * grad_inner, axis=-1, keepdims=True) * (inverse * inverse / width)
            back = (grad_y + exact(scaled[s], q_t) - resid_s[s] * along).astype(BF16)
        else:
            t_in[s] = jnp.zeros((rank, size), F32)
    scaled_t = pick(scaled, here).T
    ids = [[(who ^ m) * 2 + k for m in every] for k in range(2) for who in (spot ^ 1, spot)]
    blocks = outer_blocks(ids, scaled_t, base, part // 2)
    sum_in = jnp.concatenate([scatter_sum(*blocks[:2]), scatter_sum(*blocks[2:])], axis=1)
    lift = lambda thin: exact(thin, subspace, ((1,), (1,)))
    if sections == 2:
        lifted = lift(sum_thin(jnp.where(is_last, t_in[1], t_out[0])))
        lift_in = jnp.where(is_last, lifted, 0.0)
        lift_out = lifted
    else:
        lift_in = lift(sum_thin(pick(t_in, here)))
        lift_out = lift(sum_thin(pick(t_out, here)))
    grad_in = (row_gain * (sum_in + lift_in)).T
    grad_out = jnp.where(is_last, sum_out, lift_out).T
    return pick(codes, here)[None], grad_in[None], grad_out[None]


def solution(mesh):
    placed = (
        P("dp", None),
        P("dp", None),
        P("section", None),
        P("section", "dp", None),
        P("section", "dp", None),
        P("dp", None),
    )
    return jax.shard_map(
        on_device,
        mesh=mesh,
        in_specs=placed,
        out_specs=(P("section", "dp", None), P("section", "dp", None), P("section", "dp", None)),
        check_vma=False,
    )
```

```python
import functools

import functools

import jax
import jax.numpy as jnp
from jax import lax
from jax.experimental import pallas as pl
from jax.experimental.pallas import tpu as pltpu
from jax.sharding import PartitionSpec as P

F32 = jnp.float32
BF16 = jnp.bfloat16
VMEM_BYTES = 20 * 1024 * 1024


def mm(a, b, dims=((1,), (0,))):
    return lax.dot_general(a, b, (dims, ((), ())), preferred_element_type=F32)


def exact(a, b, dims=((1,), (0,))):
    return lax.dot_general(
        a.astype(F32),
        b.astype(F32),
        (dims, ((), ())),
        precision=lax.Precision.HIGH,
        preferred_element_type=F32,
    )


def swap(value, bits, axis="dp"):
    peers = lax.axis_size(axis)
    return lax.ppermute(value, axis, [(i, i ^ bits) for i in range(peers)])


def share_sections(value):
    sections = lax.axis_size("section")
    here = lax.axis_index("section")
    if sections == 2:
        other = swap(value, 1, "section")
        return [jnp.where(here == 0, value, other), jnp.where(here == 0, other, value)]
    around = [(i, (i + 1) % sections) for i in range(sections)]
    held = [value]
    for _ in range(sections - 1):
        held.append(lax.ppermute(held[-1], "section", around))
    stacked = jnp.stack(held)
    order = (here - jnp.arange(sections)) % sections
    return [lax.dynamic_index_in_dim(stacked, order[s], 0, keepdims=False) for s in range(sections)]


def share_sections_of(own, sent):
    here = lax.axis_index("section")
    all_sent = share_sections(sent)
    return [jnp.where(here == s, own, v.astype(F32)) for s, v in enumerate(all_sent)]


def pick(values, index):
    if len(values) == 2:
        return jnp.where(index == 0, values[0], values[1])
    return lax.dynamic_index_in_dim(jnp.stack(values), index, 0, keepdims=False)


def after(value, *others):
    return lax.optimization_barrier((value, *others))[0]


def rest_kernel(count, ids, base_ref, cot_ref, *refs):
    pieces, acc_ref, out_ref = refs[:count], refs[count], refs[count + 1]
    tall, rank = pieces[0].shape
    part = tall * 2 // 3
    half = part // 2
    out_ref[...] = acc_ref[...]
    skip = ids[count] * half
    for t, piece in enumerate(pieces):
        start = pl.multiple_of(ids[t] * part, part)
        half_start = pl.multiple_of(start + skip, half)
        for at, tokens in ((0, base_ref), (2 * rank, cot_ref)):
            out_ref[:, at : at + rank] += mm(tokens[:, pl.ds(start, part)], piece[:part])
            out_ref[:, at + rank : at + 2 * rank] += mm(
                tokens[:, pl.ds(half_start, half)], piece[part:]
            )
    if len(refs) > count + 2:
        refs[count + 2][...] = out_ref[...].astype(BF16)


def in_kernel(count, ids, base_ref, gain_ref, *refs):
    pieces, acc_ref, out_ref = refs[:count], refs[count], refs[count + 1]
    part, rank = pieces[0].shape
    out_ref[...] = acc_ref[...]
    lanes = out_ref.shape[1] - rank
    for t, piece in enumerate(pieces):
        start = pl.multiple_of(ids[t] * part, part)
        block = base_ref[:, pl.ds(start, part)].astype(F32)
        normed = (block * gain_ref[:, pl.ds(start, part)]).astype(BF16)
        square = block * block
        total = square[:, :lanes]
        for at in range(lanes, part, lanes):
            total = total + square[:, at : at + lanes]
        out_ref[:, :rank] += mm(normed, piece[...])
        out_ref[:, rank:] += total
    if len(refs) > count + 2:
        refs[count + 2][...] = out_ref[:, :rank].astype(BF16)


def project(kernel, ids, tokens, pieces, acc, rounded_width):
    rows = acc.shape[0]
    count = len(pieces)
    tall, rank = pieces[0].shape
    in_vmem = pl.BlockSpec(memory_space=pltpu.VMEM)
    shapes = [jax.ShapeDtypeStruct(acc.shape, F32)]
    if rounded_width:
        shapes.append(jax.ShapeDtypeStruct((rows, rounded_width), BF16))
    return pl.pallas_call(
        functools.partial(kernel, count),
        in_specs=[pl.BlockSpec(memory_space=pltpu.SMEM)] + [in_vmem] * (count + 1 + len(tokens)),
        out_specs=[in_vmem] * len(shapes),
        out_shape=shapes,
        compiler_params=pltpu.CompilerParams(vmem_limit_bytes=VMEM_BYTES),
        cost_estimate=pl.CostEstimate(
            flops=4 * rows * count * tall * rank,
            bytes_accessed=2 * count * tall * (rows + rank),
            transcendentals=0,
        ),
    )(ids, *tokens, *pieces, acc)


def outer_kernel(ids, small_ref, tokens_ref, *outs):
    small = small_ref[...]
    at = 0
    for out in outs:
        count, _, columns = out.shape
        for j in range(count):
            start = pl.multiple_of(ids[at] * columns, columns)
            out[j] = mm(small, tokens_ref[:, pl.ds(start, columns)]).astype(BF16)
            at += 1


def outer_blocks(id_lists, small_t, tokens, columns):
    rank, rows = small_t.shape
    counts = [len(ids) for ids in id_lists]
    in_vmem = pl.BlockSpec(memory_space=pltpu.VMEM)
    return pl.pallas_call(
        outer_kernel,
        in_specs=[pl.BlockSpec(memory_space=pltpu.SMEM), in_vmem, in_vmem],
        out_specs=[in_vmem] * len(counts),
        out_shape=[jax.ShapeDtypeStruct((n, rank, columns), BF16) for n in counts],
        compiler_params=pltpu.CompilerParams(vmem_limit_bytes=VMEM_BYTES),
        cost_estimate=pl.CostEstimate(
            flops=2 * rows * sum(counts) * columns * rank,
            bytes_accessed=2 * sum(counts) * columns * (rows + rank),
            transcendentals=0,
        ),
    )(jnp.stack(sum(id_lists, [])).astype(jnp.int32), small_t, tokens)


def gather_shards(own):
    peers = lax.axis_size("dp")
    order = sorted(range(4, peers, 4), key=lambda m: (m.bit_count(), m))
    held = {0: own}
    for m in order:
        if m.bit_count() == 1:
            held[m] = swap(own, m)
    held[2] = swap(own, 2)
    for k, m in enumerate(order):
        low = m & -m
        before = held[(order[k - 1] if k else 0) ^ 2]
        if m != low:
            held[m] = swap(after(held[m ^ low], held[order[k - 2] ^ 2]), low)
        held[m ^ 2] = swap(after(held[m], before), 2)
    for m in list(held):
        held[m ^ 1] = swap(held[m], 1)
    return [0] + order, held


def sum_small(local, wait_for):
    peers = lax.axis_size("dp")
    core = lax.axis_index("dp") % 2
    half = local.shape[0] // 2
    keep = lax.dynamic_slice_in_dim(local, core * half, half, 0)
    give = lax.dynamic_slice_in_dim(local, (1 - core) * half, half, 0)
    keep = after(keep + swap(give, 1), wait_for)
    bit = peers // 2
    while bit > 2:
        keep = keep + swap(keep, bit)
        bit //= 2
    return keep + swap(keep.astype(BF16), 2).astype(F32)


def sum_thin(value, waits):
    peers = lax.axis_size("dp")
    bit, step = 1, 0
    while bit < peers:
        if step:
            value = after(value, waits[min(step, len(waits)) - 1])
        value = value + swap(value, bit)
        bit, step = bit * 2, step + 1
    return value


def block_marks():
    near = [4 * k for k in range(lax.axis_size("dp") // 4)]
    return near, near + [m ^ 2 for m in near]


def scatter_sum(give, keep):
    near, _ = block_marks()
    half = len(near)
    got = swap(give, 1)
    summed = (keep[half:].astype(F32) + got[half:].astype(F32)).astype(BF16)
    got_x = swap(summed, 2)
    total = keep[:half].astype(F32) + got[:half].astype(F32) + got_x.astype(F32)
    sent = total[1:].astype(BF16)
    result = total[0]
    for k, m in enumerate(near[1:]):
        result = result + swap(sent[k], m).astype(F32)
    return result, got, got_x


def on_device(base, cotangent, gain, weight_in, weight_out, subspace):
    sections = lax.axis_size("section")
    here = lax.axis_index("section")
    spot = lax.axis_index("dp")
    rows, width = base.shape
    part, size = subspace.shape
    rank = weight_in.shape[2]
    last = sections - 1
    is_last = here == last
    flag = is_last.astype(jnp.int32)
    own_in, own_out = weight_in[0], weight_out[0]
    own_rest = jnp.where(
        is_last,
        jnp.concatenate([own_out, subspace[part // 2 :, rank:]]),
        jnp.concatenate([subspace[:, :rank], subspace[: part // 2, rank:]]),
    )
    near, rest = gather_shards(own_rest)
    _, ins = gather_shards(own_in)

    row_gain = lax.dynamic_slice_in_dim(gain, spot * part, part, 1)
    gram_cols = jnp.where(is_last, subspace[:, rank:], subspace[:, :rank])
    late_in, late_out, late_gram, late_space, _ = lax.optimization_barrier(
        (own_in, own_out, gram_cols, subspace, ins[4])
    )
    scaled_in = (row_gain.reshape(part, 1) * late_in.astype(F32)).astype(BF16)
    local = jnp.concatenate(
        [mm(a, late_space, ((0,), (0,))) for a in (late_out, scaled_in, late_gram)]
    )
    small = sum_small(local, rest[4])
    mine = jnp.stack(share_sections(small))
    other = swap(mine, 1)
    smalls = jnp.where(
        spot % 2 == 0,
        jnp.concatenate([mine, other], axis=1),
        jnp.concatenate([other, mine], axis=1),
    )

    marks = [
        near,
        [m ^ 1 for m in near],
        [m ^ 2 for m in near[:-1]] + [m ^ 3 for m in near[:-1]],
        [near[-1] ^ 2, near[-1] ^ 3],
    ]
    acc_rest = jnp.zeros((rows, 4 * rank), F32)
    acc_in = jnp.zeros((rows, 2 * rank), F32)
    for k, some in enumerate(marks):
        ids = jnp.stack([spot ^ m for m in some] + [flag]).astype(jnp.int32)
        final = k == len(marks) - 1
        acc_rest, *sent_rest = project(
            rest_kernel, ids, (base, cotangent), [rest[m] for m in some], acc_rest, final * 4 * rank
        )
        acc_in, *sent_in = project(
            in_kernel, ids, (base, gain), [ins[m] for m in some], acc_in, final * rank
        )
    wide = share_sections_of(acc_rest, sent_rest[0])
    base_p = share_sections_of(acc_in[:, :rank], sent_in[0])
    split = lambda at: jnp.concatenate(
        [
            wide[0][:, at : at + rank],
            wide[0][:, at + rank : at + 2 * rank] + wide[last][:, at + rank : at + 2 * rank],
        ],
        axis=1,
    )
    base_s, cot_s = split(0), split(2 * rank)
    cot_w = wide[last][:, 2 * rank : 3 * rank]
    gram = jnp.concatenate([smalls[0, 2 * rank :], smalls[last, 2 * rank :]])
    square = jnp.sum(acc_in[:, rank:], axis=1, keepdims=True)

    acts, codes, inners, inverses, resid_s = [], [], [], [], []
    for s in range(sections):
        m_s, q_t = smalls[s, :rank], smalls[s, rank : 2 * rank]
        if s == 0:
            total, moved, inner = square, None, base_p[s]
            resid_s.append(base_s)
        else:
            moved = exact(codes[-1], gram)
            total = square + jnp.sum(
                (2.0 * base_s + moved) * codes[-1].astype(F32), axis=-1, keepdims=True
            )
            inner = base_p[s] + exact(codes[-1], q_t, ((1,), (1,)))
            resid_s.append(base_s + moved)
        inverse = lax.rsqrt(jnp.maximum(total, 0.0) / width + 1e-05)
        inner = inner * inverse
        active = inner * jax.nn.sigmoid(inner)
        grown = exact(active, m_s)
        codes.append((grown if s == 0 else moved + grown).astype(BF16))
        acts.append(active.astype(BF16))
        inners.append(inner)
        inverses.append(inverse)

    _, every = block_marks()
    if sections == 2:
        ids = [[(who ^ m) * 2 + flag for m in every] for who in (spot ^ 1, spot)]
        half_out, got_first, got_x = scatter_sum(*outer_blocks(ids, acts[last].T, cotangent, part // 2))
        whole_out = swap(half_out, 1, "section")
        sum_out = jnp.concatenate([whole_out, half_out], axis=1)
    else:
        ids = [[who ^ m for m in every] for who in (spot ^ 1, spot)]
        sum_out, got_first, got_x = scatter_sum(*outer_blocks(ids, acts[last].T, cotangent, part))

    scaled, t_in, t_out = [None] * sections, [None] * sections, [None] * sections
    back = None
    for s in range(last, -1, -1):
        m_s, q_t = smalls[s, :rank], smalls[s, rank : 2 * rank]
        if s == last:
            grad_active, grad_y = cot_w, cot_s
            t_out[s] = jnp.zeros((rank, size), F32)
        else:
            grad_active = exact(back, m_s, ((1,), (1,)))
            grad_y = exact(back, gram) if s > 0 else None
            t_out[s] = mm(acts[s], back, ((0,), (0,)))
        inner, inverse = inners[s], inverses[s]
        logistic = jax.nn.sigmoid(inner)
        grad_inner = grad_active * logistic * (1.0 + inner * (1.0 - logistic))
        scaled[s] = (inverse * grad_inner).astype(BF16)
        if s > 0:
            t_in[s] = mm(scaled[s], codes[s - 1], ((0,), (0,)))
            along = jnp.sum(inner * grad_inner, axis=-1, keepdims=True) * (inverse * inverse / width)
            back = (grad_y + exact(scaled[s], q_t) - resid_s[s] * along).astype(BF16)
        else:
            t_in[s] = jnp.zeros((rank, size), F32)
    scaled_t = after(pick(scaled, here).T, got_first)
    ids = [[(who ^ m) * 2 + k for m in every] for k in range(2) for who in (spot ^ 1, spot)]
    blocks = outer_blocks(ids, scaled_t, base, part // 2)
    lower, upper = scatter_sum(*blocks[:2]), scatter_sum(*blocks[2:])
    sum_in = jnp.concatenate([lower[0], upper[0]], axis=1)
    waits = [got_x, lower[2], upper[2]]
    lift = lambda thin: exact(thin, subspace, ((1,), (1,)))
    if sections == 2:
        lifted = lift(sum_thin(jnp.where(is_last, t_in[1], t_out[0]), waits))
        lift_in = jnp.where(is_last, lifted, 0.0)
        lift_out = lifted
    else:
        lift_in = lift(sum_thin(pick(t_in, here), waits))
        lift_out = lift(sum_thin(pick(t_out, here), waits))
    grad_in = (row_gain * (sum_in + lift_in)).T
    grad_out = jnp.where(is_last, sum_out, lift_out).T
    return pick(codes, here)[None], grad_in[None], grad_out[None]


def solution(mesh):
    placed = (
        P("dp", None),
        P("dp", None),
        P("section", None),
        P("section", "dp", None),
        P("section", "dp", None),
        P("dp", None),
    )
    return jax.shard_map(
        on_device,
        mesh=mesh,
        in_specs=placed,
        out_specs=(P("section", "dp", None), P("section", "dp", None), P("section", "dp", None)),
        check_vma=False,
    )
```

```python
import functools

import jax
import jax.numpy as jnp
from jax import lax
from jax.experimental import pallas as pl
from jax.experimental.pallas import tpu as pltpu
from jax.sharding import PartitionSpec as P

F32 = jnp.float32
BF16 = jnp.bfloat16
VMEM_BYTES = 12 * 1024 * 1024
IN_VMEM = pl.BlockSpec(memory_space=pltpu.VMEM)
IN_SMEM = pl.BlockSpec(memory_space=pltpu.SMEM)
CONTRACT = ((1,), (0,))
ROWS = ((0,), (0,))
COLUMNS = ((1,), (1,))


def mm(a, b, dims=CONTRACT):
    return lax.dot_general(a, b, (dims, ((), ())), preferred_element_type=F32)


def parts_of(a):
    if a.dtype == BF16:
        return [a]
    high = a.astype(BF16)
    return [high, (a - high.astype(F32)).astype(BF16)]


def exact(a, b, dims=CONTRACT):
    left, right = parts_of(a), parts_of(b)
    total = mm(left[0], right[0], dims)
    for i, x in enumerate(left):
        for j, y in enumerate(right):
            if i + j == 1:
                total = total + mm(x, y, dims)
    return total


def call(kernel, scalars, arrays, shapes, flops, vmem_bytes=VMEM_BYTES):
    size = lambda shape, dtype: jnp.dtype(dtype).itemsize * functools.reduce(lambda x, y: x * y, shape, 1)
    moved = sum(size(a.shape, a.dtype) for a in arrays) + sum(size(*s) for s in shapes)
    return pl.pallas_call(
        kernel,
        in_specs=[IN_SMEM] + [IN_VMEM] * len(arrays),
        out_specs=[IN_VMEM] * len(shapes),
        out_shape=[jax.ShapeDtypeStruct(*s) for s in shapes],
        compiler_params=pltpu.CompilerParams(vmem_limit_bytes=vmem_bytes),
        cost_estimate=pl.CostEstimate(flops=flops, bytes_accessed=moved, transcendentals=0),
    )(jnp.stack(scalars).astype(jnp.int32), *arrays)


def swap(value, bits, axis="dp"):
    peers = lax.axis_size(axis)
    return lax.ppermute(value, axis, [(i, i ^ bits) for i in range(peers)])


def after(value, *others):
    return lax.optimization_barrier((value, *others))[0]


def from_sections(value):
    sections = lax.axis_size("section")
    here = lax.axis_index("section")
    if sections == 2:
        return [swap(value, 1, "section")]
    around = [(i, (i + 1) % sections) for i in range(sections)]
    held = [value]
    for _ in range(sections - 1):
        held.append(lax.ppermute(held[-1], "section", around))
    stacked = jnp.stack(held)
    order = (here - jnp.arange(sections)) % sections
    return [lax.dynamic_index_in_dim(stacked, order[s], 0, keepdims=False) for s in range(sections)]


def own_kernel(scalars, in_ref, out_ref, space_ref, own_ref):
    is_last = scalars[0] == 1
    part, rank = in_ref.shape
    half = part // 2
    own_ref[:part] = in_ref[...]
    own_ref[part : 2 * part] = jnp.where(is_last, out_ref[...], space_ref[:, :rank])
    own_ref[2 * part :] = jnp.where(is_last, space_ref[half:, rank:], space_ref[:half, rank:])


def small_kernel(scalars, in_ref, out_ref, space_ref, gain_ref, keep_ref, give_ref, all_ref):
    is_last, core = scalars[0] == 1, scalars[1]
    part, rank = in_ref.shape
    space = space_ref[...]
    start = pl.multiple_of(scalars[2] * part, part)
    scaled_t = in_ref[...].astype(F32).T * gain_ref[:, pl.ds(start, part)]
    all_ref[:rank] = mm(out_ref[...], space, ROWS)
    all_ref[rank : 2 * rank] = mm(scaled_t.astype(BF16), space)
    columns = jnp.where(is_last, space_ref[:, rank:], space_ref[:, :rank])
    all_ref[2 * rank :] = mm(columns, space, ROWS)
    half = keep_ref.shape[0]
    first, second = all_ref[:half], all_ref[half:]
    keep_ref[...] = jnp.where(core == 0, first, second)
    give_ref[...] = jnp.where(core == 0, second, first)


def project_kernel(shape, stack, with_base, with_cot, count, scalars, *refs):
    tall, rank = shape
    part = tall * 2 // 5
    half = part // 2
    skip = scalars[count] * half
    refs = list(refs)
    take = lambda n: [refs.pop(0) for _ in range(n)]
    base_ref, gain_ref = take(2) if with_base else (None, None)
    cot_ref = take(1)[0] if with_cot else None
    shards = []
    while len(shards) < count:
        ref = refs.pop(0)
        shards += [ref] if len(ref.shape) == 2 else [ref.at[i] for i in range(ref.shape[0])]
    acc_b = take(1)[0] if with_base else None
    acc_c = take(1)[0] if with_cot else None
    out_b = take(1)[0] if with_base else None
    out_c = take(1)[0] if with_cot else None
    if with_base:
        out_b[...] = acc_b[...]
    if with_cot:
        out_c[...] = acc_c[...]
    for t, shard in enumerate(shards):
        start = pl.multiple_of(scalars[t] * part, part)
        half_start = pl.multiple_of(start + skip, half)
        if with_base:
            block = base_ref[:, pl.ds(start, part)]
            block_f = block.astype(F32)
            normed = (block_f * gain_ref[:, pl.ds(start, part)]).astype(BF16)
            square = block_f * block_f
            total = square[:, :rank]
            for at in range(rank, part, rank):
                total = total + square[:, at : at + rank]
            out_b[:, :rank] += mm(normed, shard[:part])
            out_b[:, rank : 2 * rank] += mm(block, shard[part : 2 * part])
            out_b[:, 2 * rank : 3 * rank] += mm(
                base_ref[:, pl.ds(half_start, half)], shard[2 * part :]
            )
            out_b[:, 3 * rank :] += total
        if with_cot:
            out_c[:, :rank] += mm(cot_ref[:, pl.ds(start, part)], shard[part : 2 * part])
            out_c[:, rank:] += mm(cot_ref[:, pl.ds(half_start, half)], shard[2 * part :])
        if stack:
            refs[0][t] = shard[...]
    if not stack and refs:
        if with_base:
            refs.pop(0)[...] = out_b[:, : 3 * rank].astype(BF16)
        if with_cot:
            refs.pop(0)[...] = out_c[...].astype(BF16)


def project(ids, flag, shards, base=None, cot=None, stack=False, final=False):
    tall, rank = shards[0].shape[-2:]
    count = len(ids)
    tokens, accs, shapes, rounded = [], [], [], []
    if base:
        rows = base[0].shape[0]
        tokens += base[:2]
        accs.append(base[2])
        shapes.append(((rows, 4 * rank), F32))
        rounded.append(((rows, 3 * rank), BF16))
    if cot:
        rows = cot[0].shape[0]
        tokens += cot[:1]
        accs.append(cot[1])
        shapes.append(((rows, 2 * rank), F32))
        rounded.append(((rows, 2 * rank), BF16))
    if stack:
        shapes.append(((count, tall, rank), BF16))
    if final:
        shapes += rounded
    kernel = functools.partial(project_kernel, (tall, rank), stack, bool(base), bool(cot), count)
    flops = 2 * rows * count * tall * rank * len(accs)
    return call(kernel, [*ids, flag], [*tokens, *shards, *accs], shapes, flops)


def outer_into(scalars, at, small, tokens_ref, outs):
    for out in outs:
        count, _, columns = out.shape
        for j in range(count):
            start = pl.multiple_of(scalars[at] * columns, columns)
            out[j] = mm(small, tokens_ref[:, pl.ds(start, columns)]).astype(BF16)
            at += 1


def small_parts(sections, here, core, keeps, others, s):
    value = lambda refs: (
        jnp.where(here == s, refs[0][...], refs[1][...]) if sections == 2 else refs[1 + s][...]
    )
    mine, theirs = value(keeps), value(others)
    whole = jnp.concatenate(
        [jnp.where(core == 0, mine, theirs), jnp.where(core == 0, theirs, mine)]
    )
    rank = whole.shape[0] // 3
    return whole[:rank], whole[rank : 2 * rank], whole[2 * rank :]


def forward_chain(sections, width, here, core, own_b, sent_b, keeps, others):
    rank = own_b.shape[1] // 4
    last = sections - 1
    sent = lambda s: sent_b[0 if sections == 2 else s][...].astype(F32)
    based = lambda s, at: jnp.where(
        here == s, own_b[:, at : at + rank], sent(s)[:, at : at + rank]
    )
    base_s = jnp.concatenate(
        [based(0, rank), based(0, 2 * rank) + based(last, 2 * rank)], axis=1
    )
    square = jnp.sum(own_b[:, 3 * rank :], axis=1, keepdims=True)
    smalls = [small_parts(sections, here, core, keeps, others, s) for s in range(sections)]
    gram = jnp.concatenate([smalls[0][2], smalls[last][2]])
    state = []
    code = None
    for s in range(sections):
        m_s, q_t, _ = smalls[s]
        inner, total, resid_s, moved = based(s, 0), square, base_s, None
        if s:
            moved = exact(code, gram)
            total = square + jnp.sum(
                (2.0 * base_s + moved) * code.astype(F32), axis=1, keepdims=True
            )
            inner = inner + exact(code, q_t, COLUMNS)
            resid_s = base_s + moved
        inverse = lax.rsqrt(jnp.maximum(total, 0.0) * (1.0 / width) + 1e-05)
        inner = inner * inverse
        logistic = 1.0 / (1.0 + jnp.exp(-inner))
        active = inner * logistic
        before = code
        state.append((m_s, q_t, inner, logistic, inverse, active, resid_s, before))
        if s == last:
            yield state, gram, before, moved
            code = (moved + exact(active, m_s)).astype(BF16)
            yield code
            return
        grown = exact(active, m_s)
        code = (grown if s == 0 else moved + grown).astype(BF16)


def forward_kernel(sections, width, scalars, own_b, *refs):
    here, core = scalars[0], scalars[1]
    n = 1 if sections == 2 else sections
    sent_b, refs = refs[:n], refs[n:]
    keeps, refs = refs[: n + 1], refs[n + 1 :]
    others, refs = refs[: n + 1], refs[n + 1 :]
    tokens_ref, outs = refs[0], refs[1:]
    state = next(forward_chain(sections, width, here, core, own_b, sent_b, keeps, others))[0]
    outer_into(scalars, 2, state[-1][5].T.astype(BF16), tokens_ref, outs)


def backward_kernel(sections, width, scalars, own_b, own_c, *refs):
    here, core = scalars[0], scalars[1]
    n = 1 if sections == 2 else sections
    sent_b, refs = refs[:n], refs[n:]
    sent_c, refs = refs[:n], refs[n:]
    keeps, refs = refs[: n + 1], refs[n + 1 :]
    others, refs = refs[: n + 1], refs[n + 1 :]
    tokens_ref, codes_ref, refs = refs[0], refs[1], refs[2:]
    thin_count = 1 if sections == 2 else 2
    thin_refs, outs = refs[:thin_count], refs[thin_count:]
    rank = own_c.shape[1] // 2
    last = sections - 1
    chain = forward_chain(sections, width, here, core, own_b, sent_b, keeps, others)
    state, gram, _, _ = next(chain)
    final_code = next(chain)
    sent = lambda s: sent_c[0 if sections == 2 else s][...].astype(F32)
    cot = lambda s, at: jnp.where(
        here == s, own_c[:, at : at + rank], sent(s)[:, at : at + rank]
    )
    grad_active = cot(last, 0)
    grad_y = jnp.concatenate([cot(0, 0), cot(0, rank) + cot(last, rank)], axis=1)
    mine = None
    mine_code = final_code
    thin_in = thin_out = None
    choose = lambda s, value, other: value if other is None else jnp.where(here == s, value, other)
    for s in range(last, -1, -1):
        m_s, q_t, inner, logistic, inverse, active, resid_s, before = state[s]
        if s < last:
            grad_active = exact(back, m_s, COLUMNS)
            grad_y = exact(back, gram) if s else None
            thin_out = choose(s, mm(active.T.astype(BF16), back), thin_out)
        grad_inner = grad_active * logistic * (1.0 + inner * (1.0 - logistic))
        scaled = inverse * grad_inner
        scaled_t = scaled.T.astype(BF16)
        scaled = scaled.astype(BF16)
        mine = choose(s, scaled_t, mine)
        if s:
            mine_code = jnp.where(here == s - 1, before, mine_code)
            thin_in = choose(s, mm(scaled_t, before), thin_in)
            along = jnp.sum(inner * grad_inner, axis=1, keepdims=True)
            along = along * (inverse * inverse * (1.0 / width))
            back = (grad_y + exact(scaled, q_t) - resid_s * along).astype(BF16)
    codes_ref[...] = mine_code
    if sections == 2:
        thin_refs[0][...] = jnp.where(here == last, thin_in, thin_out)
    else:
        thin_refs[0][...] = jnp.where(here == 0, 0.0, thin_in)
        thin_refs[1][...] = thin_out
    outer_into(scalars, 2, mine, tokens_ref, outs)


def end_kernel(sections, scalars, space_ref, gain_ref, *refs):
    is_last = scalars[0] == 1
    part = space_ref.shape[0]
    grad_in, grad_out = refs[-2:]
    refs = list(refs[:-2])
    pair = lambda: refs.pop(0)[...].astype(F32) + refs.pop(0)[...].astype(F32)
    thin_in = pair()
    thin_out = thin_in if sections == 2 else pair()
    space = space_ref[...]
    lift_in = exact(thin_in, space, COLUMNS)
    lift_out = lift_in if sections == 2 else exact(thin_out, space, COLUMNS)
    if sections == 2:
        lift_in = jnp.where(is_last, lift_in, 0.0)
        half_first, half_second = refs.pop(0)[...], refs.pop(0)[...]
        sum_out = jnp.concatenate([half_first, half_second], axis=1)
    else:
        sum_out = refs.pop(0)[...]
    sum_in = jnp.concatenate([pair(), pair()], axis=1)
    start = pl.multiple_of(scalars[1] * part, part)
    total = gain_ref[:, pl.ds(start, part)] * (sum_in + lift_in)
    grad_in[...] = total.T
    grad_out[...] = jnp.where(is_last, sum_out, lift_out).T


def gather_shards(own):
    peers = lax.axis_size("dp")
    order = sorted(range(4, peers, 4), key=lambda m: (m.bit_count(), m))
    held = {0: own}
    for m in order:
        if m.bit_count() == 1:
            held[m] = swap(own, m)
    held[2] = swap(own, 2)
    for k, m in enumerate(order):
        low = m & -m
        before = held[(order[k - 1] if k else 0) ^ 2]
        if m != low:
            held[m] = swap(after(held[m ^ low], held[order[k - 2] ^ 2]), low)
        held[m ^ 2] = swap(after(held[m], before), 2)
    return [0] + order, held


def sum_small(keep, give, far):
    peers = lax.axis_size("dp")
    keep = keep + swap(give, 1)
    bit = 4
    while bit < peers // 2:
        keep = keep + swap(keep, bit)
        bit *= 2
    keep = keep + swap(keep.astype(BF16), 2).astype(F32)
    keep = after(keep, far)
    return keep + swap(keep, peers // 2)


def sum_thin(value, waits):
    peers = lax.axis_size("dp")
    bit, step = 1, 0
    while bit < peers:
        if step:
            value = after(value + got, waits[min(step, len(waits)) - 1])
        got = swap(value, bit)
        bit, step = bit * 2, step + 1
    return value, got


def block_marks():
    near = list(range(0, lax.axis_size("dp"), 4))
    return near + [m ^ 2 for m in near]


def scatter_sum(give, keep):
    half = give.shape[0] // 2
    got = swap(give, 1)
    summed = (keep[half:].astype(F32) + got[half:].astype(F32)).astype(BF16)
    got_x = swap(summed, 2)
    total = keep[:half].astype(F32) + got[:half].astype(F32) + got_x.astype(F32)
    bit = 4
    while True:
        left = total.reshape((total.shape[0] // 2, 2) + total.shape[1:])
        arrived = swap(left[:, 1].astype(BF16), bit)
        if left.shape[0] == 1:
            return (left[0, 0], arrived[0]), got, got_x
        total = left[:, 0] + arrived.astype(F32)
        bit *= 2


def on_device(base, cotangent, gain, weight_in, weight_out, subspace):
    sections = lax.axis_size("section")
    here = lax.axis_index("section")
    spot = lax.axis_index("dp")
    core = spot % 2
    rows, width = base.shape
    part, size = subspace.shape
    rank = weight_in.shape[2]
    last = sections - 1
    flag = (here == last).astype(jnp.int32)
    own_in, own_out = weight_in[0], weight_out[0]
    own = call(own_kernel, [flag], [own_in, own_out, subspace], [((part * 5 // 2, rank), BF16)], 0)[0]
    near, shards = gather_shards(own)

    late_in, late_out, late_space, _ = lax.optimization_barrier(
        (own_in, own_out, subspace, shards[4])
    )
    tall = (3 * rank, size)
    keep, give, _ = call(
        small_kernel,
        [flag, core, spot],
        [late_in, late_out, late_space, gain],
        [((tall[0] // 2, size), F32)] * 2 + [(tall, F32)],
        2 * part * tall[0] * size,
    )
    small = sum_small(keep, give, shards[near[-1]])
    small_other = swap(small, 1)
    keeps = [small, *from_sections(small)]
    others = [small_other, *from_sections(small_other)]

    acc_b = jnp.zeros((rows, 4 * rank), F32)
    acc_c = jnp.zeros((rows, 2 * rank), F32)
    ids = lambda marks: [spot ^ m for m in marks]
    early = near[:-1]
    steps = [(near, [shards[m] for m in near]), ([m ^ 2 for m in early], [shards[m ^ 2] for m in early])]
    for marks, some in steps:
        acc_b, acc_c, stacked = project(
            ids(marks), flag, some, (base, gain, acc_b), (cotangent, acc_c), stack=True
        )
        acc_b, acc_c = project(
            ids([m ^ 1 for m in marks]),
            flag,
            [swap(stacked, 1)],
            (base, gain, acc_b),
            (cotangent, acc_c),
        )
    end = near[-1] ^ 2
    pair = [shards[end], swap(shards[end], 1)]
    acc_b, send_b = project(ids([end, end ^ 1]), flag, pair, base=(base, gain, acc_b), final=True)
    acc_c, send_c = project(ids([end, end ^ 1]), flag, pair, cot=(cotangent, acc_c), final=True)
    sent_b, sent_c = from_sections(send_b), from_sections(send_c)
    sent_b = [after(v, send_c) for v in sent_b]

    every = block_marks()
    half = part // 2
    if sections == 2:
        columns, block_ids = half, lambda who: [(who ^ m) * 2 + flag for m in every]
    else:
        columns, block_ids = part, lambda who: [who ^ m for m in every]
    blocks = lambda n: ((len(every), rank, n), BF16)
    chain_flops = 2 * rows * size * rank * 20 * sections
    block_flops = 2 * rows * width * rank
    chain_bytes = VMEM_BYTES if sections == 2 else 4 * VMEM_BYTES
    give_out, keep_out = call(
        functools.partial(forward_kernel, sections, width),
        [here, core, *block_ids(spot ^ 1), *block_ids(spot)],
        [acc_b, *sent_b, *keeps, *others, cotangent],
        [blocks(columns)] * 2,
        chain_flops + block_flops,
        chain_bytes,
    )
    sum_out, got_out, got_out_x = scatter_sum(give_out, keep_out)
    sum_out = sum_out[0] + sum_out[1].astype(F32)
    ends_out = [sum_out]
    if sections == 2:
        ends_out = [swap(sum_out, 1, "section"), sum_out]

    sent_c = [after(v, got_out) for v in sent_c]
    halves = [
        (who ^ m) * 2 + k for k in range(2) for who in (spot ^ 1, spot) for m in every
    ]
    thin_count = 1 if sections == 2 else 2
    codes, *rest = call(
        functools.partial(backward_kernel, sections, width),
        [here, core, *halves],
        [acc_b, acc_c, *sent_b, *sent_c, *keeps, *others, base],
        [((rows, size), BF16)] + [((rank, size), F32)] * thin_count + [blocks(half)] * 4,
        2 * chain_flops + block_flops,
        chain_bytes,
    )
    thins, halves = rest[:thin_count], rest[thin_count:]
    lower, got_lower, got_lower_x = scatter_sum(*halves[:2])
    upper, got_upper, got_upper_x = scatter_sum(*halves[2:])
    waits = [got_lower, got_out_x, got_lower_x]
    terms = [term for thin in thins for term in sum_thin(thin, waits)]
    grad_in, grad_out = call(
        functools.partial(end_kernel, sections),
        [flag, spot],
        [subspace, gain, *terms, *ends_out, *lower, *upper],
        [((part, rank), F32)] * 2,
        4 * part * size * rank,
    )
    return codes[None], grad_in[None], grad_out[None]


def solution(mesh):
    placed = (
        P("dp", None),
        P("dp", None),
        P("section", None),
        P("section", "dp", None),
        P("section", "dp", None),
        P("dp", None),
    )
    return jax.shard_map(
        on_device,
        mesh=mesh,
        in_specs=placed,
        out_specs=(P("section", "dp", None), P("section", "dp", None), P("section", "dp", None)),
        check_vma=False,
    )
```

```python
import functools

import jax
import jax.numpy as jnp
from jax import lax
from jax.experimental import pallas as pl
from jax.experimental.pallas import tpu as pltpu
from jax.sharding import PartitionSpec as P

F32 = jnp.float32
BF16 = jnp.bfloat16
VMEM_BYTES = 50 * 1024 * 1024
IN_VMEM = pl.BlockSpec(memory_space=pltpu.VMEM)
IN_SMEM = pl.BlockSpec(memory_space=pltpu.SMEM)
IN_HBM = pl.BlockSpec(memory_space=pltpu.HBM)
CONTRACT = ((1,), (0,))
ROWS = ((0,), (0,))
COLUMNS = ((1,), (1,))


def mm(a, b, dims=CONTRACT):
    return lax.dot_general(a, b, (dims, ((), ())), preferred_element_type=F32)


def parts_of(a):
    if a.dtype == BF16:
        return [a]
    high = a.astype(BF16)
    return [high, (a - high.astype(F32)).astype(BF16)]


def exact(a, b, dims=CONTRACT):
    left, right = parts_of(a), parts_of(b)
    total = mm(left[0], right[0], dims)
    for i, x in enumerate(left):
        for j, y in enumerate(right):
            if i + j == 1:
                total = total + mm(x, y, dims)
    return total


def call(kernel, scalars, far, arrays, shapes, scratch=(), vmem_bytes=VMEM_BYTES):
    return pl.pallas_call(
        kernel,
        in_specs=[IN_SMEM] + [IN_HBM] * len(far) + [IN_VMEM] * len(arrays),
        out_specs=[IN_VMEM] * len(shapes),
        out_shape=[jax.ShapeDtypeStruct(*s) for s in shapes],
        scratch_shapes=list(scratch),
        compiler_params=pltpu.CompilerParams(vmem_limit_bytes=vmem_bytes),
        cost_estimate=pl.CostEstimate(flops=0, bytes_accessed=0, transcendentals=0),
    )(jnp.stack(scalars).astype(jnp.int32), *far, *arrays)


def fetch(pairs, sems, first=0):
    copies = [pltpu.make_async_copy(a, b, sems.at[first + i]) for i, (a, b) in enumerate(pairs)]
    for copy in copies:
        copy.start()
    return copies


def swap(value, bits, axis="dp"):
    peers = lax.axis_size(axis)
    return lax.ppermute(value, axis, [(i, i ^ bits) for i in range(peers)])


def after(value, *others):
    return lax.optimization_barrier((value, *others))[0]


def from_sections(value):
    sections = lax.axis_size("section")
    here = lax.axis_index("section")
    if sections == 2:
        return [swap(value, 1, "section")]
    around = [(i, (i + 1) % sections) for i in range(sections)]
    held = [value]
    for _ in range(sections - 1):
        held.append(lax.ppermute(held[-1], "section", around))
    stacked = jnp.stack(held)
    order = (here - jnp.arange(sections)) % sections
    return [lax.dynamic_index_in_dim(stacked, order[s], 0, keepdims=False) for s in range(sections)]


def own_kernel(scalars, in_far, out_ref, space_ref, gain_far, own_ref, in_ref, gain_ref, sems):
    part, rank = in_ref.shape
    half = part // 2
    start = pl.multiple_of(scalars[1] * part, part)
    first = fetch([(in_far, in_ref), (gain_far.at[:, pl.ds(start, part)], gain_ref)], sems)
    places = own_ref.at[part : 2 * part], own_ref.at[2 * part :]

    def copy_both(sources):
        for copy in fetch(list(zip(sources, places)), sems, 2):
            copy.wait()

    @pl.when(scalars[0] == 1)
    def _():
        copy_both((out_ref, space_ref.at[half:, rank:]))

    @pl.when(scalars[0] == 0)
    def _():
        copy_both((space_ref.at[:, :rank], space_ref.at[:half, rank:]))

    for copy in first:
        copy.wait()
    column = jnp.broadcast_to(gain_ref[...], (rank, part)).T
    own_ref[:part] = (in_ref[...].astype(F32) * column).astype(BF16)


def small_kernel(scalars, out_far, space_far, own_ref, keep_ref, give_ref, *scratch):
    out_ref, space_ref, all_ref, sems = scratch
    is_last, core = scalars[0] == 1, scalars[1]
    part, rank = out_ref.shape
    for copy in fetch([(space_far, space_ref), (out_far, out_ref)], sems):
        copy.wait()
    space = space_ref[...]
    all_ref[:rank] = mm(out_ref[...], space, ROWS)
    all_ref[rank : 2 * rank] = mm(own_ref[:part], space, ROWS)
    columns = jnp.where(is_last, space_ref[:, rank:], space_ref[:, :rank])
    all_ref[2 * rank :] = mm(columns, space, ROWS)
    half = keep_ref.shape[0]
    first, second = all_ref[:half], all_ref[half:]
    keep_ref[...] = jnp.where(core == 0, first, second)
    give_ref[...] = jnp.where(core == 0, second, first)


def project_kernel(stacked, final, count, scalars, base_far, cot_far, *refs):
    refs = list(refs)
    base_ref, cot_ref, sems = refs[-3:]
    shards, refs = [], refs[:-3]
    while len(shards) < count:
        ref = refs.pop(0)
        shards += [ref] if len(ref.shape) == 2 else [ref.at[i] for i in range(ref.shape[0])]
    acc, out = refs.pop(0), refs.pop(0)
    rank = out.shape[1] // 6
    part = base_ref.shape[2]
    half = part // 2
    starts = [pl.multiple_of(scalars[t] * part, part) for t in range(count)]
    block = lambda ref, t: ref.at[:, pl.ds(starts[t], part)]
    copies = []
    for t in range(count):
        pairs = [(block(base_far, t), base_ref.at[t]), (block(cot_far, t), cot_ref.at[t])]
        copies.append(fetch(pairs, sems, 2 * t))
    skip = pl.multiple_of(scalars[count] * half, half)
    out[...] = acc[...]
    for t, shard in enumerate(shards):
        if stacked:
            refs[0][t] = shard[...]
        copies[t][0].wait()
        tokens = base_ref[t]
        tokens_f = tokens.astype(F32)
        square = tokens_f * tokens_f
        total = square[:, :rank]
        for at in range(rank, part, rank):
            total = total + square[:, at : at + rank]
        wide = jnp.concatenate([shard[:part], shard[part : 2 * part]], axis=1)
        out[:, : 2 * rank] += mm(tokens, wide)
        out[:, 2 * rank : 3 * rank] += mm(base_ref[t, :, pl.ds(skip, half)], shard[2 * part :])
        out[:, 5 * rank :] += total
        copies[t][1].wait()
        out[:, 3 * rank : 4 * rank] += mm(cot_ref[t], shard[part : 2 * part])
        out[:, 4 * rank : 5 * rank] += mm(cot_ref[t, :, pl.ds(skip, half)], shard[2 * part :])
    if final:
        refs[0][...] = out[:, : 5 * rank].astype(BF16)


def project(ids, flag, shards, tokens, acc, stacked=False, final=False):
    base, cotangent = tokens
    tall, rank = shards[0].shape[-2:]
    rows, part, count = base.shape[0], tall * 2 // 5, len(ids)
    shapes = [(acc.shape, F32)]
    if stacked:
        shapes.append(((count, tall, rank), BF16))
    if final:
        shapes.append(((rows, 5 * rank), BF16))
    blocks = pltpu.VMEM((count, rows, part), BF16)
    return call(
        functools.partial(project_kernel, stacked, final, count),
        [*ids, flag],
        [base, cotangent],
        [*shards, acc],
        shapes,
        [blocks, blocks, pltpu.SemaphoreType.DMA((2 * count,))],
    )


def outer_into(small, copies, blocks_ref, outs):
    at = 0
    for out in outs:
        for j in range(out.shape[0]):
            copies[at].wait()
            out[j] = mm(small, blocks_ref[at]).astype(BF16)
            at += 1


def small_parts(sections, here, core, keeps, others, s):
    value = lambda refs: (
        jnp.where(here == s, refs[0][...], refs[1][...].astype(F32))
        if sections == 2
        else refs[1 + s][...].astype(F32)
    )
    mine, theirs = value(keeps), value(others)
    whole = jnp.concatenate(
        [jnp.where(core == 0, mine, theirs), jnp.where(core == 0, theirs, mine)]
    )
    rank = whole.shape[0] // 3
    return whole[:rank], whole[rank : 2 * rank], whole[2 * rank :]


def chain_kernel(sections, width, scalars, base_far, cot_far, own, *refs):
    here, core = scalars[0], scalars[1]
    n = 1 if sections == 2 else sections
    thin_count = 1 if sections == 2 else 2
    refs = list(refs)
    take = lambda count: [refs.pop(0) for _ in range(count)]
    sent, keeps, others = take(n), take(n + 1), take(n + 1)
    codes_ref, thin_refs = take(1)[0], take(thin_count)
    outs_c, outs_b = take(2), take(4)
    cot_ref, base_ref, sems = refs
    at, copies = 2, []
    for far, blocks_ref in ((cot_far, cot_ref), (base_far, base_ref)):
        count, _, columns = blocks_ref.shape
        pairs = []
        for j in range(count):
            start = pl.multiple_of(scalars[at + j] * columns, columns)
            pairs.append((far.at[:, pl.ds(start, columns)], blocks_ref.at[j]))
        copies.append(fetch(pairs, sems, at - 2))
        at += count

    rank = own.shape[1] // 6
    last = sections - 1
    values = [
        jnp.where(
            here == s, own[:, : 5 * rank], sent[0 if sections == 2 else s][...].astype(F32)
        )
        for s in range(sections)
    ]
    column = lambda s, k: values[s][:, k * rank : (k + 1) * rank]
    spread = lambda k: jnp.concatenate(
        [column(0, k), column(0, k + 1) + column(last, k + 1)], axis=1
    )
    base_s = spread(1)
    square = jnp.sum(own[:, 5 * rank :], axis=1, keepdims=True)
    smalls = [small_parts(sections, here, core, keeps, others, s) for s in range(sections)]
    gram = jnp.concatenate([smalls[0][2], smalls[last][2]])
    choose = lambda s, value, other: value if other is None else jnp.where(here == s, value, other)
    state = []
    code = mine_code = None
    for s in range(sections):
        m_s, q_t, _ = smalls[s]
        inner, total, resid_s, before = column(s, 0), square, base_s, code
        if s:
            moved = exact(code, gram)
            total = square + jnp.sum(
                (2.0 * base_s + moved) * code.astype(F32), axis=1, keepdims=True
            )
            inner = inner + exact(code, q_t, COLUMNS)
            resid_s = base_s + moved
        inverse = lax.rsqrt(jnp.maximum(total, 0.0) * (1.0 / width) + 1e-05)
        inner = inner * inverse
        logistic = 1.0 / (1.0 + jnp.exp(-inner))
        active = inner * logistic
        grown = exact(active, m_s)
        code = (moved + grown if s else grown).astype(BF16)
        mine_code = choose(s, code, mine_code)
        state.append((m_s, q_t, inner, logistic, inverse, active, resid_s, before))
    codes_ref[...] = mine_code
    active_t = state[last][5].T.astype(BF16)
    outer_into(active_t, copies[0], cot_ref, outs_c)

    grad_active, grad_y = column(last, 3), spread(3)
    mine = thin_in = thin_out = None
    for s in range(last, -1, -1):
        m_s, q_t, inner, logistic, inverse, active, resid_s, before = state[s]
        if s < last:
            grad_active = exact(back, m_s, COLUMNS)
            grad_y = exact(back, gram) if s else None
            thin_out = choose(s, mm(active.T.astype(BF16), back), thin_out)
        grad_inner = grad_active * logistic * (1.0 + inner * (1.0 - logistic))
        scaled = inverse * grad_inner
        scaled_t = scaled.T.astype(BF16)
        scaled = scaled.astype(BF16)
        mine = choose(s, scaled_t, mine)
        if s:
            thin_in = choose(s, mm(scaled_t, before), thin_in)
            along = jnp.sum(inner * grad_inner, axis=1, keepdims=True)
            along = along * (inverse * inverse * (1.0 / width))
            back = (grad_y + exact(scaled, q_t) - resid_s * along).astype(BF16)
    if sections == 2:
        thin_refs[0][...] = jnp.where(here == last, thin_in, thin_out)
    else:
        thin_refs[0][...] = jnp.where(here == 0, 0.0, thin_in)
        thin_refs[1][...] = thin_out
    outer_into(mine, copies[1], base_ref, outs_b)


def end_kernel(sections, scalars, gain_ref, space_ref, *refs):
    is_last = scalars[0] == 1
    part = space_ref.shape[0]
    grad_in, grad_out = refs[-2:]
    refs = list(refs[:-2])
    pair = lambda: refs.pop(0)[...].astype(F32) + refs.pop(0)[...].astype(F32)
    thin_in = pair()
    thin_out = thin_in if sections == 2 else pair()
    space = space_ref[...]
    lift_in = exact(thin_in, space, COLUMNS)
    lift_out = lift_in if sections == 2 else exact(thin_out, space, COLUMNS)
    if sections == 2:
        lift_in = jnp.where(is_last, lift_in, 0.0)
        half_first, half_second = refs.pop(0)[...], refs.pop(0)[...]
        sum_out = jnp.concatenate([half_first, half_second], axis=1)
    else:
        sum_out = refs.pop(0)[...]
    sum_in = jnp.concatenate([pair(), pair()], axis=1)
    start = pl.multiple_of(scalars[1] * part, part)
    total = gain_ref[:, pl.ds(start, part)] * (sum_in + lift_in)
    grad_in[...] = total.T
    grad_out[...] = jnp.where(is_last, sum_out, lift_out).T


def sum_thin(value, waits):
    peers = lax.axis_size("dp")
    bit, step = 1, 0
    while bit < peers:
        if step:
            value = after(value + got, waits[min(step, len(waits)) - 1])
        got = swap(value, bit)
        bit, step = bit * 2, step + 1
    return value, got


def scatter_sum(got, keep, waits=()):
    half = got.shape[0] // 2
    summed = (keep[half:].astype(F32) + got[half:].astype(F32)).astype(BF16)
    got_x = swap(summed, 2)
    total = keep[:half].astype(F32) + got[:half].astype(F32) + got_x.astype(F32)
    bit = 4
    while True:
        left = total.reshape((total.shape[0] // 2, 2) + total.shape[1:])
        give = left[:, 1].astype(BF16)
        if waits:
            give = after(give, *waits[0])
            waits = waits[1:]
        arrived = swap(give, bit)
        if left.shape[0] == 1:
            return (left[0, 0], arrived[0]), got_x
        total = left[:, 0] + arrived.astype(F32)
        bit *= 2


def on_device(base, cotangent, gain, weight_in, weight_out, subspace):
    sections = lax.axis_size("section")
    here = lax.axis_index("section")
    spot = lax.axis_index("dp")
    core = spot % 2
    rows, width = base.shape
    part, size = subspace.shape
    rank = weight_in.shape[2]
    last = sections - 1
    flag = (here == last).astype(jnp.int32)
    own_in, own_out = weight_in[0], weight_out[0]
    own = call(
        own_kernel,
        [flag, spot],
        [own_in, own_out, subspace, gain],
        [],
        [((part * 5 // 2, rank), BF16)],
        [pltpu.VMEM((part, rank), BF16), pltpu.VMEM((1, part), F32), pltpu.SemaphoreType.DMA((4,))],
        62 * 1024 * 1024,
    )[0]

    peers = lax.axis_size("dp")
    order = sorted(range(4, peers, 4), key=lambda m: (m.bit_count(), m))
    shards = {0: own}
    for m in order:
        if m.bit_count() == 1:
            shards[m] = swap(own, m)
    shards[2] = swap(own, 2)

    tall = (3 * rank, size)
    keep, give = call(
        small_kernel,
        [flag, core],
        [own_out, subspace],
        [after(own, shards[peers // 2])],
        [((tall[0] // 2, size), F32)] * 2,
        [
            pltpu.VMEM((part, rank), BF16),
            pltpu.VMEM((part, size), BF16),
            pltpu.VMEM(tall, F32),
            pltpu.SemaphoreType.DMA((2,)),
        ],
        60 * 1024 * 1024,
    )
    small = keep + swap(give, 1)
    bit = 4
    while bit < peers // 2:
        small = small + swap(small, bit)
        bit *= 2

    tokens = (base, cotangent)
    acc = jnp.zeros((rows, 6 * rank), F32)

    def both_cores(marks, acc):
        ids = [spot ^ m for m in marks]
        acc, stacked = project(ids, flag, [shards[m] for m in marks], tokens, acc, stacked=True)
        ids = [spot ^ m ^ 1 for m in marks]
        return acc, lambda acc: project(ids, flag, [swap(stacked, 1)], tokens, acc)[0]

    ends = order[-1] ^ 2
    first_marks = [0, order[0], 2]
    for k, m in enumerate(order):
        low = m & -m
        if m != low:
            shards[m] = swap(after(shards[m ^ low], shards[order[k - 2] ^ 2]), low)
        before = shards[order[k - 1] ^ 2] if k else shards[2]
        shards[m ^ 2] = swap(after(shards[m], before, *([small] if m ^ 2 == ends else [])), 2)
    near_sum = small
    small = after(small, shards[peers // 2])
    small = small + swap(small, peers // 2)
    small = small + swap(small.astype(BF16), 2).astype(F32)
    small_other = swap(small, 1)
    keeps = [small, *from_sections(small.astype(BF16))]
    others = [small_other, *from_sections(small_other.astype(BF16))]

    acc = after(acc, shards[order[-1]], shards[order[-2] ^ 2], near_sum)
    acc, other_core = both_cores(first_marks, acc)
    acc = other_core(acc)
    rest_marks = [m for m in order + [m ^ 2 for m in order] if m not in (*first_marks, ends)]
    acc, other_core = both_cores(rest_marks, acc)
    acc = other_core(acc)
    acc, send = project(
        [spot ^ ends, spot ^ ends ^ 1],
        flag,
        [shards[ends], swap(shards[ends], 1)],
        tokens,
        acc,
        final=True,
    )
    sent = from_sections(send)

    near = list(range(0, peers, 4))
    every = near + [m ^ 2 for m in near]
    half = part // 2
    if sections == 2:
        columns, block_id = half, lambda i: i * 2 + flag
    else:
        columns, block_id = part, lambda i: i
    both = (spot ^ 1, spot)
    out_ids = [block_id(who ^ m) for who in both for m in every]
    in_ids = [(who ^ m) * 2 + k for k in range(2) for who in both for m in every]
    blocks = lambda n: ((len(every), rank, n), BF16)
    thin_count = 1 if sections == 2 else 2
    codes, *rest = call(
        functools.partial(chain_kernel, sections, width),
        [here, core, *out_ids, *in_ids],
        [base, cotangent],
        [acc, *sent, *keeps, *others],
        [((rows, size), BF16)]
        + [((rank, size), F32)] * thin_count
        + [blocks(columns)] * 2
        + [blocks(half)] * 4,
        [
            pltpu.VMEM((len(out_ids), rows, columns), BF16),
            pltpu.VMEM((len(in_ids), rows, half), BF16),
            pltpu.SemaphoreType.DMA((len(out_ids) + len(in_ids),)),
        ],
        (50 if sections == 2 else 58) * 1024 * 1024,
    )
    thins, chunks = rest[:thin_count], rest[thin_count:]
    got = [swap(give, 1) for give in chunks[::2]]
    lower, lower_x = scatter_sum(got[1], chunks[3])
    upper, upper_x = scatter_sum(got[2], chunks[5])
    sum_out, _ = scatter_sum(got[0], chunks[1], [got[1:], [lower_x], [upper_x]])
    sum_out = sum_out[0] + sum_out[1].astype(F32)
    ends_out = [sum_out]
    if sections == 2:
        ends_out = [swap(sum_out, 1, "section"), sum_out]
    waits = [got[2], lower_x, upper_x]
    terms = [term for thin in thins for term in sum_thin(thin, waits)]
    grad_in, grad_out = call(
        functools.partial(end_kernel, sections),
        [flag, spot],
        [],
        [gain, subspace, *terms, *ends_out, *lower, *upper],
        [((part, rank), F32)] * 2,
    )
    return codes[None], grad_in[None], grad_out[None]


def solution(mesh):
    placed = (
        P("dp", None),
        P("dp", None),
        P("section", None),
        P("section", "dp", None),
        P("section", "dp", None),
        P("dp", None),
    )
    return jax.shard_map(
        on_device,
        mesh=mesh,
        in_specs=placed,
        out_specs=(P("section", "dp", None), P("section", "dp", None), P("section", "dp", None)),
        check_vma=False,
    )
```

```python
import functools

import jax
import jax.numpy as jnp
from jax import lax
from jax.experimental import pallas as pl
from jax.experimental.pallas import tpu as pltpu
from jax.sharding import PartitionSpec as P

F32 = jnp.float32
BF16 = jnp.bfloat16
VMEM_BYTES = 16 * 1024 * 1024
IN_VMEM = pl.BlockSpec(memory_space=pltpu.VMEM)
IN_SMEM = pl.BlockSpec(memory_space=pltpu.SMEM)
IN_HBM = pl.BlockSpec(memory_space=pltpu.HBM)
CONTRACT = ((1,), (0,))
ROWS = ((0,), (0,))
COLUMNS = ((1,), (1,))


def mm(a, b, dims=CONTRACT):
    return lax.dot_general(a, b, (dims, ((), ())), preferred_element_type=F32)


def parts_of(a):
    if a.dtype == BF16:
        return [a]
    high = a.astype(BF16)
    return [high, (a - high.astype(F32)).astype(BF16)]


def exact(a, b, dims=CONTRACT):
    left, right = parts_of(a), parts_of(b)
    total = mm(left[0], right[0], dims)
    for i, x in enumerate(left):
        for j, y in enumerate(right):
            if i + j == 1:
                total = total + mm(x, y, dims)
    return total


def call(kernel, scalars, far, arrays, shapes, scratch=(), vmem_bytes=VMEM_BYTES, flops=0):
    return pl.pallas_call(
        kernel,
        in_specs=[IN_SMEM] + [IN_HBM] * len(far) + [IN_VMEM] * len(arrays),
        out_specs=[IN_VMEM] * len(shapes),
        out_shape=[jax.ShapeDtypeStruct(*s) for s in shapes],
        scratch_shapes=list(scratch),
        compiler_params=pltpu.CompilerParams(vmem_limit_bytes=vmem_bytes),
        cost_estimate=pl.CostEstimate(flops=flops, bytes_accessed=0, transcendentals=0),
    )(jnp.stack(scalars).astype(jnp.int32), *far, *arrays)


def fetch(pairs, sems, first=0):
    copies = [pltpu.make_async_copy(a, b, sems.at[first + i]) for i, (a, b) in enumerate(pairs)]
    for copy in copies:
        copy.start()
    return copies


def swap(value, bits, axis="dp"):
    peers = lax.axis_size(axis)
    return lax.ppermute(value, axis, [(i, i ^ bits) for i in range(peers)])


def after(value, *others):
    return lax.optimization_barrier((value, *others))[0]


def from_sections(value):
    sections = lax.axis_size("section")
    here = lax.axis_index("section")
    if sections == 2:
        return [swap(value, 1, "section")]
    around = [(i, (i + 1) % sections) for i in range(sections)]
    held = [value]
    for _ in range(sections - 1):
        held.append(lax.ppermute(held[-1], "section", around))
    stacked = jnp.stack(held)
    order = (here - jnp.arange(sections)) % sections
    return [lax.dynamic_index_in_dim(stacked, order[s], 0, keepdims=False) for s in range(sections)]


def own_kernel(scalars, in_far, out_ref, space_ref, gain_far, own_ref, in_ref, gain_ref, sems):
    part, rank = in_ref.shape
    half = part // 2
    start = pl.multiple_of(scalars[1] * part, part)
    first = fetch([(in_far, in_ref), (gain_far.at[:, pl.ds(start, part)], gain_ref)], sems)
    places = own_ref.at[part : 2 * part], own_ref.at[2 * part :]

    def copy_both(sources):
        for copy in fetch(list(zip(sources, places)), sems, 2):
            copy.wait()

    @pl.when(scalars[0] == 1)
    def _():
        copy_both((out_ref, space_ref.at[half:, rank:]))

    @pl.when(scalars[0] == 0)
    def _():
        copy_both((space_ref.at[:, :rank], space_ref.at[:half, rank:]))

    for copy in first:
        copy.wait()
    column = jnp.broadcast_to(gain_ref[...], (rank, part)).T
    own_ref[:part] = (in_ref[...].astype(F32) * column).astype(BF16)


def small_kernel(scalars, out_far, space_far, own_ref, keep_ref, give_ref, *scratch):
    out_ref, space_ref, all_ref, sems = scratch
    is_last, core = scalars[0] == 1, scalars[1]
    part, rank = out_ref.shape
    for copy in fetch([(space_far, space_ref), (out_far, out_ref)], sems):
        copy.wait()
    space = space_ref[...]
    all_ref[:rank] = mm(out_ref[...], space, ROWS)
    all_ref[rank : 2 * rank] = mm(own_ref[:part], space, ROWS)
    columns = jnp.where(is_last, space_ref[:, rank:], space_ref[:, :rank])
    all_ref[2 * rank :] = mm(columns, space, ROWS)
    half = keep_ref.shape[0]
    first, second = all_ref[:half], all_ref[half:]
    keep_ref[...] = jnp.where(core == 0, first, second)
    give_ref[...] = jnp.where(core == 0, second, first)


def project_kernel(first, final, count, scalars, base_ref, cot_ref, *refs):
    shards, refs = refs[:count], list(refs[count:])
    acc = None if first else refs.pop(0)
    out = refs.pop(0)
    rank = out.shape[1] // 6
    part = shards[0].shape[0] * 2 // 5
    half = part // 2
    skip = scalars[count] * half
    out[...] = jnp.zeros_like(out) if first else acc[...]
    for t, shard in enumerate(shards):
        start = pl.multiple_of(scalars[t] * part, part)
        half_start = pl.multiple_of(start + skip, half)
        tokens = base_ref[:, pl.ds(start, part)]
        tokens_f = tokens.astype(F32)
        square = tokens_f * tokens_f
        total = square[:, :rank]
        for at in range(rank, part, rank):
            total = total + square[:, at : at + rank]
        wide = jnp.concatenate([shard[:part], shard[part : 2 * part]], axis=1)
        out[:, : 2 * rank] += mm(tokens, wide)
        out[:, 2 * rank : 3 * rank] += mm(base_ref[:, pl.ds(half_start, half)], shard[2 * part :])
        out[:, 3 * rank : 4 * rank] += mm(cot_ref[:, pl.ds(start, part)], shard[part : 2 * part])
        out[:, 4 * rank : 5 * rank] += mm(cot_ref[:, pl.ds(half_start, half)], shard[2 * part :])
        out[:, 5 * rank :] += total
    if final:
        refs[0][...] = out[:, : 5 * rank].astype(BF16)


def project(ids, flag, shards, tokens, acc=None, final=False):
    tall, rank = shards[0].shape
    rows, count = tokens[0].shape[0], len(ids)
    shapes = [((rows, 6 * rank), F32)]
    if final:
        shapes.append(((rows, 5 * rank), BF16))
    return call(
        functools.partial(project_kernel, acc is None, final, count),
        [*ids, flag],
        [],
        [*tokens, *shards] + ([] if acc is None else [acc]),
        shapes,
        flops=4 * rows * tall * rank * count,
    )


def outer_into(scalars, at, small, tokens_ref, outs):
    for out in outs:
        count, _, columns = out.shape
        for j in range(count):
            start = pl.multiple_of(scalars[at] * columns, columns)
            out[j] = mm(small, tokens_ref[:, pl.ds(start, columns)]).astype(BF16)
            at += 1


def small_parts(sections, here, core, keeps, others, s):
    value = lambda refs: (
        jnp.where(here == s, refs[0][...], refs[1][...].astype(F32))
        if sections == 2
        else refs[1 + s][...].astype(F32)
    )
    mine, theirs = value(keeps), value(others)
    whole = jnp.concatenate(
        [jnp.where(core == 0, mine, theirs), jnp.where(core == 0, theirs, mine)]
    )
    rank = whole.shape[0] // 3
    return whole[:rank], whole[rank : 2 * rank], whole[2 * rank :]


def chain_kernel(sections, width, scalars, base_ref, cot_ref, own, *refs):
    here, core = scalars[0], scalars[1]
    n = 1 if sections == 2 else sections
    thin_count = 1 if sections == 2 else 2
    refs = list(refs)
    take = lambda count: [refs.pop(0) for _ in range(count)]
    sent, keeps, others = take(n), take(n + 1), take(n + 1)
    codes_ref, thin_refs = take(1)[0], take(thin_count)
    outs_c, outs_b = take(2), take(4)
    rank = own.shape[1] // 6
    last = sections - 1
    values = [
        jnp.where(
            here == s, own[:, : 5 * rank], sent[0 if sections == 2 else s][...].astype(F32)
        )
        for s in range(sections)
    ]
    column = lambda s, k: values[s][:, k * rank : (k + 1) * rank]
    spread = lambda k: jnp.concatenate(
        [column(0, k), column(0, k + 1) + column(last, k + 1)], axis=1
    )
    base_s = spread(1)
    square = jnp.sum(own[:, 5 * rank :], axis=1, keepdims=True)
    smalls = [small_parts(sections, here, core, keeps, others, s) for s in range(sections)]
    gram = jnp.concatenate([smalls[0][2], smalls[last][2]])
    choose = lambda s, value, other: value if other is None else jnp.where(here == s, value, other)
    state = []
    code = mine_code = None
    for s in range(sections):
        m_s, q_t, _ = smalls[s]
        inner, total, resid_s, before = column(s, 0), square, base_s, code
        if s:
            moved = exact(code, gram)
            total = square + jnp.sum(
                (2.0 * base_s + moved) * code.astype(F32), axis=1, keepdims=True
            )
            inner = inner + exact(code, q_t, COLUMNS)
            resid_s = base_s + moved
        inverse = lax.rsqrt(jnp.maximum(total, 0.0) * (1.0 / width) + 1e-05)
        inner = inner * inverse
        logistic = 1.0 / (1.0 + jnp.exp(-inner))
        active = inner * logistic
        grown = exact(active, m_s)
        code = (moved + grown if s else grown).astype(BF16)
        mine_code = choose(s, code, mine_code)
        state.append((m_s, q_t, inner, logistic, inverse, active, resid_s, before))
    codes_ref[...] = mine_code
    active_t = state[last][5].T.astype(BF16)
    outer_into(scalars, 2, active_t, cot_ref, outs_c)

    grad_active, grad_y = column(last, 3), spread(3)
    mine = thin_in = thin_out = None
    for s in range(last, -1, -1):
        m_s, q_t, inner, logistic, inverse, active, resid_s, before = state[s]
        if s < last:
            grad_active = exact(back, m_s, COLUMNS)
            grad_y = exact(back, gram) if s else None
            thin_out = choose(s, mm(active.T.astype(BF16), back), thin_out)
        grad_inner = grad_active * logistic * (1.0 + inner * (1.0 - logistic))
        scaled = inverse * grad_inner
        scaled_t = scaled.T.astype(BF16)
        scaled = scaled.astype(BF16)
        mine = choose(s, scaled_t, mine)
        if s:
            thin_in = choose(s, mm(scaled_t, before), thin_in)
            along = jnp.sum(inner * grad_inner, axis=1, keepdims=True)
            along = along * (inverse * inverse * (1.0 / width))
            back = (grad_y + exact(scaled, q_t) - resid_s * along).astype(BF16)
    if sections == 2:
        thin_refs[0][...] = jnp.where(here == last, thin_in, thin_out)
    else:
        thin_refs[0][...] = jnp.where(here == 0, 0.0, thin_in)
        thin_refs[1][...] = thin_out
    outer_into(scalars, 2 + 2 * outs_c[0].shape[0], mine, base_ref, outs_b)


def end_kernel(sections, scalars, gain_ref, space_ref, *refs):
    is_last = scalars[0] == 1
    part = space_ref.shape[0]
    grad_in, grad_out = refs[-2:]
    refs = list(refs[:-2])
    pair = lambda: refs.pop(0)[...].astype(F32) + refs.pop(0)[...].astype(F32)
    thin_in = pair()
    thin_out = thin_in if sections == 2 else pair()
    space = space_ref[...]
    lift_in = exact(thin_in, space, COLUMNS)
    lift_out = lift_in if sections == 2 else exact(thin_out, space, COLUMNS)
    if sections == 2:
        lift_in = jnp.where(is_last, lift_in, 0.0)
        half_first, half_second = refs.pop(0)[...], refs.pop(0)[...]
        sum_out = jnp.concatenate([half_first, half_second], axis=1)
    else:
        sum_out = refs.pop(0)[...]
    sum_in = jnp.concatenate([pair(), pair()], axis=1)
    start = pl.multiple_of(scalars[1] * part, part)
    total = gain_ref[:, pl.ds(start, part)] * (sum_in + lift_in)
    grad_in[...] = total.T
    grad_out[...] = jnp.where(is_last, sum_out, lift_out).T


def sum_thin(value, waits):
    peers = lax.axis_size("dp")
    bit, step = 1, 0
    while bit < peers:
        if step:
            wait = waits[min(step, len(waits)) - 1]
            value = value + got if wait is None else after(value + got, wait)
        got = swap(value, bit)
        bit, step = bit * 2, step + 1
    return value, got


def scatter_sum(got, keep, waits=()):
    half = got.shape[0] // 2
    summed = (keep[half:].astype(F32) + got[half:].astype(F32)).astype(BF16)
    got_x = swap(summed, 2)
    total = keep[:half].astype(F32) + got[:half].astype(F32) + got_x.astype(F32)
    bit = 4
    while True:
        left = total.reshape((total.shape[0] // 2, 2) + total.shape[1:])
        give = left[:, 1].astype(BF16)
        if waits:
            give = after(give, *waits[0])
            waits = waits[1:]
        arrived = swap(give, bit)
        if left.shape[0] == 1:
            return (left[0, 0], arrived[0]), got_x
        total = left[:, 0] + arrived.astype(F32)
        bit *= 2


def on_device(base, cotangent, gain, weight_in, weight_out, subspace):
    sections = lax.axis_size("section")
    here = lax.axis_index("section")
    spot = lax.axis_index("dp")
    core = spot % 2
    rows, width = base.shape
    part, size = subspace.shape
    rank = weight_in.shape[2]
    last = sections - 1
    flag = (here == last).astype(jnp.int32)
    own_in, own_out = weight_in[0], weight_out[0]
    own = call(
        own_kernel,
        [flag, spot],
        [own_in, own_out, subspace, gain],
        [],
        [((part * 5 // 2, rank), BF16)],
        [pltpu.VMEM((part, rank), BF16), pltpu.VMEM((1, part), F32), pltpu.SemaphoreType.DMA((4,))],
        62 * 1024 * 1024,
    )[0]

    peers = lax.axis_size("dp")
    order = sorted(range(4, peers, 4), key=lambda m: (m.bit_count(), m))
    shards = {0: own}
    for m in order:
        if m.bit_count() == 1:
            shards[m] = swap(own, m)
    shards[2] = swap(own, 2)

    tall = (3 * rank, size)
    keep, give = call(
        small_kernel,
        [flag, core],
        [own_out, subspace],
        [after(own, shards[peers // 2])],
        [((tall[0] // 2, size), F32)] * 2,
        [
            pltpu.VMEM((part, rank), BF16),
            pltpu.VMEM((part, size), BF16),
            pltpu.VMEM(tall, F32),
            pltpu.SemaphoreType.DMA((2,)),
        ],
        60 * 1024 * 1024,
    )
    small = keep + swap(give, 1)
    bit = 4
    while bit < peers // 2:
        small = small + swap(small, bit)
        bit *= 2

    tokens = (base, cotangent)
    ends = order[-1] ^ 2
    for k, m in enumerate(order):
        low = m & -m
        if m != low:
            shards[m] = swap(after(shards[m ^ low], shards[order[k - 2] ^ 2]), low)
        before = shards[order[k - 1] ^ 2] if k else shards[2]
        shards[m ^ 2] = swap(after(shards[m], before, *([small] if m ^ 2 == ends else [])), 2)
    small = after(small, shards[peers // 2])
    small = small + swap(small, peers // 2)
    small = small + swap(small.astype(BF16), 2).astype(F32)
    small_other = swap(small, 1)
    keeps = [small, *from_sections(small.astype(BF16))]
    others = [small_other, *from_sections(small_other.astype(BF16))]

    marks = [m for m in range(0, peers, 2) if m != ends]
    for m in marks:
        shards[m ^ 1] = swap(shards[m], 1)
    marks += [m ^ 1 for m in marks]
    acc = project([spot ^ m for m in marks], flag, [shards[m] for m in marks], tokens)[0]
    pair = [shards[ends], swap(shards[ends], 1)]
    acc, send = project([spot ^ ends, spot ^ ends ^ 1], flag, pair, tokens, acc, final=True)
    sent = from_sections(send)

    near = list(range(0, peers, 4))
    every = near + [m ^ 2 for m in near]
    half = part // 2
    if sections == 2:
        columns, block_id = half, lambda i: i * 2 + flag
    else:
        columns, block_id = part, lambda i: i
    both = (spot ^ 1, spot)
    out_ids = [block_id(who ^ m) for who in both for m in every]
    in_ids = [(who ^ m) * 2 + k for k in range(2) for who in both for m in every]
    blocks = lambda n: ((len(every), rank, n), BF16)
    thin_count = 1 if sections == 2 else 2
    codes, *rest = call(
        functools.partial(chain_kernel, sections, width),
        [here, core, *out_ids, *in_ids],
        [],
        [base, cotangent, acc, *sent, *keeps, *others],
        [((rows, size), BF16)]
        + [((rank, size), F32)] * thin_count
        + [blocks(columns)] * 2
        + [blocks(half)] * 4,
        vmem_bytes=(VMEM_BYTES if sections == 2 else 32 * 1024 * 1024),
    )
    thins, chunks = rest[:thin_count], rest[thin_count:]
    got = [swap(give, 1) for give in chunks[::2]]
    lower, lower_x = scatter_sum(got[1], chunks[3])
    upper, upper_x = scatter_sum(got[2], chunks[5])
    sum_out, _ = scatter_sum(got[0], chunks[1], [got[1:], [lower_x], [upper_x]])
    sum_out = sum_out[0] + sum_out[1].astype(F32)
    ends_out = [sum_out]
    if sections == 2:
        ends_out = [swap(sum_out, 1, "section"), sum_out]
    waits = [None, got[2], lower_x]
    terms = [term for thin in thins for term in sum_thin(thin, waits)]
    grad_in, grad_out = call(
        functools.partial(end_kernel, sections),
        [flag, spot],
        [],
        [gain, subspace, *terms, *ends_out, *lower, *upper],
        [((part, rank), F32)] * 2,
    )
    return codes[None], grad_in[None], grad_out[None]


def solution(mesh):
    placed = (
        P("dp", None),
        P("dp", None),
        P("section", None),
        P("section", "dp", None),
        P("section", "dp", None),
        P("dp", None),
    )
    return jax.shard_map(
        on_device,
        mesh=mesh,
        in_specs=placed,
        out_specs=(P("section", "dp", None), P("section", "dp", None), P("section", "dp", None)),
        check_vma=False,
    )
```

```python
import functools

import jax
import jax.numpy as jnp
from jax import lax
from jax.experimental import pallas as pl
from jax.experimental.pallas import tpu as pltpu
from jax.sharding import PartitionSpec as P

F32 = jnp.float32
BF16 = jnp.bfloat16
VMEM_BYTES = 16 * 1024 * 1024
IN_VMEM = pl.BlockSpec(memory_space=pltpu.VMEM)
IN_SMEM = pl.BlockSpec(memory_space=pltpu.SMEM)
IN_HBM = pl.BlockSpec(memory_space=pltpu.HBM)
CONTRACT = ((1,), (0,))
ROWS = ((0,), (0,))
COLUMNS = ((1,), (1,))


def mm(a, b, dims=CONTRACT):
    return lax.dot_general(a, b, (dims, ((), ())), preferred_element_type=F32)


def parts_of(a):
    if a.dtype == BF16:
        return [a]
    high = a.astype(BF16)
    return [high, (a - high.astype(F32)).astype(BF16)]


def exact(a, b, dims=CONTRACT):
    left, right = parts_of(a), parts_of(b)
    total = mm(left[0], right[0], dims)
    for i, x in enumerate(left):
        for j, y in enumerate(right):
            if i + j == 1:
                total = total + mm(x, y, dims)
    return total


def call(kernel, scalars, far, arrays, shapes, scratch=(), vmem_bytes=VMEM_BYTES, flops=0):
    return pl.pallas_call(
        kernel,
        in_specs=[IN_SMEM] + [IN_HBM] * len(far) + [IN_VMEM] * len(arrays),
        out_specs=[IN_VMEM] * len(shapes),
        out_shape=[jax.ShapeDtypeStruct(*s) for s in shapes],
        scratch_shapes=list(scratch),
        compiler_params=pltpu.CompilerParams(vmem_limit_bytes=vmem_bytes),
        cost_estimate=pl.CostEstimate(flops=flops, bytes_accessed=0, transcendentals=0),
    )(jnp.stack(scalars).astype(jnp.int32), *far, *arrays)


def fetch(pairs, sems, first=0):
    copies = [pltpu.make_async_copy(a, b, sems.at[first + i]) for i, (a, b) in enumerate(pairs)]
    for copy in copies:
        copy.start()
    return copies


def swap(value, bits, axis="dp"):
    peers = lax.axis_size(axis)
    return lax.ppermute(value, axis, [(i, i ^ bits) for i in range(peers)])


def after(value, *others):
    return lax.optimization_barrier((value, *others))[0]


def from_sections(value):
    sections = lax.axis_size("section")
    here = lax.axis_index("section")
    if sections == 2:
        return [swap(value, 1, "section")]
    around = [(i, (i + 1) % sections) for i in range(sections)]
    held = [value]
    for _ in range(sections - 1):
        held.append(lax.ppermute(held[-1], "section", around))
    stacked = jnp.stack(held)
    order = (here - jnp.arange(sections)) % sections
    return [lax.dynamic_index_in_dim(stacked, order[s], 0, keepdims=False) for s in range(sections)]


def own_kernel(scalars, in_far, out_ref, space_ref, gain_far, own_ref, in_ref, gain_ref, sems):
    part, rank = in_ref.shape
    half = part // 2
    start = pl.multiple_of(scalars[1] * part, part)
    first = fetch([(in_far, in_ref), (gain_far.at[:, pl.ds(start, part)], gain_ref)], sems)
    places = own_ref.at[part : 2 * part], own_ref.at[2 * part :]

    def copy_both(sources):
        for copy in fetch(list(zip(sources, places)), sems, 2):
            copy.wait()

    @pl.when(scalars[0] == 1)
    def _():
        copy_both((out_ref, space_ref.at[half:, rank:]))

    @pl.when(scalars[0] == 0)
    def _():
        copy_both((space_ref.at[:, :rank], space_ref.at[:half, rank:]))

    for copy in first:
        copy.wait()
    column = jnp.broadcast_to(gain_ref[...], (rank, part)).T
    own_ref[:part] = (in_ref[...].astype(F32) * column).astype(BF16)


def small_kernel(scalars, out_far, space_far, own_ref, keep_ref, give_ref, *scratch):
    out_ref, space_ref, all_ref, sems = scratch
    is_last, core = scalars[0] == 1, scalars[1]
    part, rank = out_ref.shape
    for copy in fetch([(space_far, space_ref), (out_far, out_ref)], sems):
        copy.wait()
    space = space_ref[...]
    all_ref[:rank] = mm(out_ref[...], space, ROWS)
    all_ref[rank : 2 * rank] = mm(own_ref[:part], space, ROWS)
    columns = jnp.where(is_last, space_ref[:, rank:], space_ref[:, :rank])
    all_ref[2 * rank :] = mm(columns, space, ROWS)
    half = keep_ref.shape[0]
    first, second = all_ref[:half], all_ref[half:]
    keep_ref[...] = jnp.where(core == 0, first, second)
    give_ref[...] = jnp.where(core == 0, second, first)


def project_kernel(first, final, count, scalars, base_ref, cot_ref, *refs):
    shards, refs = refs[:count], list(refs[count:])
    acc = None if first else refs.pop(0)
    out = refs.pop(0)
    rank = out.shape[1] // 6
    part = shards[0].shape[0] * 2 // 5
    half = part // 2
    skip = scalars[count] * half
    out[...] = jnp.zeros_like(out) if first else acc[...]
    for t, shard in enumerate(shards):
        start = pl.multiple_of(scalars[t] * part, part)
        half_start = pl.multiple_of(start + skip, half)
        tokens = base_ref[:, pl.ds(start, part)]
        tokens_f = tokens.astype(F32)
        square = tokens_f * tokens_f
        total = square[:, :rank]
        for at in range(rank, part, rank):
            total = total + square[:, at : at + rank]
        wide = jnp.concatenate([shard[:part], shard[part : 2 * part]], axis=1)
        out[:, : 2 * rank] += mm(tokens, wide)
        out[:, 2 * rank : 3 * rank] += mm(base_ref[:, pl.ds(half_start, half)], shard[2 * part :])
        out[:, 3 * rank : 4 * rank] += mm(cot_ref[:, pl.ds(start, part)], shard[part : 2 * part])
        out[:, 4 * rank : 5 * rank] += mm(cot_ref[:, pl.ds(half_start, half)], shard[2 * part :])
        out[:, 5 * rank :] += total
    if final:
        refs[0][...] = out[:, : 5 * rank].astype(BF16)


def project(ids, flag, shards, tokens, acc=None, final=False):
    tall, rank = shards[0].shape
    rows, count = tokens[0].shape[0], len(ids)
    shapes = [((rows, 6 * rank), F32)]
    if final:
        shapes.append(((rows, 5 * rank), BF16))
    return call(
        functools.partial(project_kernel, acc is None, final, count),
        [*ids, flag],
        [],
        [*tokens, *shards] + ([] if acc is None else [acc]),
        shapes,
        flops=4 * rows * tall * rank * count,
    )


def outer_into(scalars, at, small, tokens_ref, outs):
    for out in outs:
        count, _, columns = out.shape
        for j in range(count):
            start = pl.multiple_of(scalars[at] * columns, columns)
            out[j] = mm(small, tokens_ref[:, pl.ds(start, columns)]).astype(BF16)
            at += 1


def small_parts(sections, here, core, keeps, others, s):
    value = lambda refs: (
        jnp.where(here == s, refs[0][...], refs[1][...].astype(F32))
        if sections == 2
        else refs[1 + s][...].astype(F32)
    )
    mine, theirs = value(keeps), value(others)
    whole = jnp.concatenate(
        [jnp.where(core == 0, mine, theirs), jnp.where(core == 0, theirs, mine)]
    )
    rank = whole.shape[0] // 3
    return whole[:rank], whole[rank : 2 * rank], whole[2 * rank :]


def chain_kernel(sections, width, scalars, base_far, cot_far, own, *refs):
    here, core = scalars[0], scalars[1]
    n = 1 if sections == 2 else sections
    thin_count = 1 if sections == 2 else 2
    refs = list(refs)
    take = lambda count: [refs.pop(0) for _ in range(count)]
    sent, keeps, others = take(n), take(n + 1), take(n + 1)
    codes_ref, thin_refs = take(1)[0], take(thin_count)
    outs_c, outs_b = take(2), take(4)
    base_ref, cot_ref, sems = refs
    count = sems.shape[0] // 2
    step = base_ref.shape[0] // count
    slices = [slice(k * step, (k + 1) * step) for k in range(count)]
    cot_copies = fetch([(cot_far.at[k], cot_ref.at[k]) for k in slices], sems)
    base_copies = fetch([(base_far.at[k], base_ref.at[k]) for k in slices], sems, count)
    rank = own.shape[1] // 6
    last = sections - 1
    values = [
        jnp.where(
            here == s, own[:, : 5 * rank], sent[0 if sections == 2 else s][...].astype(F32)
        )
        for s in range(sections)
    ]
    column = lambda s, k: values[s][:, k * rank : (k + 1) * rank]
    spread = lambda k: jnp.concatenate(
        [column(0, k), column(0, k + 1) + column(last, k + 1)], axis=1
    )
    base_s = spread(1)
    square = jnp.sum(own[:, 5 * rank :], axis=1, keepdims=True)
    smalls = [small_parts(sections, here, core, keeps, others, s) for s in range(sections)]
    gram = jnp.concatenate([smalls[0][2], smalls[last][2]])
    choose = lambda s, value, other: value if other is None else jnp.where(here == s, value, other)
    state = []
    code = mine_code = None
    for s in range(sections):
        m_s, q_t, _ = smalls[s]
        inner, total, resid_s, before = column(s, 0), square, base_s, code
        if s:
            moved = exact(code, gram)
            total = square + jnp.sum(
                (2.0 * base_s + moved) * code.astype(F32), axis=1, keepdims=True
            )
            inner = inner + exact(code, q_t, COLUMNS)
            resid_s = base_s + moved
        inverse = lax.rsqrt(jnp.maximum(total, 0.0) * (1.0 / width) + 1e-05)
        inner = inner * inverse
        logistic = 1.0 / (1.0 + jnp.exp(-inner))
        active = inner * logistic
        grown = exact(active, m_s)
        code = (moved + grown if s else grown).astype(BF16)
        mine_code = choose(s, code, mine_code)
        state.append((m_s, q_t, inner, logistic, inverse, active, resid_s, before))
    codes_ref[...] = mine_code
    active_t = state[last][5].T.astype(BF16)
    for copy in cot_copies:
        copy.wait()
    outer_into(scalars, 2, active_t, cot_ref, outs_c)

    grad_active, grad_y = column(last, 3), spread(3)
    mine = thin_in = thin_out = None
    for s in range(last, -1, -1):
        m_s, q_t, inner, logistic, inverse, active, resid_s, before = state[s]
        if s < last:
            grad_active = exact(back, m_s, COLUMNS)
            grad_y = exact(back, gram) if s else None
            thin_out = choose(s, mm(active.T.astype(BF16), back), thin_out)
        grad_inner = grad_active * logistic * (1.0 + inner * (1.0 - logistic))
        scaled = inverse * grad_inner
        scaled_t = scaled.T.astype(BF16)
        scaled = scaled.astype(BF16)
        mine = choose(s, scaled_t, mine)
        if s:
            thin_in = choose(s, mm(scaled_t, before), thin_in)
            along = jnp.sum(inner * grad_inner, axis=1, keepdims=True)
            along = along * (inverse * inverse * (1.0 / width))
            back = (grad_y + exact(scaled, q_t) - resid_s * along).astype(BF16)
    if sections == 2:
        thin_refs[0][...] = jnp.where(here == last, thin_in, thin_out)
    else:
        thin_refs[0][...] = jnp.where(here == 0, 0.0, thin_in)
        thin_refs[1][...] = thin_out
    for copy in base_copies:
        copy.wait()
    outer_into(scalars, 2 + 2 * outs_c[0].shape[0], mine, base_ref, outs_b)


def end_kernel(sections, scalars, gain_ref, space_ref, *refs):
    is_last = scalars[0] == 1
    part = space_ref.shape[0]
    grad_in, grad_out = refs[-2:]
    refs = list(refs[:-2])
    pair = lambda: refs.pop(0)[...].astype(F32) + refs.pop(0)[...].astype(F32)
    thin_in = pair()
    thin_out = thin_in if sections == 2 else pair()
    space = space_ref[...]
    lift_in = exact(thin_in, space, COLUMNS)
    lift_out = lift_in if sections == 2 else exact(thin_out, space, COLUMNS)
    if sections == 2:
        lift_in = jnp.where(is_last, lift_in, 0.0)
        half_first, half_second = refs.pop(0)[...], refs.pop(0)[...]
        sum_out = jnp.concatenate([half_first, half_second], axis=1)
    else:
        sum_out = refs.pop(0)[...]
    sum_in = jnp.concatenate([pair(), pair()], axis=1)
    start = pl.multiple_of(scalars[1] * part, part)
    total = gain_ref[:, pl.ds(start, part)] * (sum_in + lift_in)
    grad_in[...] = total.T
    grad_out[...] = jnp.where(is_last, sum_out, lift_out).T


def sum_thin(value, waits):
    peers = lax.axis_size("dp")
    bit, step = 1, 0
    while bit < peers:
        if step:
            wait = waits[min(step, len(waits)) - 1]
            value = value + got if wait is None else after(value + got, wait)
        got = swap(value, bit)
        bit, step = bit * 2, step + 1
    return value, got


def scatter_sum(got, keep, waits=()):
    half = got.shape[0] // 2
    summed = (keep[half:].astype(F32) + got[half:].astype(F32)).astype(BF16)
    got_x = swap(summed, 2)
    total = keep[:half].astype(F32) + got[:half].astype(F32) + got_x.astype(F32)
    bit = 4
    while True:
        left = total.reshape((total.shape[0] // 2, 2) + total.shape[1:])
        give = left[:, 1].astype(BF16)
        if waits:
            give = after(give, *waits[0])
            waits = waits[1:]
        arrived = swap(give, bit)
        if left.shape[0] == 1:
            return (left[0, 0], arrived[0]), got_x, total
        total = left[:, 0] + arrived.astype(F32)
        bit *= 2


def on_device(base, cotangent, gain, weight_in, weight_out, subspace):
    sections = lax.axis_size("section")
    here = lax.axis_index("section")
    spot = lax.axis_index("dp")
    core = spot % 2
    rows, width = base.shape
    part, size = subspace.shape
    rank = weight_in.shape[2]
    last = sections - 1
    flag = (here == last).astype(jnp.int32)
    own_in, own_out = weight_in[0], weight_out[0]
    own = call(
        own_kernel,
        [flag, spot],
        [own_in, own_out, subspace, gain],
        [],
        [((part * 5 // 2, rank), BF16)],
        [pltpu.VMEM((part, rank), BF16), pltpu.VMEM((1, part), F32), pltpu.SemaphoreType.DMA((4,))],
        62 * 1024 * 1024,
    )[0]

    peers = lax.axis_size("dp")
    order = sorted(range(4, peers, 4), key=lambda m: (m.bit_count(), m))
    shards = {0: own}
    shards[2] = swap(own, 2)
    for k, m in enumerate(order):
        if m.bit_count() == 1:
            shards[m] = swap(after(own, shards[order[k - 1]]) if k else own, m)

    shards[order[0] ^ 2] = swap(after(shards[order[0]], shards[2]), 2)
    tall = (3 * rank, size)
    keep, give = call(
        small_kernel,
        [flag, core],
        [own_out, subspace],
        [after(own, shards[order[0] ^ 2])],
        [((tall[0] // 2, size), F32)] * 2,
        [
            pltpu.VMEM((part, rank), BF16),
            pltpu.VMEM((part, size), BF16),
            pltpu.VMEM(tall, F32),
            pltpu.SemaphoreType.DMA((2,)),
        ],
        60 * 1024 * 1024,
    )
    small = keep + swap(give, 1)
    small = small + swap(small.astype(BF16), 2).astype(F32)
    bit = 4
    while bit < peers // 2:
        small = small + swap(small, bit)
        bit *= 2

    tokens = (base, cotangent)
    ends = order[-1] ^ 2
    for k, m in enumerate(order):
        low = m & -m
        if m != low:
            shards[m] = swap(after(shards[m ^ low], shards[order[k - 2] ^ 2]), low)
        if k:
            ties = [small] if m ^ 2 == ends else []
            shards[m ^ 2] = swap(after(shards[m], shards[order[k - 1] ^ 2], *ties), 2)
    small = after(small, shards[peers // 2])
    small = small + swap(small, peers // 2)
    small_other = swap(small, 1)
    keeps = [small, *from_sections(small.astype(BF16))]
    others = [small_other, *from_sections(small_other.astype(BF16))]

    marks = [m for m in range(0, peers, 2) if m != ends]
    for m in marks:
        shards[m ^ 1] = swap(shards[m], 1)
    marks += [m ^ 1 for m in marks]
    acc = project([spot ^ m for m in marks], flag, [shards[m] for m in marks], tokens)[0]
    pair = [shards[ends], swap(after(shards[ends], acc), 1)]
    acc, send = project([spot ^ ends, spot ^ ends ^ 1], flag, pair, tokens, acc, final=True)
    sent = from_sections(send)

    near = list(range(0, peers, 4))
    every = near + [m ^ 2 for m in near]
    half = part // 2
    if sections == 2:
        columns, block_id = half, lambda i: i * 2 + flag
    else:
        columns, block_id = part, lambda i: i
    both = (spot ^ 1, spot)
    out_ids = [block_id(who ^ m) for who in both for m in every]
    in_ids = [(who ^ m) * 2 + k for k in range(2) for who in both for m in every]
    blocks = lambda n: ((len(every), rank, n), BF16)
    thin_count = 1 if sections == 2 else 2
    codes, *rest = call(
        functools.partial(chain_kernel, sections, width),
        [here, core, *out_ids, *in_ids],
        [base, cotangent],
        [acc, *sent, *keeps, *others],
        [((rows, size), BF16)]
        + [((rank, size), F32)] * thin_count
        + [blocks(columns)] * 2
        + [blocks(half)] * 4,
        [
            pltpu.VMEM(base.shape, BF16),
            pltpu.VMEM(base.shape, BF16),
            pltpu.SemaphoreType.DMA((8,)),
        ],
        50 * 1024 * 1024,
    )
    thins, chunks = rest[:thin_count], rest[thin_count:]
    got = [swap(give, 1) for give in chunks[::2]]
    sum_out, out_x, out_near = scatter_sum(got[0], chunks[1])
    lower, lower_x, _ = scatter_sum(got[1], chunks[3], [[out_x]])
    upper, _, _ = scatter_sum(got[2], chunks[5], [[out_near]])
    sum_out = sum_out[0] + sum_out[1].astype(F32)
    ends_out = [sum_out]
    if sections == 2:
        ends_out = [swap(sum_out, 1, "section"), sum_out]
    waits = [got[2], out_x, lower_x]
    terms = [term for thin in thins for term in sum_thin(thin, waits)]
    grad_in, grad_out = call(
        functools.partial(end_kernel, sections),
        [flag, spot],
        [],
        [gain, subspace, *terms, *ends_out, *lower, *upper],
        [((part, rank), F32)] * 2,
    )
    return codes[None], grad_in[None], grad_out[None]


def solution(mesh):
    placed = (
        P("dp", None),
        P("dp", None),
        P("section", None),
        P("section", "dp", None),
        P("section", "dp", None),
        P("dp", None),
    )
    return jax.shard_map(
        on_device,
        mesh=mesh,
        in_specs=placed,
        out_specs=(P("section", "dp", None), P("section", "dp", None), P("section", "dp", None)),
        check_vma=False,
    )
```

```python
import functools

import jax
import jax.numpy as jnp
from jax import lax
from jax.experimental import pallas as pl
from jax.experimental.pallas import tpu as pltpu
from jax.sharding import PartitionSpec as P

F32 = jnp.float32
BF16 = jnp.bfloat16
VMEM_BYTES = 16 * 1024 * 1024
IN_VMEM = pl.BlockSpec(memory_space=pltpu.VMEM)
IN_SMEM = pl.BlockSpec(memory_space=pltpu.SMEM)
IN_HBM = pl.BlockSpec(memory_space=pltpu.HBM)
CONTRACT = ((1,), (0,))
ROWS = ((0,), (0,))
COLUMNS = ((1,), (1,))


def mm(a, b, dims=CONTRACT):
    return lax.dot_general(a, b, (dims, ((), ())), preferred_element_type=F32)


def parts_of(a):
    if a.dtype == BF16:
        return [a]
    high = a.astype(BF16)
    return [high, (a - high.astype(F32)).astype(BF16)]


def exact(a, b, dims=CONTRACT):
    left, right = parts_of(a), parts_of(b)
    total = mm(left[0], right[0], dims)
    for i, x in enumerate(left):
        for j, y in enumerate(right):
            if i + j == 1:
                total = total + mm(x, y, dims)
    return total


def call(kernel, scalars, far, arrays, shapes, scratch=(), vmem_bytes=VMEM_BYTES, flops=0):
    return pl.pallas_call(
        kernel,
        in_specs=[IN_SMEM] + [IN_HBM] * len(far) + [IN_VMEM] * len(arrays),
        out_specs=[IN_VMEM] * len(shapes),
        out_shape=[jax.ShapeDtypeStruct(*s) for s in shapes],
        scratch_shapes=list(scratch),
        compiler_params=pltpu.CompilerParams(vmem_limit_bytes=vmem_bytes),
        cost_estimate=pl.CostEstimate(flops=flops, bytes_accessed=0, transcendentals=0),
    )(jnp.stack(scalars).astype(jnp.int32), *far, *arrays)


def fetch(pairs, sems, first=0):
    copies = [pltpu.make_async_copy(a, b, sems.at[first + i]) for i, (a, b) in enumerate(pairs)]
    for copy in copies:
        copy.start()
    return copies


def swap(value, bits, axis="dp"):
    peers = lax.axis_size(axis)
    return lax.ppermute(value, axis, [(i, i ^ bits) for i in range(peers)])


def after(value, *others):
    return lax.optimization_barrier((value, *others))[0]


def from_sections(value):
    sections = lax.axis_size("section")
    here = lax.axis_index("section")
    if sections == 2:
        return [swap(value, 1, "section")]
    around = [(i, (i + 1) % sections) for i in range(sections)]
    held = [value]
    for _ in range(sections - 1):
        held.append(lax.ppermute(held[-1], "section", around))
    stacked = jnp.stack(held)
    order = (here - jnp.arange(sections)) % sections
    return [lax.dynamic_index_in_dim(stacked, order[s], 0, keepdims=False) for s in range(sections)]


def own_kernel(scalars, in_far, out_ref, space_ref, gain_far, own_ref, in_ref, gain_ref, sems):
    part, rank = in_ref.shape
    half = part // 2
    start = pl.multiple_of(scalars[1] * part, part)
    first = fetch([(in_far, in_ref), (gain_far.at[:, pl.ds(start, part)], gain_ref)], sems)
    places = own_ref.at[part : 2 * part], own_ref.at[2 * part :]

    def copy_both(sources):
        for copy in fetch(list(zip(sources, places)), sems, 2):
            copy.wait()

    @pl.when(scalars[0] == 1)
    def _():
        copy_both((out_ref, space_ref.at[half:, rank:]))

    @pl.when(scalars[0] == 0)
    def _():
        copy_both((space_ref.at[:, :rank], space_ref.at[:half, rank:]))

    for copy in first:
        copy.wait()
    column = jnp.broadcast_to(gain_ref[...], (rank, part)).T
    own_ref[:part] = (in_ref[...].astype(F32) * column).astype(BF16)


def small_kernel(scalars, out_far, space_far, own_ref, keep_ref, give_ref, *scratch):
    out_ref, space_ref, all_ref, sems = scratch
    is_last, core = scalars[0] == 1, scalars[1]
    part, rank = out_ref.shape
    for copy in fetch([(space_far, space_ref), (out_far, out_ref)], sems):
        copy.wait()
    space = space_ref[...]
    all_ref[:rank] = mm(out_ref[...], space, ROWS)
    all_ref[rank : 2 * rank] = mm(own_ref[:part], space, ROWS)
    columns = jnp.where(is_last, space_ref[:, rank:], space_ref[:, :rank])
    all_ref[2 * rank :] = mm(columns, space, ROWS)
    half = keep_ref.shape[0]
    first, second = all_ref[:half], all_ref[half:]
    keep_ref[...] = jnp.where(core == 0, first, second)
    give_ref[...] = jnp.where(core == 0, second, first)


def project_kernel(first, final, count, scalars, base_ref, cot_ref, *refs):
    shards, refs = refs[:count], list(refs[count:])
    acc = None if first else refs.pop(0)
    out = refs.pop(0)
    rank = out.shape[1] // 6
    part = shards[0].shape[0] * 2 // 5
    half = part // 2
    skip = scalars[count] * half
    out[...] = jnp.zeros_like(out) if first else acc[...]
    for t, shard in enumerate(shards):
        start = pl.multiple_of(scalars[t] * part, part)
        half_start = pl.multiple_of(start + skip, half)
        tokens = base_ref[:, pl.ds(start, part)]
        tokens_f = tokens.astype(F32)
        square = tokens_f * tokens_f
        total = square[:, :rank]
        for at in range(rank, part, rank):
            total = total + square[:, at : at + rank]
        wide = jnp.concatenate([shard[:part], shard[part : 2 * part]], axis=1)
        out[:, : 2 * rank] += mm(tokens, wide)
        out[:, 2 * rank : 3 * rank] += mm(base_ref[:, pl.ds(half_start, half)], shard[2 * part :])
        out[:, 3 * rank : 4 * rank] += mm(cot_ref[:, pl.ds(start, part)], shard[part : 2 * part])
        out[:, 4 * rank : 5 * rank] += mm(cot_ref[:, pl.ds(half_start, half)], shard[2 * part :])
        out[:, 5 * rank :] += total
    if final:
        refs[0][...] = out[:, : 5 * rank].astype(BF16)


def project(ids, flag, shards, tokens, acc=None, final=False):
    tall, rank = shards[0].shape
    rows, count = tokens[0].shape[0], len(ids)
    shapes = [((rows, 6 * rank), F32)]
    if final:
        shapes.append(((rows, 5 * rank), BF16))
    return call(
        functools.partial(project_kernel, acc is None, final, count),
        [*ids, flag],
        [],
        [*tokens, *shards] + ([] if acc is None else [acc]),
        shapes,
        flops=4 * rows * tall * rank * count,
    )


def outer_into(scalars, at, small, tokens_ref, outs):
    for out in outs:
        count, _, columns = out.shape
        for j in range(count):
            start = pl.multiple_of(scalars[at] * columns, columns)
            out[j] = mm(small, tokens_ref[:, pl.ds(start, columns)]).astype(BF16)
            at += 1


def small_parts(sections, here, core, keeps, others, s):
    value = lambda refs: (
        jnp.where(here == s, refs[0][...], refs[1][...].astype(F32))
        if sections == 2
        else refs[1 + s][...].astype(F32)
    )
    mine, theirs = value(keeps), value(others)
    whole = jnp.concatenate(
        [jnp.where(core == 0, mine, theirs), jnp.where(core == 0, theirs, mine)]
    )
    rank = whole.shape[0] // 3
    return whole[:rank], whole[rank : 2 * rank], whole[2 * rank :]


def chain_kernel(sections, width, scalars, base_ref, cot_ref, own, *refs):
    here, core = scalars[0], scalars[1]
    n = 1 if sections == 2 else sections
    thin_count = 1 if sections == 2 else 2
    refs = list(refs)
    take = lambda count: [refs.pop(0) for _ in range(count)]
    sent, keeps, others = take(n), take(n + 1), take(n + 1)
    codes_ref, thin_refs = take(1)[0], take(thin_count)
    outs_c, outs_b = take(2), take(2)
    rank = own.shape[1] // 6
    last = sections - 1
    values = [
        jnp.where(
            here == s, own[:, : 5 * rank], sent[0 if sections == 2 else s][...].astype(F32)
        )
        for s in range(sections)
    ]
    column = lambda s, k: values[s][:, k * rank : (k + 1) * rank]
    spread = lambda k: jnp.concatenate(
        [column(0, k), column(0, k + 1) + column(last, k + 1)], axis=1
    )
    base_s = spread(1)
    square = jnp.sum(own[:, 5 * rank :], axis=1, keepdims=True)
    smalls = [small_parts(sections, here, core, keeps, others, s) for s in range(sections)]
    gram = jnp.concatenate([smalls[0][2], smalls[last][2]])
    choose = lambda s, value, other: value if other is None else jnp.where(here == s, value, other)
    state = []
    code = mine_code = None
    for s in range(sections):
        m_s, q_t, _ = smalls[s]
        inner, total, resid_s, before = column(s, 0), square, base_s, code
        if s:
            moved = exact(code, gram)
            total = square + jnp.sum(
                (2.0 * base_s + moved) * code.astype(F32), axis=1, keepdims=True
            )
            inner = inner + exact(code, q_t, COLUMNS)
            resid_s = base_s + moved
        inverse = lax.rsqrt(jnp.maximum(total, 0.0) * (1.0 / width) + 1e-05)
        inner = inner * inverse
        logistic = 1.0 / (1.0 + jnp.exp(-inner))
        active = inner * logistic
        grown = exact(active, m_s)
        code = (moved + grown if s else grown).astype(BF16)
        mine_code = choose(s, code, mine_code)
        state.append((m_s, q_t, inner, logistic, inverse, active, resid_s, before))
    codes_ref[...] = mine_code
    active_t = state[last][5].T.astype(BF16)
    outer_into(scalars, 2, active_t, cot_ref, outs_c)

    grad_active, grad_y = column(last, 3), spread(3)
    mine = thin_in = thin_out = None
    for s in range(last, -1, -1):
        m_s, q_t, inner, logistic, inverse, active, resid_s, before = state[s]
        if s < last:
            grad_active = exact(back, m_s, COLUMNS)
            grad_y = exact(back, gram) if s else None
            thin_out = choose(s, mm(active.T.astype(BF16), back), thin_out)
        grad_inner = grad_active * logistic * (1.0 + inner * (1.0 - logistic))
        scaled = inverse * grad_inner
        scaled_t = scaled.T.astype(BF16)
        scaled = scaled.astype(BF16)
        mine = choose(s, scaled_t, mine)
        if s:
            thin_in = choose(s, mm(scaled_t, before), thin_in)
            along = jnp.sum(inner * grad_inner, axis=1, keepdims=True)
            along = along * (inverse * inverse * (1.0 / width))
            back = (grad_y + exact(scaled, q_t) - resid_s * along).astype(BF16)
    if sections == 2:
        thin_refs[0][...] = jnp.where(here == last, thin_in, thin_out)
    else:
        thin_refs[0][...] = jnp.where(here == 0, 0.0, thin_in)
        thin_refs[1][...] = thin_out
    outer_into(scalars, 2 + 2 * outs_c[0].shape[0], mine, base_ref, outs_b)


def end_kernel(sections, scalars, gain_ref, space_ref, *refs):
    is_last = scalars[0] == 1
    part = space_ref.shape[0]
    grad_in, grad_out = refs[-2:]
    refs = list(refs[:-2])
    pair = lambda: refs.pop(0)[...].astype(F32) + refs.pop(0)[...].astype(F32)
    thin_in = pair()
    thin_out = thin_in if sections == 2 else pair()
    space = space_ref[...]
    lift_in = exact(thin_in, space, COLUMNS)
    lift_out = lift_in if sections == 2 else exact(thin_out, space, COLUMNS)
    if sections == 2:
        lift_in = jnp.where(is_last, lift_in, 0.0)
        half_first, half_second = refs.pop(0)[...], refs.pop(0)[...]
        sum_out = jnp.concatenate([half_first, half_second], axis=1)
    else:
        sum_out = refs.pop(0)[...]
    sum_in = pair()
    start = pl.multiple_of(scalars[1] * part, part)
    total = gain_ref[:, pl.ds(start, part)] * (sum_in + lift_in)
    grad_in[...] = total.T
    grad_out[...] = jnp.where(is_last, sum_out, lift_out).T


def sum_thin(value, waits):
    peers = lax.axis_size("dp")
    bit, step = 1, 0
    while bit < peers:
        if step:
            wait = waits[min(step, len(waits)) - 1]
            value = value + got if wait is None else after(value + got, wait)
        got = swap(value, bit)
        bit, step = bit * 2, step + 1
    return value, got


def scatter_sum(got, keep, waits=()):
    half = got.shape[0] // 2
    summed = (keep[half:].astype(F32) + got[half:].astype(F32)).astype(BF16)
    got_x = swap(summed, 2)
    total = keep[:half].astype(F32) + got[:half].astype(F32) + got_x.astype(F32)
    bit = 4
    while True:
        left = total.reshape((total.shape[0] // 2, 2) + total.shape[1:])
        give = left[:, 1].astype(BF16)
        if waits:
            give = after(give, *waits[0])
            waits = waits[1:]
        arrived = swap(give, bit)
        if left.shape[0] == 1:
            return (left[0, 0], arrived[0]), got_x
        total = left[:, 0] + arrived.astype(F32)
        bit *= 2


def on_device(base, cotangent, gain, weight_in, weight_out, subspace):
    sections = lax.axis_size("section")
    here = lax.axis_index("section")
    spot = lax.axis_index("dp")
    core = spot % 2
    rows, width = base.shape
    part, size = subspace.shape
    rank = weight_in.shape[2]
    last = sections - 1
    flag = (here == last).astype(jnp.int32)
    own_in, own_out = weight_in[0], weight_out[0]
    own = call(
        own_kernel,
        [flag, spot],
        [own_in, own_out, subspace, gain],
        [],
        [((part * 5 // 2, rank), BF16)],
        [pltpu.VMEM((part, rank), BF16), pltpu.VMEM((1, part), F32), pltpu.SemaphoreType.DMA((4,))],
        62 * 1024 * 1024,
    )[0]

    peers = lax.axis_size("dp")
    order = sorted(range(4, peers, 4), key=lambda m: (m.bit_count(), m))
    shards = {0: own}
    shards[2] = swap(own, 2)
    for k, m in enumerate(order):
        if m.bit_count() == 1:
            shards[m] = swap(after(own, shards[order[k - 1]]) if k else own, m)

    shards[order[0] ^ 2] = swap(after(shards[order[0]], shards[2]), 2)
    tall = (3 * rank, size)
    keep, give = call(
        small_kernel,
        [flag, core],
        [own_out, subspace],
        [after(own, shards[order[0] ^ 2])],
        [((tall[0] // 2, size), F32)] * 2,
        [
            pltpu.VMEM((part, rank), BF16),
            pltpu.VMEM((part, size), BF16),
            pltpu.VMEM(tall, F32),
            pltpu.SemaphoreType.DMA((2,)),
        ],
        60 * 1024 * 1024,
    )
    small = keep + swap(give, 1)
    bit = 4
    while bit < peers // 2:
        small = small + swap(small, bit)
        bit *= 2

    tokens = (base, cotangent)
    ends = order[-1] ^ 2
    for k, m in enumerate(order):
        low = m & -m
        if m != low:
            shards[m] = swap(after(shards[m ^ low], shards[order[k - 2] ^ 2]), low)
        if k:
            ties = [small] if m ^ 2 == ends else []
            shards[m ^ 2] = swap(after(shards[m], shards[order[k - 1] ^ 2], *ties), 2)
    small = after(small, shards[peers // 2])
    small = small + swap(small, peers // 2)
    small = small + swap(small.astype(BF16), 2).astype(F32)
    small_other = swap(small, 1)
    keeps = [small, *from_sections(small.astype(BF16))]
    others = [small_other, *from_sections(small_other.astype(BF16))]

    marks = [m for m in range(0, peers, 2) if m != ends]
    for m in marks:
        shards[m ^ 1] = swap(shards[m], 1)
    marks += [m ^ 1 for m in marks]
    acc = project([spot ^ m for m in marks], flag, [shards[m] for m in marks], tokens)[0]
    pair = [shards[ends], swap(after(shards[ends], acc), 1)]
    acc, send = project([spot ^ ends, spot ^ ends ^ 1], flag, pair, tokens, acc, final=True)
    sent = from_sections(send)

    near = list(range(0, peers, 4))
    every = near + [m ^ 2 for m in near]
    half = part // 2
    if sections == 2:
        columns, block_id = half, lambda i: i * 2 + flag
    else:
        columns, block_id = part, lambda i: i
    both = (spot ^ 1, spot)
    out_ids = [block_id(who ^ m) for who in both for m in every]
    in_ids = [who ^ m for who in both for m in every]
    blocks = lambda n: ((len(every), rank, n), BF16)
    thin_count = 1 if sections == 2 else 2
    codes, *rest = call(
        functools.partial(chain_kernel, sections, width),
        [here, core, *out_ids, *in_ids],
        [],
        [base, cotangent, acc, *sent, *keeps, *others],
        [((rows, size), BF16)]
        + [((rank, size), F32)] * thin_count
        + [blocks(columns)] * 2
        + [blocks(part)] * 2,
        vmem_bytes=(VMEM_BYTES if sections == 2 else 32 * 1024 * 1024),
    )
    thins, chunks = rest[:thin_count], rest[thin_count:]
    got = [swap(give, 1) for give in chunks[::2]]
    sum_out, out_x = scatter_sum(got[0], chunks[1])
    sum_in, in_x = scatter_sum(got[1], chunks[3])
    sum_out = sum_out[0] + sum_out[1].astype(F32)
    ends_out = [sum_out]
    if sections == 2:
        ends_out = [swap(sum_out, 1, "section"), sum_out]
    waits = [got[1], out_x, in_x]
    terms = [term for thin in thins for term in sum_thin(thin, waits)]
    grad_in, grad_out = call(
        functools.partial(end_kernel, sections),
        [flag, spot],
        [],
        [gain, subspace, *terms, *ends_out, *sum_in],
        [((part, rank), F32)] * 2,
    )
    return codes[None], grad_in[None], grad_out[None]


def solution(mesh):
    placed = (
        P("dp", None),
        P("dp", None),
        P("section", None),
        P("section", "dp", None),
        P("section", "dp", None),
        P("dp", None),
    )
    return jax.shard_map(
        on_device,
        mesh=mesh,
        in_specs=placed,
        out_specs=(P("section", "dp", None), P("section", "dp", None), P("section", "dp", None)),
        check_vma=False,
    )
```

```python
import functools

import jax
import jax.numpy as jnp
from jax import lax
from jax.experimental import pallas as pl
from jax.experimental.pallas import tpu as pltpu
from jax.sharding import PartitionSpec as P

F32 = jnp.float32
BF16 = jnp.bfloat16
VMEM_BYTES = 16 * 1024 * 1024
IN_VMEM = pl.BlockSpec(memory_space=pltpu.VMEM)
IN_SMEM = pl.BlockSpec(memory_space=pltpu.SMEM)
IN_HBM = pl.BlockSpec(memory_space=pltpu.HBM)
CONTRACT = ((1,), (0,))
ROWS = ((0,), (0,))
COLUMNS = ((1,), (1,))


def mm(a, b, dims=CONTRACT):
    return lax.dot_general(a, b, (dims, ((), ())), preferred_element_type=F32)


def parts_of(a):
    if a.dtype == BF16:
        return [a]
    high = a.astype(BF16)
    return [high, (a - high.astype(F32)).astype(BF16)]


def exact(a, b, dims=CONTRACT):
    left, right = parts_of(a), parts_of(b)
    total = mm(left[0], right[0], dims)
    for i, x in enumerate(left):
        for j, y in enumerate(right):
            if i + j == 1:
                total = total + mm(x, y, dims)
    return total


def call(kernel, scalars, far, arrays, shapes, scratch=(), vmem_bytes=VMEM_BYTES, flops=0):
    return pl.pallas_call(
        kernel,
        in_specs=[IN_SMEM] + [IN_HBM] * len(far) + [IN_VMEM] * len(arrays),
        out_specs=[IN_VMEM] * len(shapes),
        out_shape=[jax.ShapeDtypeStruct(*s) for s in shapes],
        scratch_shapes=list(scratch),
        compiler_params=pltpu.CompilerParams(vmem_limit_bytes=vmem_bytes),
        cost_estimate=pl.CostEstimate(flops=flops, bytes_accessed=0, transcendentals=0),
    )(jnp.stack(scalars).astype(jnp.int32), *far, *arrays)


def fetch(pairs, sems, first=0):
    copies = [pltpu.make_async_copy(a, b, sems.at[first + i]) for i, (a, b) in enumerate(pairs)]
    for copy in copies:
        copy.start()
    return copies


def swap(value, bits, axis="dp"):
    peers = lax.axis_size(axis)
    return lax.ppermute(value, axis, [(i, i ^ bits) for i in range(peers)])


def after(value, *others):
    return lax.optimization_barrier((value, *others))[0]


def from_sections(value):
    sections = lax.axis_size("section")
    here = lax.axis_index("section")
    if sections == 2:
        return [swap(value, 1, "section")]
    around = [(i, (i + 1) % sections) for i in range(sections)]
    held = [value]
    for _ in range(sections - 1):
        held.append(lax.ppermute(held[-1], "section", around))
    stacked = jnp.stack(held)
    order = (here - jnp.arange(sections)) % sections
    return [lax.dynamic_index_in_dim(stacked, order[s], 0, keepdims=False) for s in range(sections)]


def own_kernel(scalars, in_far, out_ref, space_ref, gain_far, own_ref, in_ref, gain_ref, sems):
    part, rank = in_ref.shape
    half = part // 2
    start = pl.multiple_of(scalars[1] * part, part)
    first = fetch([(in_far, in_ref), (gain_far.at[:, pl.ds(start, part)], gain_ref)], sems)
    places = own_ref.at[part : 2 * part], own_ref.at[2 * part :]

    def copy_both(sources):
        for copy in fetch(list(zip(sources, places)), sems, 2):
            copy.wait()

    @pl.when(scalars[0] == 1)
    def _():
        copy_both((out_ref, space_ref.at[half:, rank:]))

    @pl.when(scalars[0] == 0)
    def _():
        copy_both((space_ref.at[:, :rank], space_ref.at[:half, rank:]))

    for copy in first:
        copy.wait()
    column = jnp.broadcast_to(gain_ref[...], (rank, part)).T
    own_ref[:part] = (in_ref[...].astype(F32) * column).astype(BF16)


def small_kernel(scalars, out_far, space_far, own_ref, keep_ref, give_ref, *scratch):
    out_ref, space_ref, all_ref, sems = scratch
    is_last, core = scalars[0] == 1, scalars[1]
    part, rank = out_ref.shape
    for copy in fetch([(space_far, space_ref), (out_far, out_ref)], sems):
        copy.wait()
    space = space_ref[...]
    all_ref[:rank] = mm(out_ref[...], space, ROWS)
    all_ref[rank : 2 * rank] = mm(own_ref[:part], space, ROWS)
    columns = jnp.where(is_last, space_ref[:, rank:], space_ref[:, :rank])
    all_ref[2 * rank :] = mm(columns, space, ROWS)
    half = keep_ref.shape[0]
    first, second = all_ref[:half], all_ref[half:]
    keep_ref[...] = jnp.where(core == 0, first, second)
    give_ref[...] = jnp.where(core == 0, second, first)


def project_kernel(first, final, count, scalars, base_ref, cot_ref, *refs):
    shards, refs = refs[:count], list(refs[count:])
    acc = None if first else refs.pop(0)
    out = refs.pop(0)
    rank = out.shape[1] // 6
    part = shards[0].shape[0] * 2 // 5
    half = part // 2
    skip = scalars[count] * half
    out[...] = jnp.zeros_like(out) if first else acc[...]
    for t, shard in enumerate(shards):
        start = pl.multiple_of(scalars[t] * part, part)
        half_start = pl.multiple_of(start + skip, half)
        tokens = base_ref[:, pl.ds(start, part)]
        tokens_f = tokens.astype(F32)
        square = tokens_f * tokens_f
        total = square[:, :rank]
        for at in range(rank, part, rank):
            total = total + square[:, at : at + rank]
        wide = jnp.concatenate([shard[:part], shard[part : 2 * part]], axis=1)
        out[:, : 2 * rank] += mm(tokens, wide)
        out[:, 2 * rank : 3 * rank] += mm(base_ref[:, pl.ds(half_start, half)], shard[2 * part :])
        out[:, 3 * rank : 4 * rank] += mm(cot_ref[:, pl.ds(start, part)], shard[part : 2 * part])
        out[:, 4 * rank : 5 * rank] += mm(cot_ref[:, pl.ds(half_start, half)], shard[2 * part :])
        out[:, 5 * rank :] += total
    if final:
        refs[0][...] = out[:, : 5 * rank].astype(BF16)


def project(ids, flag, shards, tokens, acc=None, final=False):
    tall, rank = shards[0].shape
    rows, count = tokens[0].shape[0], len(ids)
    shapes = [((rows, 6 * rank), F32)]
    if final:
        shapes.append(((rows, 5 * rank), BF16))
    return call(
        functools.partial(project_kernel, acc is None, final, count),
        [*ids, flag],
        [],
        [*tokens, *shards] + ([] if acc is None else [acc]),
        shapes,
        flops=4 * rows * tall * rank * count,
    )


def outer_into(scalars, at, small, tokens_ref, outs):
    for out in outs:
        count, _, columns = out.shape
        for j in range(count):
            start = pl.multiple_of(scalars[at] * columns, columns)
            out[j] = mm(small, tokens_ref[:, pl.ds(start, columns)]).astype(BF16)
            at += 1


def small_parts(sections, here, core, keeps, others, s):
    value = lambda refs: (
        jnp.where(here == s, refs[0][...], refs[1][...].astype(F32))
        if sections == 2
        else refs[1 + s][...].astype(F32)
    )
    mine, theirs = value(keeps), value(others)
    whole = jnp.concatenate(
        [jnp.where(core == 0, mine, theirs), jnp.where(core == 0, theirs, mine)]
    )
    rank = whole.shape[0] // 3
    return whole[:rank], whole[rank : 2 * rank], whole[2 * rank :]


def chain_kernel(sections, width, scalars, base_ref, cot_ref, own, *refs):
    here, core = scalars[0], scalars[1]
    n = 1 if sections == 2 else sections
    thin_count = 1 if sections == 2 else 2
    refs = list(refs)
    take = lambda count: [refs.pop(0) for _ in range(count)]
    sent, keeps, others = take(n), take(n + 1), take(n + 1)
    codes_ref, thin_refs = take(1)[0], take(thin_count)
    outs_c, outs_b = take(2), take(2)
    rank = own.shape[1] // 6
    last = sections - 1
    values = [
        jnp.where(
            here == s, own[:, : 5 * rank], sent[0 if sections == 2 else s][...].astype(F32)
        )
        for s in range(sections)
    ]
    column = lambda s, k: values[s][:, k * rank : (k + 1) * rank]
    spread = lambda k: jnp.concatenate(
        [column(0, k), column(0, k + 1) + column(last, k + 1)], axis=1
    )
    base_s = spread(1)
    square = jnp.sum(own[:, 5 * rank :], axis=1, keepdims=True)
    smalls = [small_parts(sections, here, core, keeps, others, s) for s in range(sections)]
    gram = jnp.concatenate([smalls[0][2], smalls[last][2]])
    choose = lambda s, value, other: value if other is None else jnp.where(here == s, value, other)
    state = []
    code = mine_code = None
    for s in range(sections):
        m_s, q_t, _ = smalls[s]
        inner, total, resid_s, before = column(s, 0), square, base_s, code
        if s:
            moved = exact(code, gram)
            total = square + jnp.sum(
                (2.0 * base_s + moved) * code.astype(F32), axis=1, keepdims=True
            )
            inner = inner + exact(code, q_t, COLUMNS)
            resid_s = base_s + moved
        inverse = lax.rsqrt(jnp.maximum(total, 0.0) * (1.0 / width) + 1e-05)
        inner = inner * inverse
        logistic = 1.0 / (1.0 + jnp.exp(-inner))
        active = inner * logistic
        grown = exact(active, m_s)
        code = (moved + grown if s else grown).astype(BF16)
        mine_code = choose(s, code, mine_code)
        state.append((m_s, q_t, inner, logistic, inverse, active, resid_s, before))
    codes_ref[...] = mine_code
    active_t = state[last][5].T.astype(BF16)
    outer_into(scalars, 2, active_t, cot_ref, outs_c)

    grad_active, grad_y = column(last, 3), spread(3)
    mine = thin_in = thin_out = None
    for s in range(last, -1, -1):
        m_s, q_t, inner, logistic, inverse, active, resid_s, before = state[s]
        if s < last:
            grad_active = exact(back, m_s, COLUMNS)
            grad_y = exact(back, gram) if s else None
            thin_out = choose(s, mm(active.T.astype(BF16), back), thin_out)
        grad_inner = grad_active * logistic * (1.0 + inner * (1.0 - logistic))
        scaled = inverse * grad_inner
        scaled_t = scaled.T.astype(BF16)
        scaled = scaled.astype(BF16)
        mine = choose(s, scaled_t, mine)
        if s:
            thin_in = choose(s, mm(scaled_t, before), thin_in)
            along = jnp.sum(inner * grad_inner, axis=1, keepdims=True)
            along = along * (inverse * inverse * (1.0 / width))
            back = (grad_y + exact(scaled, q_t) - resid_s * along).astype(BF16)
    if sections == 2:
        thin_refs[0][...] = jnp.where(here == last, thin_in, thin_out)
    else:
        thin_refs[0][...] = jnp.where(here == 0, 0.0, thin_in)
        thin_refs[1][...] = thin_out
    outer_into(scalars, 2 + 2 * outs_c[0].shape[0], mine, base_ref, outs_b)


def end_kernel(sections, scalars, gain_ref, space_ref, *refs):
    is_last = scalars[0] == 1
    part = space_ref.shape[0]
    grad_in, grad_out = refs[-2:]
    refs = list(refs[:-2])
    pair = lambda: refs.pop(0)[...].astype(F32) + refs.pop(0)[...].astype(F32)
    thin_in = pair()
    thin_out = thin_in if sections == 2 else pair()
    space = space_ref[...]
    lift_in = exact(thin_in, space, COLUMNS)
    lift_out = lift_in if sections == 2 else exact(thin_out, space, COLUMNS)
    if sections == 2:
        lift_in = jnp.where(is_last, lift_in, 0.0)
        half_first, half_second = refs.pop(0)[...], refs.pop(0)[...]
        sum_out = jnp.concatenate([half_first, half_second], axis=1)
    else:
        sum_out = refs.pop(0)[...]
    sum_in = pair()
    start = pl.multiple_of(scalars[1] * part, part)
    total = gain_ref[:, pl.ds(start, part)] * (sum_in + lift_in)
    grad_in[...] = total.T
    grad_out[...] = jnp.where(is_last, sum_out, lift_out).T


def sum_thin(value, waits):
    peers = lax.axis_size("dp")
    bit, step = 1, 0
    while bit < peers:
        if step:
            wait = waits[min(step, len(waits)) - 1]
            value = value + got if wait is None else after(value + got, wait)
        got = swap(value, bit)
        bit, step = bit * 2, step + 1
    return value, got


def scatter_sum(got, keep, waits=()):
    half = got.shape[0] // 2
    summed = (keep[half:].astype(F32) + got[half:].astype(F32)).astype(BF16)
    got_x = swap(summed, 2)
    total = keep[:half].astype(F32) + got[:half].astype(F32) + got_x.astype(F32)
    bit = 4
    while True:
        left = total.reshape((total.shape[0] // 2, 2) + total.shape[1:])
        give = left[:, 1].astype(BF16)
        if waits:
            give = after(give, *waits[0])
            waits = waits[1:]
        arrived = swap(give, bit)
        if left.shape[0] == 1:
            return (left[0, 0], arrived[0]), got_x
        total = left[:, 0] + arrived.astype(F32)
        bit *= 2


def on_device(base, cotangent, gain, weight_in, weight_out, subspace):
    sections = lax.axis_size("section")
    here = lax.axis_index("section")
    spot = lax.axis_index("dp")
    core = spot % 2
    rows, width = base.shape
    part, size = subspace.shape
    rank = weight_in.shape[2]
    last = sections - 1
    flag = (here == last).astype(jnp.int32)
    own_in, own_out = weight_in[0], weight_out[0]
    own = call(
        own_kernel,
        [flag, spot],
        [own_in, own_out, subspace, gain],
        [],
        [((part * 5 // 2, rank), BF16)],
        [pltpu.VMEM((part, rank), BF16), pltpu.VMEM((1, part), F32), pltpu.SemaphoreType.DMA((4,))],
        62 * 1024 * 1024,
    )[0]

    peers = lax.axis_size("dp")
    order = sorted(range(4, peers, 4), key=lambda m: (m.bit_count(), m))
    shards = {0: own}
    shards[2] = swap(own, 2)
    for k, m in enumerate(order):
        if m.bit_count() == 1:
            shards[m] = swap(after(own, shards[order[k - 1]]) if k else own, m)

    shards[order[0] ^ 2] = swap(after(shards[order[0]], shards[2]), 2)
    tall = (3 * rank, size)
    keep, give = call(
        small_kernel,
        [flag, core],
        [own_out, subspace],
        [after(own, shards[order[0] ^ 2])],
        [((tall[0] // 2, size), F32)] * 2,
        [
            pltpu.VMEM((part, rank), BF16),
            pltpu.VMEM((part, size), BF16),
            pltpu.VMEM(tall, F32),
            pltpu.SemaphoreType.DMA((2,)),
        ],
        60 * 1024 * 1024,
    )
    small = keep + swap(give, 1)
    bit = 4
    while bit < peers // 2:
        small = small + swap(small, bit)
        bit *= 2

    tokens = (base, cotangent)
    ends = order[-1] ^ 2
    for k, m in enumerate(order):
        low = m & -m
        if m != low:
            shards[m] = swap(after(shards[m ^ low], shards[order[k - 2] ^ 2]), low)
        if k:
            shards[m ^ 2] = swap(after(shards[m], shards[order[k - 1] ^ 2]), 2)
    small = after(small, shards[peers // 2])
    small = small + swap(small, peers // 2)
    small = small + swap(small.astype(BF16), 2).astype(F32)
    small_other = swap(small, 1)
    keeps = [small, *from_sections(small.astype(BF16))]
    others = [small_other, *from_sections(small_other.astype(BF16))]

    marks = [m for m in range(0, peers, 2) if m != ends]
    for m in marks:
        shards[m ^ 1] = swap(shards[m], 1)
    marks += [m ^ 1 for m in marks]
    acc = project([spot ^ m for m in marks], flag, [shards[m] for m in marks], tokens)[0]
    pair = [shards[ends], swap(after(shards[ends], acc), 1)]
    acc, send = project([spot ^ ends, spot ^ ends ^ 1], flag, pair, tokens, acc, final=True)
    sent = from_sections(send)

    near = list(range(0, peers, 4))
    every = near + [m ^ 2 for m in near]
    half = part // 2
    if sections == 2:
        columns, block_id = half, lambda i: i * 2 + flag
    else:
        columns, block_id = part, lambda i: i
    both = (spot ^ 1, spot)
    out_ids = [block_id(who ^ m) for who in both for m in every]
    in_ids = [who ^ m for who in both for m in every]
    blocks = lambda n: ((len(every), rank, n), BF16)
    thin_count = 1 if sections == 2 else 2
    codes, *rest = call(
        functools.partial(chain_kernel, sections, width),
        [here, core, *out_ids, *in_ids],
        [],
        [base, cotangent, acc, *sent, *keeps, *others],
        [((rows, size), BF16)]
        + [((rank, size), F32)] * thin_count
        + [blocks(columns)] * 2
        + [blocks(part)] * 2,
        vmem_bytes=(VMEM_BYTES if sections == 2 else 32 * 1024 * 1024),
    )
    thins, chunks = rest[:thin_count], rest[thin_count:]
    got = [swap(give, 1) for give in chunks[::2]]
    sum_in, in_x = scatter_sum(got[1], chunks[3])
    sum_out, out_x = scatter_sum(got[0], chunks[1], [[in_x]])
    sum_out = sum_out[0] + sum_out[1].astype(F32)
    ends_out = [sum_out]
    if sections == 2:
        ends_out = [swap(sum_out, 1, "section"), sum_out]
    waits = [None, out_x, None]
    terms = [term for thin in thins for term in sum_thin(thin, waits)]
    grad_in, grad_out = call(
        functools.partial(end_kernel, sections),
        [flag, spot],
        [],
        [gain, subspace, *terms, *ends_out, *sum_in],
        [((part, rank), F32)] * 2,
    )
    return codes[None], grad_in[None], grad_out[None]


def solution(mesh):
    placed = (
        P("dp", None),
        P("dp", None),
        P("section", None),
        P("section", "dp", None),
        P("section", "dp", None),
        P("dp", None),
    )
    return jax.shard_map(
        on_device,
        mesh=mesh,
        in_specs=placed,
        out_specs=(P("section", "dp", None), P("section", "dp", None), P("section", "dp", None)),
        check_vma=False,
    )
```

```python
import functools

import jax
import jax.numpy as jnp
from jax import lax
from jax.experimental import pallas as pl
from jax.experimental.pallas import tpu as pltpu
from jax.sharding import PartitionSpec as P

F32 = jnp.float32
BF16 = jnp.bfloat16
VMEM_BYTES = 16 * 1024 * 1024
IN_VMEM = pl.BlockSpec(memory_space=pltpu.VMEM)
IN_SMEM = pl.BlockSpec(memory_space=pltpu.SMEM)
IN_HBM = pl.BlockSpec(memory_space=pltpu.HBM)
CONTRACT = ((1,), (0,))
ROWS = ((0,), (0,))
COLUMNS = ((1,), (1,))


def mm(a, b, dims=CONTRACT):
    return lax.dot_general(a, b, (dims, ((), ())), preferred_element_type=F32)


def parts_of(a):
    if a.dtype == BF16:
        return [a]
    high = a.astype(BF16)
    return [high, (a - high.astype(F32)).astype(BF16)]


def exact(a, b, dims=CONTRACT):
    left, right = parts_of(a), parts_of(b)
    total = mm(left[0], right[0], dims)
    for i, x in enumerate(left):
        for j, y in enumerate(right):
            if i + j == 1:
                total = total + mm(x, y, dims)
    return total


def call(kernel, scalars, far, arrays, shapes, scratch=(), vmem_bytes=VMEM_BYTES, flops=0):
    return pl.pallas_call(
        kernel,
        in_specs=[IN_SMEM] + [IN_HBM] * len(far) + [IN_VMEM] * len(arrays),
        out_specs=[IN_VMEM] * len(shapes),
        out_shape=[jax.ShapeDtypeStruct(*s) for s in shapes],
        scratch_shapes=list(scratch),
        compiler_params=pltpu.CompilerParams(vmem_limit_bytes=vmem_bytes),
        cost_estimate=pl.CostEstimate(flops=flops, bytes_accessed=0, transcendentals=0),
    )(jnp.stack(scalars).astype(jnp.int32), *far, *arrays)


def fetch(pairs, sems, first=0):
    copies = [pltpu.make_async_copy(a, b, sems.at[first + i]) for i, (a, b) in enumerate(pairs)]
    for copy in copies:
        copy.start()
    return copies


def swap(value, bits, axis="dp"):
    peers = lax.axis_size(axis)
    return lax.ppermute(value, axis, [(i, i ^ bits) for i in range(peers)])


def after(value, *others):
    return lax.optimization_barrier((value, *others))[0]


def from_sections(value):
    sections = lax.axis_size("section")
    here = lax.axis_index("section")
    if sections == 2:
        return [swap(value, 1, "section")]
    around = [(i, (i + 1) % sections) for i in range(sections)]
    held = [value]
    for _ in range(sections - 1):
        held.append(lax.ppermute(held[-1], "section", around))
    stacked = jnp.stack(held)
    order = (here - jnp.arange(sections)) % sections
    return [lax.dynamic_index_in_dim(stacked, order[s], 0, keepdims=False) for s in range(sections)]


def own_kernel(scalars, in_far, out_ref, space_ref, gain_far, own_ref, in_ref, gain_ref, sems):
    part, rank = in_ref.shape
    half = part // 2
    start = pl.multiple_of(scalars[1] * part, part)
    first = fetch([(in_far, in_ref), (gain_far.at[:, pl.ds(start, part)], gain_ref)], sems)
    places = own_ref.at[part : 2 * part], own_ref.at[2 * part :]

    def copy_both(sources):
        for copy in fetch(list(zip(sources, places)), sems, 2):
            copy.wait()

    @pl.when(scalars[0] == 1)
    def _():
        copy_both((out_ref, space_ref.at[half:, rank:]))

    @pl.when(scalars[0] == 0)
    def _():
        copy_both((space_ref.at[:, :rank], space_ref.at[:half, rank:]))

    for copy in first:
        copy.wait()
    column = jnp.broadcast_to(gain_ref[...], (rank, part)).T
    own_ref[:part] = (in_ref[...].astype(F32) * column).astype(BF16)


def small_kernel(scalars, out_far, space_far, own_ref, keep_ref, give_ref, *scratch):
    out_ref, space_ref, all_ref, sems = scratch
    is_last, core = scalars[0] == 1, scalars[1]
    part, rank = out_ref.shape
    for copy in fetch([(space_far, space_ref), (out_far, out_ref)], sems):
        copy.wait()
    space = space_ref[...]
    all_ref[:rank] = mm(out_ref[...], space, ROWS)
    all_ref[rank : 2 * rank] = mm(own_ref[:part], space, ROWS)
    columns = jnp.where(is_last, space_ref[:, rank:], space_ref[:, :rank])
    all_ref[2 * rank :] = mm(columns, space, ROWS)
    half = keep_ref.shape[0]
    first, second = all_ref[:half], all_ref[half:]
    keep_ref[...] = jnp.where(core == 0, first, second)
    give_ref[...] = jnp.where(core == 0, second, first)


def project_kernel(first, final, count, scalars, base_ref, cot_ref, *refs):
    shards, refs = refs[:count], list(refs[count:])
    acc = None if first else refs.pop(0)
    out = refs.pop(0)
    rank = out.shape[1] // 6
    part = shards[0].shape[0] * 2 // 5
    half = part // 2
    skip = scalars[count] * half
    out[...] = jnp.zeros_like(out) if first else acc[...]
    for t, shard in enumerate(shards):
        start = pl.multiple_of(scalars[t] * part, part)
        half_start = pl.multiple_of(start + skip, half)
        tokens = base_ref[:, pl.ds(start, part)]
        tokens_f = tokens.astype(F32)
        square = tokens_f * tokens_f
        total = square[:, :rank]
        for at in range(rank, part, rank):
            total = total + square[:, at : at + rank]
        wide = jnp.concatenate([shard[:part], shard[part : 2 * part]], axis=1)
        out[:, : 2 * rank] += mm(tokens, wide)
        out[:, 2 * rank : 3 * rank] += mm(base_ref[:, pl.ds(half_start, half)], shard[2 * part :])
        out[:, 3 * rank : 4 * rank] += mm(cot_ref[:, pl.ds(start, part)], shard[part : 2 * part])
        out[:, 4 * rank : 5 * rank] += mm(cot_ref[:, pl.ds(half_start, half)], shard[2 * part :])
        out[:, 5 * rank :] += total
    if final:
        refs[0][...] = out[:, : 5 * rank].astype(BF16)


def project(ids, flag, shards, tokens, acc=None, final=False):
    tall, rank = shards[0].shape
    rows, count = tokens[0].shape[0], len(ids)
    shapes = [((rows, 6 * rank), F32)]
    if final:
        shapes.append(((rows, 5 * rank), BF16))
    return call(
        functools.partial(project_kernel, acc is None, final, count),
        [*ids, flag],
        [],
        [*tokens, *shards] + ([] if acc is None else [acc]),
        shapes,
        flops=4 * rows * tall * rank * count,
    )


def outer_into(scalars, at, small, tokens_ref, outs):
    for out in outs:
        count, _, columns = out.shape
        for j in range(count):
            start = pl.multiple_of(scalars[at] * columns, columns)
            out[j] = mm(small, tokens_ref[:, pl.ds(start, columns)]).astype(BF16)
            at += 1


def small_parts(sections, here, core, keeps, others, s):
    value = lambda refs: (
        jnp.where(here == s, refs[0][...], refs[1][...].astype(F32))
        if sections == 2
        else refs[1 + s][...].astype(F32)
    )
    mine, theirs = value(keeps), value(others)
    whole = jnp.concatenate(
        [jnp.where(core == 0, mine, theirs), jnp.where(core == 0, theirs, mine)]
    )
    rank = whole.shape[0] // 3
    return whole[:rank], whole[rank : 2 * rank], whole[2 * rank :]


def chain_kernel(sections, width, scalars, base_ref, cot_ref, own, *refs):
    here, core = scalars[0], scalars[1]
    n = 1 if sections == 2 else sections
    thin_count = 1 if sections == 2 else 2
    refs = list(refs)
    take = lambda count: [refs.pop(0) for _ in range(count)]
    sent, keeps, others = take(n), take(n + 1), take(n + 1)
    codes_ref, thin_refs = take(1)[0], take(thin_count)
    outs_c, outs_b = take(2), take(2)
    rank = own.shape[1] // 6
    last = sections - 1
    values = [
        jnp.where(
            here == s, own[:, : 5 * rank], sent[0 if sections == 2 else s][...].astype(F32)
        )
        for s in range(sections)
    ]
    column = lambda s, k: values[s][:, k * rank : (k + 1) * rank]
    spread = lambda k: jnp.concatenate(
        [column(0, k), column(0, k + 1) + column(last, k + 1)], axis=1
    )
    base_s = spread(1)
    square = jnp.sum(own[:, 5 * rank :], axis=1, keepdims=True)
    smalls = [small_parts(sections, here, core, keeps, others, s) for s in range(sections)]
    gram = jnp.concatenate([smalls[0][2], smalls[last][2]])
    choose = lambda s, value, other: value if other is None else jnp.where(here == s, value, other)
    state = []
    code = mine_code = None
    for s in range(sections):
        m_s, q_t, _ = smalls[s]
        inner, total, resid_s, before = column(s, 0), square, base_s, code
        if s:
            moved = exact(code, gram)
            total = square + jnp.sum(
                (2.0 * base_s + moved) * code.astype(F32), axis=1, keepdims=True
            )
            inner = inner + exact(code, q_t, COLUMNS)
            resid_s = base_s + moved
        inverse = lax.rsqrt(jnp.maximum(total, 0.0) * (1.0 / width) + 1e-05)
        inner = inner * inverse
        logistic = 1.0 / (1.0 + jnp.exp(-inner))
        active = inner * logistic
        grown = exact(active, m_s)
        code = (moved + grown if s else grown).astype(BF16)
        mine_code = choose(s, code, mine_code)
        state.append((m_s, q_t, inner, logistic, inverse, active, resid_s, before))
    codes_ref[...] = mine_code
    active_t = state[last][5].T.astype(BF16)
    outer_into(scalars, 2, active_t, cot_ref, outs_c)

    grad_active, grad_y = column(last, 3), spread(3)
    mine = thin_in = thin_out = None
    for s in range(last, -1, -1):
        m_s, q_t, inner, logistic, inverse, active, resid_s, before = state[s]
        if s < last:
            grad_active = exact(back, m_s, COLUMNS)
            grad_y = exact(back, gram) if s else None
            thin_out = choose(s, mm(active.T.astype(BF16), back), thin_out)
        grad_inner = grad_active * logistic * (1.0 + inner * (1.0 - logistic))
        scaled = inverse * grad_inner
        scaled_t = scaled.T.astype(BF16)
        scaled = scaled.astype(BF16)
        mine = choose(s, scaled_t, mine)
        if s:
            thin_in = choose(s, mm(scaled_t, before), thin_in)
            along = jnp.sum(inner * grad_inner, axis=1, keepdims=True)
            along = along * (inverse * inverse * (1.0 / width))
            back = (grad_y + exact(scaled, q_t) - resid_s * along).astype(BF16)
    if sections == 2:
        thin_refs[0][...] = jnp.where(here == last, thin_in, thin_out)
    else:
        thin_refs[0][...] = jnp.where(here == 0, 0.0, thin_in)
        thin_refs[1][...] = thin_out
    outer_into(scalars, 2 + 2 * outs_c[0].shape[0], mine, base_ref, outs_b)


def end_kernel(sections, scalars, gain_ref, space_ref, *refs):
    is_last = scalars[0] == 1
    part = space_ref.shape[0]
    grad_in, grad_out = refs[-2:]
    refs = list(refs[:-2])
    pair = lambda: refs.pop(0)[...].astype(F32) + refs.pop(0)[...].astype(F32)
    thin_in = pair()
    thin_out = thin_in if sections == 2 else pair()
    space = space_ref[...]
    lift_in = exact(thin_in, space, COLUMNS)
    lift_out = lift_in if sections == 2 else exact(thin_out, space, COLUMNS)
    if sections == 2:
        lift_in = jnp.where(is_last, lift_in, 0.0)
        half_first, half_second = refs.pop(0)[...], refs.pop(0)[...]
        sum_out = jnp.concatenate([half_first, half_second], axis=1)
    else:
        sum_out = refs.pop(0)[...]
    sum_in = pair()
    start = pl.multiple_of(scalars[1] * part, part)
    total = gain_ref[:, pl.ds(start, part)] * (sum_in + lift_in)
    grad_in[...] = total.T
    grad_out[...] = jnp.where(is_last, sum_out, lift_out).T


def sum_thin(value, waits):
    peers = lax.axis_size("dp")
    bit, step = 1, 0
    while bit < peers:
        if step:
            wait = waits[min(step, len(waits)) - 1]
            value = value + got if wait is None else after(value + got, wait)
        got = swap(value, bit)
        bit, step = bit * 2, step + 1
    return value, got


def scatter_sum(got, keep, waits=()):
    half = got.shape[0] // 2
    summed = (keep[half:].astype(F32) + got[half:].astype(F32)).astype(BF16)
    got_x = swap(summed, 2)
    total = keep[:half].astype(F32) + got[:half].astype(F32) + got_x.astype(F32)
    bit = 4
    while True:
        left = total.reshape((total.shape[0] // 2, 2) + total.shape[1:])
        give = left[:, 1].astype(BF16)
        if waits:
            give = after(give, *waits[0])
            waits = waits[1:]
        arrived = swap(give, bit)
        if left.shape[0] == 1:
            return (left[0, 0], arrived[0]), got_x, total
        total = left[:, 0] + arrived.astype(F32)
        bit *= 2


def on_device(base, cotangent, gain, weight_in, weight_out, subspace):
    sections = lax.axis_size("section")
    here = lax.axis_index("section")
    spot = lax.axis_index("dp")
    core = spot % 2
    rows, width = base.shape
    part, size = subspace.shape
    rank = weight_in.shape[2]
    last = sections - 1
    flag = (here == last).astype(jnp.int32)
    own_in, own_out = weight_in[0], weight_out[0]
    own = call(
        own_kernel,
        [flag, spot],
        [own_in, own_out, subspace, gain],
        [],
        [((part * 5 // 2, rank), BF16)],
        [pltpu.VMEM((part, rank), BF16), pltpu.VMEM((1, part), F32), pltpu.SemaphoreType.DMA((4,))],
        62 * 1024 * 1024,
    )[0]

    peers = lax.axis_size("dp")
    order = sorted(range(4, peers, 4), key=lambda m: (m.bit_count(), m))
    shards = {0: own}
    shards[2] = swap(own, 2)
    for k, m in enumerate(order):
        if m.bit_count() == 1:
            shards[m] = swap(after(own, shards[order[k - 1]]) if k else own, m)

    shards[order[0] ^ 2] = swap(after(shards[order[0]], shards[2]), 2)
    tall = (3 * rank, size)
    keep, give = call(
        small_kernel,
        [flag, core],
        [own_out, subspace],
        [after(own, shards[order[0] ^ 2])],
        [((tall[0] // 2, size), F32)] * 2,
        [
            pltpu.VMEM((part, rank), BF16),
            pltpu.VMEM((part, size), BF16),
            pltpu.VMEM(tall, F32),
            pltpu.SemaphoreType.DMA((2,)),
        ],
        60 * 1024 * 1024,
    )
    small = keep + swap(give, 1)
    bit = 4
    while bit < peers // 2:
        small = small + swap(small, bit)
        bit *= 2

    tokens = (base, cotangent)
    ends = order[-1] ^ 2
    for k, m in enumerate(order):
        low = m & -m
        if m != low:
            shards[m] = swap(after(shards[m ^ low], shards[order[k - 2] ^ 2]), low)
        if k:
            shards[m ^ 2] = swap(after(shards[m], shards[order[k - 1] ^ 2]), 2)
    small = after(small, shards[peers // 2])
    small = small + swap(small, peers // 2)
    small = small + swap(small.astype(BF16), 2).astype(F32)
    small_other = swap(small, 1)
    keeps = [small, *from_sections(small.astype(BF16))]
    others = [small_other, *from_sections(small_other.astype(BF16))]

    marks = [m for m in range(0, peers, 2) if m != ends]
    for m in marks:
        shards[m ^ 1] = swap(shards[m], 1)
    marks += [m ^ 1 for m in marks]
    acc = project([spot ^ m for m in marks], flag, [shards[m] for m in marks], tokens)[0]
    pair = [shards[ends], swap(after(shards[ends], acc), 1)]
    acc, send = project([spot ^ ends, spot ^ ends ^ 1], flag, pair, tokens, acc, final=True)
    sent = from_sections(send)

    near = list(range(0, peers, 4))
    every = near + [m ^ 2 for m in near]
    half = part // 2
    if sections == 2:
        columns, block_id = half, lambda i: i * 2 + flag
    else:
        columns, block_id = part, lambda i: i
    both = (spot ^ 1, spot)
    out_ids = [block_id(who ^ m) for who in both for m in every]
    in_ids = [who ^ m for who in both for m in every]
    blocks = lambda n: ((len(every), rank, n), BF16)
    thin_count = 1 if sections == 2 else 2
    codes, *rest = call(
        functools.partial(chain_kernel, sections, width),
        [here, core, *out_ids, *in_ids],
        [],
        [base, cotangent, acc, *sent, *keeps, *others],
        [((rows, size), BF16)]
        + [((rank, size), F32)] * thin_count
        + [blocks(columns)] * 2
        + [blocks(part)] * 2,
        vmem_bytes=(VMEM_BYTES if sections == 2 else 32 * 1024 * 1024),
    )
    thins, chunks = rest[:thin_count], rest[thin_count:]
    got = [swap(give, 1) for give in chunks[::2]]
    sum_in, in_x, in_near = scatter_sum(got[1], chunks[3])
    sum_out, out_x, _ = scatter_sum(got[0], chunks[1], [[in_x], [in_near]])
    sum_out = sum_out[0] + sum_out[1].astype(F32)
    ends_out = [sum_out]
    if sections == 2:
        ends_out = [swap(sum_out, 1, "section"), sum_out]
    waits = [got[1], out_x, None]
    terms = [term for thin in thins for term in sum_thin(thin, waits)]
    grad_in, grad_out = call(
        functools.partial(end_kernel, sections),
        [flag, spot],
        [],
        [gain, subspace, *terms, *ends_out, *sum_in],
        [((part, rank), F32)] * 2,
    )
    return codes[None], grad_in[None], grad_out[None]


def solution(mesh):
    placed = (
        P("dp", None),
        P("dp", None),
        P("section", None),
        P("section", "dp", None),
        P("section", "dp", None),
        P("dp", None),
    )
    return jax.shard_map(
        on_device,
        mesh=mesh,
        in_specs=placed,
        out_specs=(P("section", "dp", None), P("section", "dp", None), P("section", "dp", None)),
        check_vma=False,
    )
```

```python
import functools

import jax
import jax.numpy as jnp
from jax import lax
from jax.experimental import pallas as pl
from jax.experimental.pallas import tpu as pltpu
from jax.sharding import PartitionSpec as P

F32 = jnp.float32
BF16 = jnp.bfloat16
VMEM_BYTES = 16 * 1024 * 1024
IN_VMEM = pl.BlockSpec(memory_space=pltpu.VMEM)
IN_SMEM = pl.BlockSpec(memory_space=pltpu.SMEM)
IN_HBM = pl.BlockSpec(memory_space=pltpu.HBM)
CONTRACT = ((1,), (0,))
ROWS = ((0,), (0,))
COLUMNS = ((1,), (1,))


def mm(a, b, dims=CONTRACT):
    return lax.dot_general(a, b, (dims, ((), ())), preferred_element_type=F32)


def parts_of(a):
    if a.dtype == BF16:
        return [a]
    high = a.astype(BF16)
    return [high, (a - high.astype(F32)).astype(BF16)]


def exact(a, b, dims=CONTRACT):
    left, right = parts_of(a), parts_of(b)
    total = mm(left[0], right[0], dims)
    for i, x in enumerate(left):
        for j, y in enumerate(right):
            if i + j == 1:
                total = total + mm(x, y, dims)
    return total


def call(kernel, scalars, far, arrays, shapes, scratch=(), vmem_bytes=VMEM_BYTES, flops=0):
    return pl.pallas_call(
        kernel,
        in_specs=[IN_SMEM] + [IN_HBM] * len(far) + [IN_VMEM] * len(arrays),
        out_specs=[IN_VMEM] * len(shapes),
        out_shape=[jax.ShapeDtypeStruct(*s) for s in shapes],
        scratch_shapes=list(scratch),
        compiler_params=pltpu.CompilerParams(vmem_limit_bytes=vmem_bytes),
        cost_estimate=pl.CostEstimate(flops=flops, bytes_accessed=0, transcendentals=0),
    )(jnp.stack(scalars).astype(jnp.int32), *far, *arrays)


def fetch(pairs, sems, first=0):
    copies = [pltpu.make_async_copy(a, b, sems.at[first + i]) for i, (a, b) in enumerate(pairs)]
    for copy in copies:
        copy.start()
    return copies


def swap(value, bits, axis="dp"):
    peers = lax.axis_size(axis)
    return lax.ppermute(value, axis, [(i, i ^ bits) for i in range(peers)])


def after(value, *others):
    return lax.optimization_barrier((value, *others))[0]


def from_sections(value):
    sections = lax.axis_size("section")
    here = lax.axis_index("section")
    if sections == 2:
        return [swap(value, 1, "section")]
    around = [(i, (i + 1) % sections) for i in range(sections)]
    held = [value]
    for _ in range(sections - 1):
        held.append(lax.ppermute(held[-1], "section", around))
    stacked = jnp.stack(held)
    order = (here - jnp.arange(sections)) % sections
    return [lax.dynamic_index_in_dim(stacked, order[s], 0, keepdims=False) for s in range(sections)]


def own_kernel(scalars, in_far, out_ref, space_ref, gain_far, own_ref, in_ref, gain_ref, sems):
    part, rank = in_ref.shape
    half = part // 2
    start = pl.multiple_of(scalars[1] * part, part)
    first = fetch([(in_far, in_ref), (gain_far.at[:, pl.ds(start, part)], gain_ref)], sems)
    places = own_ref.at[part : 2 * part], own_ref.at[2 * part :]

    def copy_both(sources):
        for copy in fetch(list(zip(sources, places)), sems, 2):
            copy.wait()

    @pl.when(scalars[0] == 1)
    def _():
        copy_both((out_ref, space_ref.at[half:, rank:]))

    @pl.when(scalars[0] == 0)
    def _():
        copy_both((space_ref.at[:, :rank], space_ref.at[:half, rank:]))

    for copy in first:
        copy.wait()
    column = jnp.broadcast_to(gain_ref[...], (rank, part)).T
    own_ref[:part] = (in_ref[...].astype(F32) * column).astype(BF16)


def small_kernel(scalars, out_far, space_far, own_ref, keep_ref, give_ref, *scratch):
    out_ref, space_ref, all_ref, sems = scratch
    is_last, core = scalars[0] == 1, scalars[1]
    part, rank = out_ref.shape
    for copy in fetch([(space_far, space_ref), (out_far, out_ref)], sems):
        copy.wait()
    space = space_ref[...]
    all_ref[:rank] = mm(out_ref[...], space, ROWS)
    all_ref[rank : 2 * rank] = mm(own_ref[:part], space, ROWS)
    columns = jnp.where(is_last, space_ref[:, rank:], space_ref[:, :rank])
    all_ref[2 * rank :] = mm(columns, space, ROWS)
    half = keep_ref.shape[0]
    first, second = all_ref[:half], all_ref[half:]
    keep_ref[...] = jnp.where(core == 0, first, second)
    give_ref[...] = jnp.where(core == 0, second, first)


def project_kernel(first, final, count, scalars, base_ref, cot_ref, *refs):
    shards, refs = refs[:count], list(refs[count:])
    acc = None if first else refs.pop(0)
    out = refs.pop(0)
    rank = out.shape[1] // 6
    part = shards[0].shape[0] * 2 // 5
    half = part // 2
    skip = scalars[count] * half
    out[...] = jnp.zeros_like(out) if first else acc[...]
    for t, shard in enumerate(shards):
        start = pl.multiple_of(scalars[t] * part, part)
        half_start = pl.multiple_of(start + skip, half)
        tokens = base_ref[:, pl.ds(start, part)]
        tokens_f = tokens.astype(F32)
        square = tokens_f * tokens_f
        total = square[:, :rank]
        for at in range(rank, part, rank):
            total = total + square[:, at : at + rank]
        wide = jnp.concatenate([shard[:part], shard[part : 2 * part]], axis=1)
        out[:, : 2 * rank] += mm(tokens, wide)
        out[:, 2 * rank : 3 * rank] += mm(base_ref[:, pl.ds(half_start, half)], shard[2 * part :])
        out[:, 3 * rank : 4 * rank] += mm(cot_ref[:, pl.ds(start, part)], shard[part : 2 * part])
        out[:, 4 * rank : 5 * rank] += mm(cot_ref[:, pl.ds(half_start, half)], shard[2 * part :])
        out[:, 5 * rank :] += total
    if final:
        refs[0][...] = out[:, : 5 * rank].astype(BF16)


def project(ids, flag, shards, tokens, acc=None, final=False):
    tall, rank = shards[0].shape
    rows, count = tokens[0].shape[0], len(ids)
    shapes = [((rows, 6 * rank), F32)]
    if final:
        shapes.append(((rows, 5 * rank), BF16))
    return call(
        functools.partial(project_kernel, acc is None, final, count),
        [*ids, flag],
        [],
        [*tokens, *shards] + ([] if acc is None else [acc]),
        shapes,
        flops=4 * rows * tall * rank * count,
    )


def outer_into(scalars, at, small, tokens_ref, outs):
    for out in outs:
        count, _, columns = out.shape
        for j in range(count):
            start = pl.multiple_of(scalars[at] * columns, columns)
            out[j] = mm(small, tokens_ref[:, pl.ds(start, columns)]).astype(BF16)
            at += 1


def small_parts(sections, here, core, keeps, others, s):
    value = lambda refs: (
        jnp.where(here == s, refs[0][...], refs[1][...].astype(F32))
        if sections == 2
        else refs[1 + s][...].astype(F32)
    )
    mine, theirs = value(keeps), value(others)
    whole = jnp.concatenate(
        [jnp.where(core == 0, mine, theirs), jnp.where(core == 0, theirs, mine)]
    )
    rank = whole.shape[0] // 3
    return whole[:rank], whole[rank : 2 * rank], whole[2 * rank :]


def chain_kernel(sections, width, scalars, base_ref, cot_ref, own, *refs):
    here, core = scalars[0], scalars[1]
    n = 1 if sections == 2 else sections
    thin_count = 1 if sections == 2 else 2
    refs = list(refs)
    take = lambda count: [refs.pop(0) for _ in range(count)]
    sent, keeps, others = take(n), take(n + 1), take(n + 1)
    codes_ref, thin_refs = take(1)[0], take(thin_count)
    outs_c, outs_b = take(2), take(2)
    rank = own.shape[1] // 6
    last = sections - 1
    values = [
        jnp.where(
            here == s, own[:, : 5 * rank], sent[0 if sections == 2 else s][...].astype(F32)
        )
        for s in range(sections)
    ]
    column = lambda s, k: values[s][:, k * rank : (k + 1) * rank]
    spread = lambda k: jnp.concatenate(
        [column(0, k), column(0, k + 1) + column(last, k + 1)], axis=1
    )
    base_s = spread(1)
    square = jnp.sum(own[:, 5 * rank :], axis=1, keepdims=True)
    smalls = [small_parts(sections, here, core, keeps, others, s) for s in range(sections)]
    gram = jnp.concatenate([smalls[0][2], smalls[last][2]])
    choose = lambda s, value, other: value if other is None else jnp.where(here == s, value, other)
    state = []
    code = mine_code = None
    for s in range(sections):
        m_s, q_t, _ = smalls[s]
        inner, total, resid_s, before = column(s, 0), square, base_s, code
        if s:
            moved = exact(code, gram)
            total = square + jnp.sum(
                (2.0 * base_s + moved) * code.astype(F32), axis=1, keepdims=True
            )
            inner = inner + exact(code, q_t, COLUMNS)
            resid_s = base_s + moved
        inverse = lax.rsqrt(jnp.maximum(total, 0.0) * (1.0 / width) + 1e-05)
        inner = inner * inverse
        logistic = 1.0 / (1.0 + jnp.exp(-inner))
        active = inner * logistic
        grown = exact(active, m_s)
        code = (moved + grown if s else grown).astype(BF16)
        mine_code = choose(s, code, mine_code)
        state.append((m_s, q_t, inner, logistic, inverse, active, resid_s, before))
    codes_ref[...] = mine_code
    active_t = state[last][5].T.astype(BF16)
    outer_into(scalars, 2, active_t, cot_ref, outs_c)

    grad_active, grad_y = column(last, 3), spread(3)
    mine = thin_in = thin_out = None
    for s in range(last, -1, -1):
        m_s, q_t, inner, logistic, inverse, active, resid_s, before = state[s]
        if s < last:
            grad_active = exact(back, m_s, COLUMNS)
            grad_y = exact(back, gram) if s else None
            thin_out = choose(s, mm(active.T.astype(BF16), back), thin_out)
        grad_inner = grad_active * logistic * (1.0 + inner * (1.0 - logistic))
        scaled = inverse * grad_inner
        scaled_t = scaled.T.astype(BF16)
        scaled = scaled.astype(BF16)
        mine = choose(s, scaled_t, mine)
        if s:
            thin_in = choose(s, mm(scaled_t, before), thin_in)
            along = jnp.sum(inner * grad_inner, axis=1, keepdims=True)
            along = along * (inverse * inverse * (1.0 / width))
            back = (grad_y + exact(scaled, q_t) - resid_s * along).astype(BF16)
    if sections == 2:
        thin_refs[0][...] = jnp.where(here == last, thin_in, thin_out)
    else:
        thin_refs[0][...] = jnp.where(here == 0, 0.0, thin_in)
        thin_refs[1][...] = thin_out
    outer_into(scalars, 2 + 2 * outs_c[0].shape[0], mine, base_ref, outs_b)


def end_kernel(sections, scalars, gain_ref, space_ref, *refs):
    is_last = scalars[0] == 1
    part = space_ref.shape[0]
    grad_in, grad_out = refs[-2:]
    refs = list(refs[:-2])
    pair = lambda: refs.pop(0)[...].astype(F32) + refs.pop(0)[...].astype(F32)
    thin_in = pair()
    thin_out = thin_in if sections == 2 else pair()
    space = space_ref[...]
    lift_in = exact(thin_in, space, COLUMNS)
    lift_out = lift_in if sections == 2 else exact(thin_out, space, COLUMNS)
    if sections == 2:
        lift_in = jnp.where(is_last, lift_in, 0.0)
        half_first, half_second = refs.pop(0)[...], refs.pop(0)[...]
        sum_out = jnp.concatenate([half_first, half_second], axis=1)
    else:
        sum_out = refs.pop(0)[...]
    sum_in = pair()
    start = pl.multiple_of(scalars[1] * part, part)
    total = gain_ref[:, pl.ds(start, part)] * (sum_in + lift_in)
    grad_in[...] = total.T
    grad_out[...] = jnp.where(is_last, sum_out, lift_out).T


def sum_thin(value, waits):
    peers = lax.axis_size("dp")
    bit, step = 1, 0
    while bit < peers:
        if step:
            wait = waits[min(step, len(waits)) - 1]
            value = value + got if wait is None else after(value + got, wait)
        got = swap(value, bit)
        bit, step = bit * 2, step + 1
    return value, got


def scatter_sum(got, keep, waits=()):
    half = got.shape[0] // 2
    summed = (keep[half:].astype(F32) + got[half:].astype(F32)).astype(BF16)
    got_x = swap(summed, 2)
    total = keep[:half].astype(F32) + got[:half].astype(F32) + got_x.astype(F32)
    bit = 4
    while True:
        left = total.reshape((total.shape[0] // 2, 2) + total.shape[1:])
        give = left[:, 1].astype(BF16)
        if waits:
            give = after(give, *waits[0])
            waits = waits[1:]
        arrived = swap(give, bit)
        if left.shape[0] == 1:
            return (left[0, 0], arrived[0]), got_x
        total = left[:, 0] + arrived.astype(F32)
        bit *= 2


def on_device(base, cotangent, gain, weight_in, weight_out, subspace):
    sections = lax.axis_size("section")
    here = lax.axis_index("section")
    spot = lax.axis_index("dp")
    core = spot % 2
    rows, width = base.shape
    part, size = subspace.shape
    rank = weight_in.shape[2]
    last = sections - 1
    flag = (here == last).astype(jnp.int32)
    own_in, own_out = weight_in[0], weight_out[0]
    own = call(
        own_kernel,
        [flag, spot],
        [own_in, own_out, subspace, gain],
        [],
        [((part * 5 // 2, rank), BF16)],
        [pltpu.VMEM((part, rank), BF16), pltpu.VMEM((1, part), F32), pltpu.SemaphoreType.DMA((4,))],
        62 * 1024 * 1024,
    )[0]

    peers = lax.axis_size("dp")
    order = sorted(range(4, peers, 4), key=lambda m: (m.bit_count(), m))
    shards = {0: own}
    shards[2] = swap(own, 2)
    for k, m in enumerate(order):
        if m.bit_count() == 1:
            shards[m] = swap(after(own, shards[order[k - 1]]) if k else own, m)

    shards[order[0] ^ 2] = swap(after(shards[order[0]], shards[2]), 2)
    tall = (3 * rank, size)
    keep, give = call(
        small_kernel,
        [flag, core],
        [own_out, subspace],
        [after(own, shards[order[0] ^ 2])],
        [((tall[0] // 2, size), F32)] * 2,
        [
            pltpu.VMEM((part, rank), BF16),
            pltpu.VMEM((part, size), BF16),
            pltpu.VMEM(tall, F32),
            pltpu.SemaphoreType.DMA((2,)),
        ],
        60 * 1024 * 1024,
    )
    small = keep + swap(give, 1)
    bit = 4
    while bit < peers // 2:
        small = small + swap(small, bit)
        bit *= 2

    tokens = (base, cotangent)
    ends = order[-1] ^ 2
    for k, m in enumerate(order):
        low = m & -m
        if m != low:
            shards[m] = swap(after(shards[m ^ low], shards[order[k - 2] ^ 2]), low)
        if k:
            ties = [small] if m ^ 2 == ends else []
            shards[m ^ 2] = swap(after(shards[m], shards[order[k - 1] ^ 2], *ties), 2)
    small = after(small, shards[peers // 2])
    small = small + swap(small, peers // 2)
    small = small + swap(small.astype(BF16), 2).astype(F32)
    small_other = swap(small, 1)
    keeps = [small, *from_sections(small.astype(BF16))]
    others = [small_other, *from_sections(small_other.astype(BF16))]

    marks = [m for m in range(0, peers, 2) if m != ends]
    for m in marks:
        shards[m ^ 1] = swap(shards[m], 1)
    marks += [m ^ 1 for m in marks]
    acc = project([spot ^ m for m in marks], flag, [shards[m] for m in marks], tokens)[0]
    pair = [shards[ends], swap(after(shards[ends], acc), 1)]
    acc, send = project([spot ^ ends, spot ^ ends ^ 1], flag, pair, tokens, acc, final=True)
    sent = from_sections(send)

    near = list(range(0, peers, 4))
    every = near + [m ^ 2 for m in near]
    half = part // 2
    if sections == 2:
        columns, block_id = half, lambda i: i * 2 + flag
    else:
        columns, block_id = part, lambda i: i
    both = (spot ^ 1, spot)
    out_ids = [block_id(who ^ m) for who in both for m in every]
    in_ids = [who ^ m for who in both for m in every]
    blocks = lambda n: ((len(every), rank, n), BF16)
    thin_count = 1 if sections == 2 else 2
    codes, *rest = call(
        functools.partial(chain_kernel, sections, width),
        [here, core, *out_ids, *in_ids],
        [],
        [base, cotangent, acc, *sent, *keeps, *others],
        [((rows, size), BF16)]
        + [((rank, size), F32)] * thin_count
        + [blocks(columns)] * 2
        + [blocks(part)] * 2,
        vmem_bytes=(VMEM_BYTES if sections == 2 else 32 * 1024 * 1024),
    )
    thins, chunks = rest[:thin_count], rest[thin_count:]
    got = [swap(give, 1) for give in chunks[::2]]
    sum_out, out_x = scatter_sum(got[0], chunks[1])
    sum_in, in_x = scatter_sum(got[1], chunks[3])
    sum_out = sum_out[0] + sum_out[1].astype(F32)
    ends_out = [sum_out]
    if sections == 2:
        ends_out = [swap(sum_out, 1, "section"), sum_out]
    waits = [got[1], out_x, None]
    terms = [term for thin in thins for term in sum_thin(thin, waits)]
    grad_in, grad_out = call(
        functools.partial(end_kernel, sections),
        [flag, spot],
        [],
        [gain, subspace, *terms, *ends_out, *sum_in],
        [((part, rank), F32)] * 2,
    )
    return codes[None], grad_in[None], grad_out[None]


def solution(mesh):
    placed = (
        P("dp", None),
        P("dp", None),
        P("section", None),
        P("section", "dp", None),
        P("section", "dp", None),
        P("dp", None),
    )
    return jax.shard_map(
        on_device,
        mesh=mesh,
        in_specs=placed,
        out_specs=(P("section", "dp", None), P("section", "dp", None), P("section", "dp", None)),
        check_vma=False,
    )
```

```python
import functools

import jax
import jax.numpy as jnp
from jax import lax
from jax.experimental import pallas as pl
from jax.experimental.pallas import tpu as pltpu
from jax.sharding import PartitionSpec as P

F32 = jnp.float32
BF16 = jnp.bfloat16
VMEM_BYTES = 16 * 1024 * 1024
IN_VMEM = pl.BlockSpec(memory_space=pltpu.VMEM)
IN_SMEM = pl.BlockSpec(memory_space=pltpu.SMEM)
IN_HBM = pl.BlockSpec(memory_space=pltpu.HBM)
CONTRACT = ((1,), (0,))
ROWS = ((0,), (0,))
COLUMNS = ((1,), (1,))


def mm(a, b, dims=CONTRACT):
    return lax.dot_general(a, b, (dims, ((), ())), preferred_element_type=F32)


def parts_of(a):
    if a.dtype == BF16:
        return [a]
    high = a.astype(BF16)
    return [high, (a - high.astype(F32)).astype(BF16)]


def exact(a, b, dims=CONTRACT):
    left, right = parts_of(a), parts_of(b)
    total = mm(left[0], right[0], dims)
    for i, x in enumerate(left):
        for j, y in enumerate(right):
            if i + j == 1:
                total = total + mm(x, y, dims)
    return total


def call(kernel, scalars, far, arrays, shapes, scratch=(), vmem_bytes=VMEM_BYTES, flops=0):
    return pl.pallas_call(
        kernel,
        in_specs=[IN_SMEM] + [IN_HBM] * len(far) + [IN_VMEM] * len(arrays),
        out_specs=[IN_VMEM] * len(shapes),
        out_shape=[jax.ShapeDtypeStruct(*s) for s in shapes],
        scratch_shapes=list(scratch),
        compiler_params=pltpu.CompilerParams(vmem_limit_bytes=vmem_bytes),
        cost_estimate=pl.CostEstimate(flops=flops, bytes_accessed=0, transcendentals=0),
    )(jnp.stack(scalars).astype(jnp.int32), *far, *arrays)


def fetch(pairs, sems, first=0):
    copies = [pltpu.make_async_copy(a, b, sems.at[first + i]) for i, (a, b) in enumerate(pairs)]
    for copy in copies:
        copy.start()
    return copies


def swap(value, bits, axis="dp"):
    peers = lax.axis_size(axis)
    return lax.ppermute(value, axis, [(i, i ^ bits) for i in range(peers)])


def after(value, *others):
    return lax.optimization_barrier((value, *others))[0]


def from_sections(value):
    sections = lax.axis_size("section")
    here = lax.axis_index("section")
    if sections == 2:
        return [swap(value, 1, "section")]
    around = [(i, (i + 1) % sections) for i in range(sections)]
    held = [value]
    for _ in range(sections - 1):
        held.append(lax.ppermute(held[-1], "section", around))
    stacked = jnp.stack(held)
    order = (here - jnp.arange(sections)) % sections
    return [lax.dynamic_index_in_dim(stacked, order[s], 0, keepdims=False) for s in range(sections)]


def own_kernel(scalars, in_far, out_ref, space_ref, gain_far, own_ref, in_ref, gain_ref, sems):
    part, rank = in_ref.shape
    half = part // 2
    start = pl.multiple_of(scalars[1] * part, part)
    first = fetch([(in_far, in_ref), (gain_far.at[:, pl.ds(start, part)], gain_ref)], sems)
    places = own_ref.at[part : 2 * part], own_ref.at[2 * part :]

    def copy_both(sources):
        for copy in fetch(list(zip(sources, places)), sems, 2):
            copy.wait()

    @pl.when(scalars[0] == 1)
    def _():
        copy_both((out_ref, space_ref.at[half:, rank:]))

    @pl.when(scalars[0] == 0)
    def _():
        copy_both((space_ref.at[:, :rank], space_ref.at[:half, rank:]))

    for copy in first:
        copy.wait()
    column = jnp.broadcast_to(gain_ref[...], (rank, part)).T
    own_ref[:part] = (in_ref[...].astype(F32) * column).astype(BF16)


def small_kernel(scalars, out_far, space_far, own_ref, keep_ref, give_ref, *scratch):
    out_ref, space_ref, all_ref, sems = scratch
    is_last, core = scalars[0] == 1, scalars[1]
    part, rank = out_ref.shape
    for copy in fetch([(space_far, space_ref), (out_far, out_ref)], sems):
        copy.wait()
    space = space_ref[...]
    all_ref[:rank] = mm(out_ref[...], space, ROWS)
    all_ref[rank : 2 * rank] = mm(own_ref[:part], space, ROWS)
    columns = jnp.where(is_last, space_ref[:, rank:], space_ref[:, :rank])
    all_ref[2 * rank :] = mm(columns, space, ROWS)
    half = keep_ref.shape[0]
    first, second = all_ref[:half], all_ref[half:]
    keep_ref[...] = jnp.where(core == 0, first, second)
    give_ref[...] = jnp.where(core == 0, second, first)


def project_kernel(first, final, count, scalars, base_ref, cot_ref, *refs):
    shards, refs = refs[:count], list(refs[count:])
    acc = None if first else refs.pop(0)
    out = refs.pop(0)
    rank = out.shape[1] // 6
    part = shards[0].shape[0] * 2 // 5
    half = part // 2
    skip = scalars[count] * half
    out[...] = jnp.zeros_like(out) if first else acc[...]
    for t, shard in enumerate(shards):
        start = pl.multiple_of(scalars[t] * part, part)
        half_start = pl.multiple_of(start + skip, half)
        tokens = base_ref[:, pl.ds(start, part)]
        tokens_f = tokens.astype(F32)
        square = tokens_f * tokens_f
        total = square[:, :rank]
        for at in range(rank, part, rank):
            total = total + square[:, at : at + rank]
        wide = jnp.concatenate([shard[:part], shard[part : 2 * part]], axis=1)
        out[:, : 2 * rank] += mm(tokens, wide)
        out[:, 2 * rank : 3 * rank] += mm(base_ref[:, pl.ds(half_start, half)], shard[2 * part :])
        out[:, 3 * rank : 4 * rank] += mm(cot_ref[:, pl.ds(start, part)], shard[part : 2 * part])
        out[:, 4 * rank : 5 * rank] += mm(cot_ref[:, pl.ds(half_start, half)], shard[2 * part :])
        out[:, 5 * rank :] += total
    if final:
        refs[0][...] = out[:, : 5 * rank].astype(BF16)


def project(ids, flag, shards, tokens, acc=None, final=False):
    tall, rank = shards[0].shape
    rows, count = tokens[0].shape[0], len(ids)
    shapes = [((rows, 6 * rank), F32)]
    if final:
        shapes.append(((rows, 5 * rank), BF16))
    return call(
        functools.partial(project_kernel, acc is None, final, count),
        [*ids, flag],
        [],
        [*tokens, *shards] + ([] if acc is None else [acc]),
        shapes,
        flops=4 * rows * tall * rank * count,
    )


def outer_into(scalars, at, small, tokens_ref, outs):
    for out in outs:
        count, _, columns = out.shape
        for j in range(count):
            start = pl.multiple_of(scalars[at] * columns, columns)
            out[j] = mm(small, tokens_ref[:, pl.ds(start, columns)]).astype(BF16)
            at += 1


def small_parts(sections, here, core, keeps, others, s):
    value = lambda refs: (
        jnp.where(here == s, refs[0][...], refs[1][...].astype(F32))
        if sections == 2
        else refs[1 + s][...].astype(F32)
    )
    mine, theirs = value(keeps), value(others)
    whole = jnp.concatenate(
        [jnp.where(core == 0, mine, theirs), jnp.where(core == 0, theirs, mine)]
    )
    rank = whole.shape[0] // 3
    return whole[:rank], whole[rank : 2 * rank], whole[2 * rank :]


def chain_kernel(sections, width, scalars, base_ref, cot_ref, own, *refs):
    here, core = scalars[0], scalars[1]
    n = 1 if sections == 2 else sections
    thin_count = 1 if sections == 2 else 2
    refs = list(refs)
    take = lambda count: [refs.pop(0) for _ in range(count)]
    sent, keeps, others = take(n), take(n + 1), take(n + 1)
    codes_ref, thin_refs = take(1)[0], take(thin_count)
    outs_c, outs_b = take(2), take(2)
    rank = own.shape[1] // 6
    last = sections - 1
    values = [
        jnp.where(
            here == s, own[:, : 5 * rank], sent[0 if sections == 2 else s][...].astype(F32)
        )
        for s in range(sections)
    ]
    column = lambda s, k: values[s][:, k * rank : (k + 1) * rank]
    spread = lambda k: jnp.concatenate(
        [column(0, k), column(0, k + 1) + column(last, k + 1)], axis=1
    )
    base_s = spread(1)
    square = jnp.sum(own[:, 5 * rank :], axis=1, keepdims=True)
    smalls = [small_parts(sections, here, core, keeps, others, s) for s in range(sections)]
    gram = jnp.concatenate([smalls[0][2], smalls[last][2]])
    choose = lambda s, value, other: value if other is None else jnp.where(here == s, value, other)
    state = []
    code = mine_code = None
    for s in range(sections):
        m_s, q_t, _ = smalls[s]
        inner, total, resid_s, before = column(s, 0), square, base_s, code
        if s:
            moved = exact(code, gram)
            total = square + jnp.sum(
                (2.0 * base_s + moved) * code.astype(F32), axis=1, keepdims=True
            )
            inner = inner + exact(code, q_t, COLUMNS)
            resid_s = base_s + moved
        inverse = lax.rsqrt(jnp.maximum(total, 0.0) * (1.0 / width) + 1e-05)
        inner = inner * inverse
        logistic = 1.0 / (1.0 + jnp.exp(-inner))
        active = inner * logistic
        grown = exact(active, m_s)
        code = (moved + grown if s else grown).astype(BF16)
        mine_code = choose(s, code, mine_code)
        state.append((m_s, q_t, inner, logistic, inverse, active, resid_s, before))
    codes_ref[...] = mine_code
    active_t = state[last][5].T.astype(BF16)
    outer_into(scalars, 2, active_t, cot_ref, outs_c)

    grad_active, grad_y = column(last, 3), spread(3)
    mine = thin_in = thin_out = None
    for s in range(last, -1, -1):
        m_s, q_t, inner, logistic, inverse, active, resid_s, before = state[s]
        if s < last:
            grad_active = exact(back, m_s, COLUMNS)
            grad_y = exact(back, gram) if s else None
            thin_out = choose(s, mm(active.T.astype(BF16), back), thin_out)
        grad_inner = grad_active * logistic * (1.0 + inner * (1.0 - logistic))
        scaled = inverse * grad_inner
        scaled_t = scaled.T.astype(BF16)
        scaled = scaled.astype(BF16)
        mine = choose(s, scaled_t, mine)
        if s:
            thin_in = choose(s, mm(scaled_t, before), thin_in)
            along = jnp.sum(inner * grad_inner, axis=1, keepdims=True)
            along = along * (inverse * inverse * (1.0 / width))
            back = (grad_y + exact(scaled, q_t) - resid_s * along).astype(BF16)
    if sections == 2:
        thin_refs[0][...] = jnp.where(here == last, thin_in, thin_out)
    else:
        thin_refs[0][...] = jnp.where(here == 0, 0.0, thin_in)
        thin_refs[1][...] = thin_out
    outer_into(scalars, 2 + 2 * outs_c[0].shape[0], mine, base_ref, outs_b)


def end_kernel(sections, scalars, gain_ref, space_ref, *refs):
    is_last = scalars[0] == 1
    part = space_ref.shape[0]
    grad_in, grad_out = refs[-2:]
    refs = list(refs[:-2])
    pair = lambda: refs.pop(0)[...].astype(F32) + refs.pop(0)[...].astype(F32)
    thin_in = pair()
    thin_out = thin_in if sections == 2 else pair()
    space = space_ref[...]
    lift_in = exact(thin_in, space, COLUMNS)
    lift_out = lift_in if sections == 2 else exact(thin_out, space, COLUMNS)
    if sections == 2:
        lift_in = jnp.where(is_last, lift_in, 0.0)
        half_first, half_second = refs.pop(0)[...], refs.pop(0)[...]
        sum_out = jnp.concatenate([half_first, half_second], axis=1)
    else:
        sum_out = refs.pop(0)[...]
    sum_in = pair()
    start = pl.multiple_of(scalars[1] * part, part)
    total = gain_ref[:, pl.ds(start, part)] * (sum_in + lift_in)
    grad_in[...] = total.T
    grad_out[...] = jnp.where(is_last, sum_out, lift_out).T


def sum_thin(value, waits):
    peers = lax.axis_size("dp")
    bit, step = 1, 0
    while bit < peers:
        if step:
            wait = waits[min(step, len(waits)) - 1]
            value = value + got if wait is None else after(value + got, wait)
        got = swap(value, bit)
        bit, step = bit * 2, step + 1
    return value, got


def scatter_sum(got, keep, waits=()):
    half = got.shape[0] // 2
    summed = (keep[half:].astype(F32) + got[half:].astype(F32)).astype(BF16)
    got_x = swap(summed, 2)
    total = keep[:half].astype(F32) + got[:half].astype(F32) + got_x.astype(F32)
    bit = 4
    while True:
        left = total.reshape((total.shape[0] // 2, 2) + total.shape[1:])
        give = left[:, 1].astype(BF16)
        if waits:
            give = after(give, *waits[0])
            waits = waits[1:]
        arrived = swap(give, bit)
        if left.shape[0] == 1:
            return (left[0, 0], arrived[0]), got_x
        total = left[:, 0] + arrived.astype(F32)
        bit *= 2


def on_device(base, cotangent, gain, weight_in, weight_out, subspace):
    sections = lax.axis_size("section")
    here = lax.axis_index("section")
    spot = lax.axis_index("dp")
    core = spot % 2
    rows, width = base.shape
    part, size = subspace.shape
    rank = weight_in.shape[2]
    last = sections - 1
    flag = (here == last).astype(jnp.int32)
    own_in, own_out = weight_in[0], weight_out[0]
    own = call(
        own_kernel,
        [flag, spot],
        [own_in, own_out, subspace, gain],
        [],
        [((part * 5 // 2, rank), BF16)],
        [pltpu.VMEM((part, rank), BF16), pltpu.VMEM((1, part), F32), pltpu.SemaphoreType.DMA((4,))],
        62 * 1024 * 1024,
    )[0]

    peers = lax.axis_size("dp")
    order = sorted(range(4, peers, 4), key=lambda m: (m.bit_count(), m))
    shards = {0: own}
    shards[2] = swap(own, 2)
    for k, m in enumerate(order):
        if m.bit_count() == 1:
            shards[m] = swap(after(own, shards[order[k - 1]]) if k else own, m)

    shards[order[0] ^ 2] = swap(after(shards[order[0]], shards[2]), 2)
    tall = (3 * rank, size)
    keep, give = call(
        small_kernel,
        [flag, core],
        [own_out, subspace],
        [after(own, shards[order[0] ^ 2])],
        [((tall[0] // 2, size), F32)] * 2,
        [
            pltpu.VMEM((part, rank), BF16),
            pltpu.VMEM((part, size), BF16),
            pltpu.VMEM(tall, F32),
            pltpu.SemaphoreType.DMA((2,)),
        ],
        60 * 1024 * 1024,
    )
    small = keep + swap(give, 1)
    bit = 4
    while bit < peers // 2:
        small = small + swap(small, bit)
        bit *= 2

    tokens = (base, cotangent)
    ends = order[-1] ^ 2
    for k, m in enumerate(order):
        low = m & -m
        if m != low:
            shards[m] = swap(after(shards[m ^ low], shards[order[k - 2] ^ 2]), low)
        if k:
            ties = [small] if m ^ 2 == ends else []
            shards[m ^ 2] = swap(after(shards[m], shards[order[k - 1] ^ 2], *ties), 2)
    small = after(small, shards[peers // 2])
    small = small + swap(small, peers // 2)
    small = small + swap(small.astype(BF16), 2).astype(F32)
    small_other = swap(small, 1)
    keeps = [small, *from_sections(small.astype(BF16))]
    others = [small_other, *from_sections(small_other.astype(BF16))]

    marks = [m for m in range(0, peers, 2) if m != ends]
    for m in marks:
        shards[m ^ 1] = swap(shards[m], 1)
    marks += [m ^ 1 for m in marks]
    acc = project([spot ^ m for m in marks], flag, [shards[m] for m in marks], tokens)[0]
    pair = [shards[ends], swap(after(shards[ends], acc), 1)]
    acc, send = project([spot ^ ends, spot ^ ends ^ 1], flag, pair, tokens, after(acc, *keeps, *others), final=True)
    sent = from_sections(send)

    near = list(range(0, peers, 4))
    every = near + [m ^ 2 for m in near]
    half = part // 2
    if sections == 2:
        columns, block_id = half, lambda i: i * 2 + flag
    else:
        columns, block_id = part, lambda i: i
    both = (spot ^ 1, spot)
    out_ids = [block_id(who ^ m) for who in both for m in every]
    in_ids = [who ^ m for who in both for m in every]
    blocks = lambda n: ((len(every), rank, n), BF16)
    thin_count = 1 if sections == 2 else 2
    codes, *rest = call(
        functools.partial(chain_kernel, sections, width),
        [here, core, *out_ids, *in_ids],
        [],
        [base, cotangent, acc, *sent, *keeps, *others],
        [((rows, size), BF16)]
        + [((rank, size), F32)] * thin_count
        + [blocks(columns)] * 2
        + [blocks(part)] * 2,
        vmem_bytes=(VMEM_BYTES if sections == 2 else 32 * 1024 * 1024),
    )
    thins, chunks = rest[:thin_count], rest[thin_count:]
    got = [swap(give, 1) for give in chunks[::2]]
    sum_out, out_x = scatter_sum(got[0], chunks[1])
    sum_in, in_x = scatter_sum(got[1], chunks[3])
    sum_out = sum_out[0] + sum_out[1].astype(F32)
    ends_out = [sum_out]
    if sections == 2:
        ends_out = [swap(sum_out, 1, "section"), sum_out]
    waits = [got[1], out_x, None]
    terms = [term for thin in thins for term in sum_thin(thin, waits)]
    grad_in, grad_out = call(
        functools.partial(end_kernel, sections),
        [flag, spot],
        [],
        [gain, subspace, *terms, *ends_out, *sum_in],
        [((part, rank), F32)] * 2,
    )
    return codes[None], grad_in[None], grad_out[None]


def solution(mesh):
    placed = (
        P("dp", None),
        P("dp", None),
        P("section", None),
        P("section", "dp", None),
        P("section", "dp", None),
        P("dp", None),
    )
    return jax.shard_map(
        on_device,
        mesh=mesh,
        in_specs=placed,
        out_specs=(P("section", "dp", None), P("section", "dp", None), P("section", "dp", None)),
        check_vma=False,
    )
```
